32 devices in a mesh: dp: 8 (over z, x), crop: 4 (over y, core).
Axes of the slice: x: 2, y: 2, z: 4, core: 2. Of those that a mesh axis runs over, the one named last changes fastest.
Arguments:
- query_crops: bfloat16 [16384, 2048], P(('dp', 'crop')), may hold values from -6 to 6
- key_crops: bfloat16 [16384, 2048], P(('dp', 'crop')), may hold values from -43 to 43
- shuffle: int32 [16384], P(('dp', 'crop')), may hold values from 0 to 16383, as said below
- distractor_bank: bfloat16 [16384, 128], replicated, may hold values from -2.5 to 2.5
- query_inner: bfloat16 [2048, 2048], replicated, may hold values from -0.125 to 0.125
- query_outer: bfloat16 [2048, 128], replicated, may hold values from -0.125 to 0.125
- key_inner: bfloat16 [2048, 2048], replicated, may hold values from -0.125 to 0.125
- key_outer: bfloat16 [2048, 128], replicated, may hold values from -0.125 to 0.125
Outputs:
- grad_inner: float32 [2048, 2048], P(('dp', 'crop'))
- grad_outer: float32 [2048, 128], P(('dp', 'crop'))
The draws below stay inside these ranges and needn't reach their ends.
Inputs may be any that keep to these rules, and one draw needn't show every extreme that they name: `shuffle`: a permutation of the 16384 key crops; shuffled position t * 512 + s * 16 + j, for j below 16, takes a crop from rows s * 512 up to (s + 1) * 512 - 1.
All inputs are finite; a program needn't handle non-finite values.
Results may differ from the reference program's by a relative error of at most 0.008.
Values may be sent and summed in bfloat16 or wider, within the bound.
No kernel may reach another device: no remote copies, remote signals or barrier semaphores. Data moves between devices by JAX's collectives and lax.ppermute only.
A program may use at most 192 MiB of HBM per device.

```python
import math
import jax
import jax.numpy as jnp
from jax import lax

D = 2048
HID = 2048
EMB = 128
QUEUE = 16384
ROWS = 512
TOTAL = 16384
N_DP = 8
N_CROP = 4


def draw_key_crops(key, part):
    group_count = TOTAL // ROWS
    seed_noise = jax.random.fold_in(key, 11)
    seed_scale = jax.random.fold_in(key, 12)
    seed_offset = jax.random.fold_in(key, 13)
    base_noise = jax.random.truncated_normal(seed_noise, -4.0, 4.0, (TOTAL, D), jnp.float32)
    row_scales = jnp.exp(jax.random.uniform(seed_scale, (TOTAL, 1), jnp.float32, 0.0, math.log(10.0)))
    offsets = jax.random.uniform(seed_offset, (group_count, 1, D), jnp.float32, -2.5, 2.5)
    values = (base_noise * row_scales).reshape(group_count, ROWS, D) + offsets
    return values.reshape(TOTAL, D).astype(jnp.bfloat16)


def draw_shuffle(key, part):
    group_count = TOTAL // ROWS
    per_peer = ROWS // group_count
    sources = jnp.arange(group_count, dtype=jnp.int32)

    def one_order(source):
        return jax.random.permutation(jax.random.fold_in(key, source), ROWS).astype(jnp.int32)
    orders = jax.vmap(one_order)(sources)
    blocks = orders.reshape(group_count, group_count, per_peer) + (sources * ROWS)[:, None, None]
    return jnp.transpose(blocks, (1, 0, 2)).reshape(TOTAL).astype(jnp.int32)


def block_levels(key, shape, cuts, low, high):
    def one(position, parts):
        draws = jax.random.uniform(jax.random.fold_in(jax.random.fold_in(key, 6), position), (parts,), jnp.float32, low / len(cuts), high / len(cuts))
        return jnp.repeat(jnp.exp(draws), shape[position] // parts).reshape((-1,) + (1,) * (len(shape) - position - 1))

    factor_of = one(*cuts[0])
    for cut in cuts[1:]:
        factor_of = factor_of * one(*cut)
    return factor_of


def normal_values(stream_key, shape, scale, reach, shards=(), held_as=jnp.bfloat16):
    entries = jax.random.normal(stream_key, shape, jnp.float32) * scale
    if len(shards) > 0:
        entries = block_levels(stream_key, shape, shards, -0.22, 0.18) * entries
    return jnp.clip(entries, min=-reach, max=reach).astype(held_as)


def setup_inputs(seed: int = 0) -> dict:
    streams_of = jax.random.split(jax.random.key(seed), 9)
    query_crops = normal_values(streams_of[0], (TOTAL, D), 1.0, 6.0, ((0, 32),))
    key_crops = draw_key_crops(jax.random.fold_in(streams_of[8], 71), 0)
    shuffle = draw_shuffle(jax.random.fold_in(streams_of[8], 71), 0)
    distractor_bank = normal_values(streams_of[3], (QUEUE, EMB), 0.3, 2.5)
    query_inner = normal_values(streams_of[4], (D, HID), D ** -0.5, 0.125)
    query_outer = normal_values(streams_of[5], (HID, EMB), HID ** -0.5, 0.125)
    key_inner = normal_values(streams_of[6], (D, HID), D ** -0.5, 0.125)
    key_outer = normal_values(streams_of[7], (HID, EMB), HID ** -0.5, 0.125)
    return {"query_crops": query_crops, "key_crops": key_crops, "shuffle": shuffle, "distractor_bank": distractor_bank, "query_inner": query_inner, "query_outer": query_outer, "key_inner": key_inner, "key_outer": key_outer}


sharpness_divisor = 0.2
loss_scale = 4096.0
bn_eps = 1e-05
norm_eps = 1e-06

def batch_stats(hidden):
    average = lax.optimization_barrier(jnp.mean(hidden, axis=0))
    variance = lax.optimization_barrier(jnp.mean(hidden * hidden, axis=0)) - average * average
    return (average, lax.rsqrt(variance + bn_eps))

def head_tail(normed, w_out):
    active = jnp.maximum(normed, 0.0).astype(jnp.bfloat16)
    projected = jnp.dot(active, w_out, preferred_element_type=jnp.float32)
    return projected * lax.rsqrt(lax.optimization_barrier(jnp.sum(projected * projected, axis=-1, keepdims=True)) + norm_eps)

def key_embed(crop_rows, w_in, w_out):
    hidden = jnp.dot(crop_rows, w_in, preferred_element_type=jnp.float32)
    average, inv_std = batch_stats(hidden)
    return head_tail((hidden - average) * inv_std, w_out)

def query_grads(crop_rows, matching_targets, distractor_bank, w_in, w_out, all_rows):
    hidden = jnp.dot(crop_rows, w_in, preferred_element_type=jnp.float32)
    average, inv_std = batch_stats(hidden)
    normed = (hidden - average) * inv_std
    active = jnp.maximum(normed, 0.0).astype(jnp.bfloat16)
    projected = jnp.dot(active, w_out, preferred_element_type=jnp.float32)
    inv_len = lax.rsqrt(lax.optimization_barrier(jnp.sum(projected * projected, axis=-1, keepdims=True)) + norm_eps)
    probe_features = projected * inv_len
    matching_similarity = lax.optimization_barrier(jnp.sum(probe_features * matching_targets, axis=-1, keepdims=True)) / sharpness_divisor
    distractor_similarities = lax.dot_general(probe_features.astype(jnp.bfloat16), distractor_bank, (((1,), (1,)), ((), ())), preferred_element_type=jnp.float32) / sharpness_divisor
    exp_pos = jnp.exp(matching_similarity)
    exp_neg = jnp.exp(distractor_similarities)
    total_exp = exp_pos + lax.optimization_barrier(jnp.sum(exp_neg, axis=-1, keepdims=True))
    scale_coef = loss_scale / all_rows
    matching_similarity_slope = scale_coef * (exp_pos / total_exp - 1.0)
    distractor_similarity_slope = (scale_coef * exp_neg / total_exp).astype(jnp.bfloat16)
    probe_feature_slope = (matching_similarity_slope * matching_targets + jnp.dot(distractor_similarity_slope, distractor_bank, preferred_element_type=jnp.float32)) / sharpness_divisor
    d_proj = ((probe_feature_slope - probe_features * lax.optimization_barrier(jnp.sum(probe_feature_slope * probe_features, axis=-1, keepdims=True))) * inv_len).astype(jnp.bfloat16)
    grad_out = lax.dot_general(active, d_proj, (((0,), (0,)), ((), ())), preferred_element_type=jnp.float32)
    d_act = lax.dot_general(d_proj, w_out, (((1,), (1,)), ((), ())), preferred_element_type=jnp.float32)
    d_norm = jnp.where(normed > 0.0, d_act, 0.0)
    d_hidden = inv_std * (d_norm - lax.optimization_barrier(jnp.mean(d_norm, axis=0)) - normed * lax.optimization_barrier(jnp.mean(d_norm * normed, axis=0)))
    grad_in = lax.dot_general(crop_rows, d_hidden.astype(jnp.bfloat16), (((0,), (0,)), ((), ())), preferred_element_type=jnp.float32)
    return (grad_in, grad_out)

def reference(query_crops, key_crops, shuffle, distractor_bank, query_inner, query_outer, key_inner, key_outer):
    group_count = N_DP * N_CROP
    shuffled = key_crops[shuffle].reshape(group_count, ROWS, D)

    def embed_group(group_rows):
        return key_embed(group_rows, key_inner, key_outer)
    embedded = lax.map(embed_group, shuffled).reshape(TOTAL, EMB)
    matching_targets = jnp.zeros((TOTAL, EMB), jnp.float32).at[shuffle].set(embedded)
    all_rows = float(TOTAL)

    def accumulate(running, block_pair):
        grad_in, grad_out = query_grads(block_pair[0], block_pair[1], distractor_bank, query_inner, query_outer, all_rows)
        return ((running[0] + grad_in, running[1] + grad_out), None)
    initial = (jnp.zeros((D, HID), jnp.float32), jnp.zeros((HID, EMB), jnp.float32))
    (grad_inner, grad_outer), _ = lax.scan(accumulate, initial, (query_crops.reshape(group_count, ROWS, D), matching_targets.reshape(group_count, ROWS, EMB)))
    return (grad_inner, grad_outer)
```

```python
import math
import jax
import jax.numpy as jnp
from jax import lax
from jax.experimental import pallas as pl
from jax.experimental.pallas import tpu as pltpu
from jax.sharding import PartitionSpec as P

sharpness_divisor = 0.2
loss_scale = 4096.0
bn_eps = 1e-05
norm_eps = 1e-06
AXES = ("dp", "crop")
QUARTER = 0.25


def neg_kernel(q_ref, bank_ref, sum_ref, u_ref):
    @pl.when(pl.program_id(0) == 0)
    def _():
        sum_ref[...] = jnp.zeros_like(sum_ref)
        u_ref[...] = jnp.zeros_like(u_ref)

    q = q_ref[...]
    step = 256
    total = sum_ref[...]
    u = u_ref[...]
    for j in range(bank_ref.shape[0] // step):
        bank = bank_ref[j * step:(j + 1) * step, :]
        s = lax.dot_general(q, bank, (((1,), (1,)), ((), ())), preferred_element_type=jnp.float32)
        e = jnp.exp2(s * (1.0 / (sharpness_divisor * math.log(2.0))) - 2.0)
        for i in range(step // 128):
            total = total + e[:, i * 128:(i + 1) * 128]
        u = u + jnp.dot(e.astype(jnp.bfloat16), bank, preferred_element_type=jnp.float32)
    sum_ref[...] = total
    u_ref[...] = u


def negatives(q, bank):
    rows, emb = q.shape
    tile = 2048
    return pl.pallas_call(
        neg_kernel,
        grid=(bank.shape[0] // tile,),
        in_specs=[
            pl.BlockSpec((rows, emb), lambda i: (0, 0)),
            pl.BlockSpec((tile, emb), lambda i: (i, 0)),
        ],
        out_specs=[
            pl.BlockSpec((rows, 128), lambda i: (0, 0)),
            pl.BlockSpec((rows, emb), lambda i: (0, 0)),
        ],
        out_shape=[
            jax.ShapeDtypeStruct((rows, 128), jnp.float32),
            jax.ShapeDtypeStruct((rows, emb), jnp.float32),
        ],
        cost_estimate=pl.CostEstimate(
            flops=4 * rows * bank.shape[0] * emb,
            bytes_accessed=bank.shape[0] * emb * 2,
            transcendentals=rows * bank.shape[0],
        ),
        compiler_params=pltpu.CompilerParams(vmem_limit_bytes=32 * 1024 * 1024),
        name="negatives",
    )(q, bank)


def swap(x, axis, bit):
    size = lax.axis_size(axis)
    return lax.ppermute(x, axis, [(i, i ^ bit) for i in range(size)])


def halve(x, dim, mine):
    keep = lax.dynamic_index_in_dim(x, mine, dim, keepdims=False)
    send = lax.dynamic_index_in_dim(x, 1 - mine, dim, keepdims=False)
    return keep, send


def add(a, b):
    return (a.astype(jnp.float32) + b.astype(jnp.float32)).astype(jnp.bfloat16)


def line_scatter(x, place, length):
    own = lax.dynamic_index_in_dim(x, place, 0, keepdims=False).astype(jnp.float32)
    right = jnp.zeros(x.shape[1:], x.dtype)
    left = right
    for k in range(1, length):
        d = jnp.clip(length - k + place, 0, length - 1)
        out = lax.dynamic_index_in_dim(x, d, 0, keepdims=False)
        out = out if k == 1 else add(out, right)
        right = lax.ppermute(
            out, "dp", [(2 * p + b, 2 * p + 2 + b) for p in range(k) for b in range(2)]
        )
        d = jnp.clip(k - length + place, 0, length - 1)
        out = lax.dynamic_index_in_dim(x, d, 0, keepdims=False)
        out = out if k == 1 else add(out, left)
        left = lax.ppermute(
            out,
            "dp",
            [
                (2 * p + b, 2 * p - 2 + b)
                for p in range(length - k, length)
                for b in range(2)
            ],
        )
    return own + right.astype(jnp.float32) + left.astype(jnp.float32)


def scatter_sum(grads):
    n_dp, n_crop = lax.axis_size("dp"), lax.axis_size("crop")
    length, half_crop = n_dp // 2, n_crop // 2
    dp, crop = lax.axis_index("dp"), lax.axis_index("crop")
    z, x, y, core = dp // 2, dp % 2, crop // 2, crop % 2
    parts = []
    for part, g in enumerate(grads):
        rows = g.shape[0] // (n_dp * n_crop)
        g = g.reshape(length, 2, half_crop, 2, rows, g.shape[1])
        keep, send = halve(g, 3, core)
        g = add(keep, swap(send, "crop", 1))
        if part % 2 == 0:
            keep, send = halve(g, 1, x)
            g = add(keep, swap(send, "dp", 1))
            keep, send = halve(g, 1, y)
            g = add(keep, swap(send, "crop", 2))
        else:
            keep, send = halve(g, 2, y)
            g = add(keep, swap(send, "crop", 2))
            keep, send = halve(g, 1, x)
            g = add(keep, swap(send, "dp", 1))
        parts.append(line_scatter(g, z, length))
    return parts


def per_device(
    query_crops, key_crops, shuffle, distractor_bank, query_inner, query_outer, key_inner, key_outer
):
    group_count = lax.axis_size(AXES)
    row_count = query_crops.shape[0]
    hid = query_inner.shape[1]
    per_peer = row_count // group_count
    all_rows = float(row_count * group_count)

    wanted = (shuffle % row_count).reshape(group_count, per_peer)
    requested = lax.all_to_all(wanted, AXES, split_axis=0, concat_axis=0, tiled=True)
    flat_req = requested.reshape(-1)
    pick = (flat_req[:, None] == lax.iota(jnp.int32, row_count)[None, :]).astype(jnp.bfloat16)

    by_group = jnp.dot(pick, key_crops, preferred_element_type=jnp.float32).astype(jnp.bfloat16)
    hidden_k = jnp.dot(by_group, key_inner, preferred_element_type=jnp.float32)
    hidden_k = hidden_k.reshape(group_count, per_peer, hid)
    sums = jnp.concatenate(
        [jnp.sum(hidden_k, axis=1), jnp.sum(hidden_k * hidden_k, axis=1)], axis=1
    )
    mine = lax.all_to_all(sums, AXES, split_axis=0, concat_axis=0, tiled=True)
    mine = jnp.sum(mine, axis=0) / row_count
    mu = mine[:hid]
    inv_std = lax.rsqrt(mine[hid:] - mu * mu + bn_eps)
    told = jnp.broadcast_to(jnp.concatenate([mu, inv_std])[None, :], (group_count, 2 * hid))
    told = lax.all_to_all(told, AXES, split_axis=0, concat_axis=0, tiled=True)

    hidden = jnp.dot(query_crops, query_inner, preferred_element_type=jnp.float32)
    average = jnp.mean(hidden, axis=0)
    inv_q = lax.rsqrt(jnp.mean(hidden * hidden, axis=0) - average * average + bn_eps)
    normed = (hidden - average) * inv_q
    active = jnp.maximum(normed, 0.0).astype(jnp.bfloat16)
    projected = jnp.dot(active, query_outer, preferred_element_type=jnp.float32)
    inv_len = lax.rsqrt(jnp.sum(projected * projected, axis=-1, keepdims=True) + norm_eps)
    q = projected * inv_len
    neg_sum, weighted = negatives(q.astype(jnp.bfloat16), distractor_bank)
    neg_sum = jnp.sum(neg_sum, axis=-1, keepdims=True)

    normed_k = (hidden_k - told[:, None, :hid]) * told[:, None, hid:]
    active_k = jnp.maximum(normed_k, 0.0).astype(jnp.bfloat16).reshape(row_count, hid)
    z_k = jnp.dot(active_k, key_outer, preferred_element_type=jnp.float32)
    z_k = z_k * lax.rsqrt(jnp.sum(z_k * z_k, axis=-1, keepdims=True) + norm_eps)
    positives = jnp.zeros_like(z_k).at[flat_req].set(z_k)

    scale_coef = loss_scale / all_rows
    pos = jnp.sum(q * positives, axis=-1, keepdims=True) / sharpness_divisor
    exp_pos = jnp.exp(pos) * QUARTER
    total = exp_pos + neg_sum
    d_pos = scale_coef * (exp_pos / total - 1.0)
    d_q = (d_pos * positives + weighted * (scale_coef / total)) / sharpness_divisor
    d_z = ((d_q - q * jnp.sum(d_q * q, axis=-1, keepdims=True)) * inv_len).astype(jnp.bfloat16)

    grad_out = lax.dot_general(
        active, d_z, (((0,), (0,)), ((), ())), preferred_element_type=jnp.float32
    ).astype(jnp.bfloat16)
    grads = []
    cols = hid // 2
    for part in range(2):
        cut = slice(part * cols, (part + 1) * cols)
        n_cut = normed[:, cut]
        d_act = lax.dot_general(
            d_z, query_outer[cut], (((1,), (1,)), ((), ())), preferred_element_type=jnp.float32
        )
        d_norm = jnp.where(n_cut > 0.0, d_act, 0.0)
        d_hidden = inv_q[cut] * (
            d_norm - jnp.mean(d_norm, axis=0) - n_cut * jnp.mean(d_norm * n_cut, axis=0)
        )
        g = lax.dot_general(
            query_crops,
            d_hidden.astype(jnp.bfloat16),
            (((0,), (0,)), ((), ())),
            preferred_element_type=jnp.float32,
        ).astype(jnp.bfloat16)
        grads.append(g)
    grads[1] = jnp.concatenate([grads[1], grad_out], axis=1)
    left, right = scatter_sum(grads)
    return (jnp.concatenate([left, right[:, :cols]], axis=1), right[:, cols:])


def solution(mesh):
    placed = (
        P(AXES, None),
        P(AXES, None),
        P(AXES),
        P(),
        P(),
        P(),
        P(),
        P(),
    )
    return jax.shard_map(
        per_device,
        mesh=mesh,
        in_specs=placed,
        out_specs=(P(AXES, None), P(AXES, None)),
        check_vma=False,
    )
```

```python
import math
import jax
import jax.numpy as jnp
from jax import lax
from jax.experimental import pallas as pl
from jax.experimental.pallas import tpu as pltpu
from jax.sharding import PartitionSpec as P

sharpness_divisor = 0.2
loss_scale = 4096.0
bn_eps = 1e-05
norm_eps = 1e-06
AXES = ("dp", "crop")
QUARTER = 0.25


def neg_kernel(q_ref, bank_ref, sum_ref, u_ref):
    @pl.when(pl.program_id(0) == 0)
    def _():
        sum_ref[...] = jnp.zeros_like(sum_ref)
        u_ref[...] = jnp.zeros_like(u_ref)

    q = q_ref[...]
    step = 256
    total = sum_ref[...]
    u = u_ref[...]
    for j in range(bank_ref.shape[0] // step):
        bank = bank_ref[j * step:(j + 1) * step, :]
        s = lax.dot_general(q, bank, (((1,), (1,)), ((), ())), preferred_element_type=jnp.float32)
        e = jnp.exp2(s * (1.0 / (sharpness_divisor * math.log(2.0))) - 2.0)
        for i in range(step // 128):
            total = total + e[:, i * 128:(i + 1) * 128]
        u = u + jnp.dot(e.astype(jnp.bfloat16), bank, preferred_element_type=jnp.float32)
    sum_ref[...] = total
    u_ref[...] = u


def negatives(q, bank):
    rows, emb = q.shape
    tile = 2048
    return pl.pallas_call(
        neg_kernel,
        grid=(bank.shape[0] // tile,),
        in_specs=[
            pl.BlockSpec((rows, emb), lambda i: (0, 0)),
            pl.BlockSpec((tile, emb), lambda i: (i, 0)),
        ],
        out_specs=[
            pl.BlockSpec((rows, 128), lambda i: (0, 0)),
            pl.BlockSpec((rows, emb), lambda i: (0, 0)),
        ],
        out_shape=[
            jax.ShapeDtypeStruct((rows, 128), jnp.float32),
            jax.ShapeDtypeStruct((rows, emb), jnp.float32),
        ],
        cost_estimate=pl.CostEstimate(
            flops=4 * rows * bank.shape[0] * emb,
            bytes_accessed=bank.shape[0] * emb * 2,
            transcendentals=rows * bank.shape[0],
        ),
        compiler_params=pltpu.CompilerParams(vmem_limit_bytes=32 * 1024 * 1024),
        name="negatives",
    )(q, bank)


TILE = 256
VMEM_LIMIT = 48 * 1024 * 1024


PAIRS = (4, 4)


def params():
    return pltpu.CompilerParams(
        dimension_semantics=("arbitrary",), vmem_limit_bytes=VMEM_LIMIT
    )


def dot(a, b):
    return jnp.dot(a, b, preferred_element_type=jnp.float32)


def dot_t(a, b):
    return lax.dot_general(a, b, (((1,), (1,)), ((), ())), preferred_element_type=jnp.float32)


def whole(shape):
    return pl.BlockSpec(shape, lambda *_: (0,) * len(shape))


def group_rows(groups, per_peer):
    rows = groups * per_peer
    row = lax.broadcasted_iota(jnp.int32, (groups, rows), 1)
    group = lax.broadcasted_iota(jnp.int32, (groups, rows), 0)
    inside = (row >= group * per_peer) & (row < (group + 1) * per_peer)
    return jnp.where(inside, 1.0, 0.0).astype(jnp.float32)


def group_sum(h, groups):
    rows, cols = h.shape
    per_peer = rows // groups
    if per_peer % 8 == 0:
        return jnp.sum(h.reshape(groups, per_peer, cols), axis=1)
    return jnp.dot(
        group_rows(groups, per_peer),
        h,
        precision=lax.Precision.HIGHEST,
        preferred_element_type=jnp.float32,
    )


def group_spread(v, rows):
    groups, cols = v.shape
    per_peer = rows // groups
    if per_peer % 8 == 0:
        return jnp.broadcast_to(v[:, None, :], (groups, per_peer, cols)).reshape(rows, cols)
    return lax.dot_general(
        group_rows(groups, per_peer),
        v,
        (((0,), (0,)), ((), ())),
        precision=lax.Precision.HIGHEST,
        preferred_element_type=jnp.float32,
    )


def key_hidden_kernel(groups, flat_ref, k_ref, w_ref, h_ref, sums_ref, sorted_ref):
    rows = k_ref.shape[0]

    @pl.when(pl.program_id(0) == 0)
    def _():
        cols = lax.broadcasted_iota(jnp.int32, (rows, rows), 1)
        pick = jnp.where(flat_ref[...] == cols, 1.0, 0.0).astype(jnp.bfloat16)
        for i in range(0, k_ref.shape[1], 512):
            sorted_ref[:, i:i + 512] = dot(pick, k_ref[:, i:i + 512]).astype(jnp.bfloat16)

    h = dot(sorted_ref[...], w_ref[...])
    h_ref[...] = h
    sums_ref[:, 0, :TILE] = group_sum(h, groups)
    sums_ref[:, 0, TILE:] = group_sum(h * h, groups)


def key_hidden(flat_col, k, w, groups):
    rows, d = k.shape
    hid = w.shape[1]
    return pl.pallas_call(
        lambda *refs: key_hidden_kernel(groups, *refs),
        grid=(hid // TILE,),
        in_specs=[
            whole((rows, 1)),
            whole((rows, d)),
            pl.BlockSpec((d, TILE), lambda i: (0, i)),
        ],
        out_specs=[
            pl.BlockSpec((rows, TILE), lambda i: (0, i)),
            pl.BlockSpec((groups, 1, 2 * TILE), lambda i: (0, 0, i)),
        ],
        out_shape=[
            jax.ShapeDtypeStruct((rows, hid), jnp.float32),
            jax.ShapeDtypeStruct((groups, 1, 2 * hid), jnp.float32),
        ],
        scratch_shapes=[pltpu.VMEM((rows, d), jnp.bfloat16)],
        cost_estimate=pl.CostEstimate(
            flops=2 * rows * d * (hid + rows), bytes_accessed=2 * d * hid, transcendentals=0
        ),
        compiler_params=params(),
        name="key_hidden",
    )(flat_col, k, w)


def batch_kernel(rows, part_ref, told_ref):
    groups = part_ref.shape[0]
    total = jnp.sum(part_ref[:, 0, :], axis=0, keepdims=True) / rows
    mu = total[:, :TILE]
    inv = lax.rsqrt(total[:, TILE:] - mu * mu + bn_eps)
    told = jnp.concatenate([mu, inv], axis=1)
    told_ref[:, 0, :] = jnp.broadcast_to(told, (groups, 2 * TILE))


def batch(part, rows):
    groups, _, size = part.shape
    block = pl.BlockSpec((groups, 1, 2 * TILE), lambda i: (0, 0, i))
    return pl.pallas_call(
        lambda *refs: batch_kernel(rows, *refs),
        grid=(size // (2 * TILE),),
        in_specs=[block],
        out_specs=block,
        out_shape=jax.ShapeDtypeStruct(part.shape, jnp.float32),
        compiler_params=params(),
        name="batch",
    )(part)


def query_kernel(x_ref, w_ref, w2_ref, n_ref, inv_ref, a_ref, z_ref, len_ref, q_ref, sum_ref):
    i = pl.program_id(0)
    rows = x_ref.shape[0]
    h = dot(x_ref[...], w_ref[...])
    mu = jnp.sum(h, axis=0, keepdims=True) / rows
    inv = lax.rsqrt(jnp.sum(h * h, axis=0, keepdims=True) / rows - mu * mu + bn_eps)
    normed = (h - mu) * inv
    active = jnp.maximum(normed, 0.0).astype(jnp.bfloat16)
    n_ref[...] = normed
    inv_ref[...] = inv
    a_ref[...] = active
    z = dot(active, w2_ref[...])

    @pl.when(i == 0)
    def _():
        sum_ref[...] = z

    @pl.when(i > 0)
    def _():
        sum_ref[...] += z

    @pl.when(i == pl.num_programs(0) - 1)
    def _():
        z = sum_ref[...]
        inv_len = lax.rsqrt(jnp.sum(z * z, axis=-1, keepdims=True) + norm_eps)
        q = z * inv_len
        z_ref[...] = q
        len_ref[...] = inv_len
        q_ref[...] = q.astype(jnp.bfloat16)


def query_forward(x, w, w2):
    rows, d = x.shape
    hid, emb = w2.shape
    return pl.pallas_call(
        query_kernel,
        grid=(hid // TILE,),
        in_specs=[
            whole((rows, d)),
            pl.BlockSpec((d, TILE), lambda i: (0, i)),
            pl.BlockSpec((TILE, emb), lambda i: (i, 0)),
        ],
        out_specs=[
            pl.BlockSpec((rows, TILE), lambda i: (0, i)),
            pl.BlockSpec((1, TILE), lambda i: (0, i)),
            pl.BlockSpec((rows, TILE), lambda i: (0, i)),
            whole((rows, emb)),
            whole((rows, 1)),
            whole((rows, emb)),
        ],
        out_shape=[
            jax.ShapeDtypeStruct((rows, hid), jnp.float32),
            jax.ShapeDtypeStruct((1, hid), jnp.float32),
            jax.ShapeDtypeStruct((rows, hid), jnp.bfloat16),
            jax.ShapeDtypeStruct((rows, emb), jnp.float32),
            jax.ShapeDtypeStruct((rows, 1), jnp.float32),
            jax.ShapeDtypeStruct((rows, emb), jnp.bfloat16),
        ],
        scratch_shapes=[pltpu.VMEM((rows, emb), jnp.float32)],
        cost_estimate=pl.CostEstimate(
            flops=2 * rows * hid * (d + emb), bytes_accessed=2 * d * hid, transcendentals=0
        ),
        compiler_params=params(),
        name="query_forward",
    )(x, w, w2)


def order_kernel(order_ref, x_ref, y_ref):
    rows = y_ref.shape[2]
    core = order_ref[pl.num_programs(0)]
    t = x_ref[...].T
    y_ref[core, 0] = t[:rows]
    y_ref[1 - core, 0] = t[rows:]


def ordered(x, order, core, blocks):
    n, d = x.shape
    half = blocks // 2
    rows = d // blocks
    width = 2 * rows
    if width % 128:
        y = x.T.reshape(half, 2, rows, n)
        y = jnp.zeros_like(y).at[order].set(y)
        return jnp.moveaxis(jnp.where(core == 0, y, y[:, ::-1]), 1, 0).reshape(d, n)
    return pl.pallas_call(
        order_kernel,
        grid_spec=pltpu.PrefetchScalarGridSpec(
            num_scalar_prefetch=1,
            grid=(half,),
            in_specs=[pl.BlockSpec((n, width), lambda i, o: (0, i))],
            out_specs=pl.BlockSpec((2, 1, rows, n), lambda i, o: (0, o[i], 0, 0)),
        ),
        out_shape=jax.ShapeDtypeStruct((2, half, rows, n), x.dtype),
        cost_estimate=pl.CostEstimate(flops=0, bytes_accessed=8 * n * d, transcendentals=0),
        compiler_params=params(),
        name="ordered",
    )(jnp.append(order, core), x).reshape(d, n)


def embed_kernel(
    all_rows,
    flat_ref, h_ref, told_ref, w2_ref, q_ref, len_ref, sum_ref, weighted_ref, dz_ref, z_ref,
):
    i = pl.program_id(0)
    rows, emb = q_ref.shape
    mu = group_spread(told_ref[:, 0, :TILE], rows)
    inv = group_spread(told_ref[:, 0, TILE:], rows)
    active = jnp.maximum((h_ref[...] - mu) * inv, 0.0).astype(jnp.bfloat16)
    z = dot(active, w2_ref[...])

    @pl.when(i == 0)
    def _():
        z_ref[...] = z

    @pl.when(i > 0)
    def _():
        z_ref[...] += z

    @pl.when(i == pl.num_programs(0) - 1)
    def _():
        z = z_ref[...]
        z = z * lax.rsqrt(jnp.sum(z * z, axis=-1, keepdims=True) + norm_eps)
        back = jnp.where(
            flat_ref[...] == lax.broadcasted_iota(jnp.int32, (rows, rows), 0), 1.0, 0.0
        ).astype(jnp.bfloat16)
        high = z.astype(jnp.bfloat16)
        rest = z - high.astype(jnp.float32)
        mid = rest.astype(jnp.bfloat16)
        low = (rest - mid.astype(jnp.float32)).astype(jnp.bfloat16)
        positives = dot(back, high) + dot(back, mid) + dot(back, low)
        q = q_ref[...]
        scale_coef = loss_scale / all_rows
        pos = jnp.sum(q * positives, axis=-1, keepdims=True) / sharpness_divisor
        exp_pos = jnp.exp(pos) * QUARTER
        total = exp_pos + jnp.sum(sum_ref[...], axis=-1, keepdims=True)
        d_pos = scale_coef * (exp_pos / total - 1.0)
        d_q = (d_pos * positives + weighted_ref[...] * (scale_coef / total)) / sharpness_divisor
        d_z = (d_q - q * jnp.sum(d_q * q, axis=-1, keepdims=True)) * len_ref[...]
        dz_ref[...] = d_z.astype(jnp.bfloat16)


def embed(flat_row, h, told, w2, q, inv_len, neg_sum, weighted, all_rows):
    rows, hid = h.shape
    emb = w2.shape[1]
    groups = told.shape[0]
    return pl.pallas_call(
        lambda *refs: embed_kernel(all_rows, *refs),
        grid=(hid // TILE,),
        in_specs=[
            whole((1, rows)),
            pl.BlockSpec((rows, TILE), lambda i: (0, i)),
            pl.BlockSpec((groups, 1, 2 * TILE), lambda i: (0, 0, i)),
            pl.BlockSpec((TILE, emb), lambda i: (i, 0)),
            whole((rows, emb)),
            whole((rows, 1)),
            whole((rows, emb)),
            whole((rows, emb)),
        ],
        out_specs=whole((rows, emb)),
        out_shape=jax.ShapeDtypeStruct((rows, emb), jnp.bfloat16),
        scratch_shapes=[pltpu.VMEM((rows, emb), jnp.float32)],
        cost_estimate=pl.CostEstimate(
            flops=2 * rows * hid * emb, bytes_accessed=4 * rows * hid, transcendentals=0
        ),
        compiler_params=params(),
        name="embed",
    )(flat_row, h, told, w2, q, inv_len, neg_sum, weighted)


def store_rows(out_ref, at, value, crossed):
    size = value.shape[0] // 4
    for i, j in enumerate((0, 2, 1, 3)):
        j = j if crossed else i
        out_ref[i * size:(i + 1) * size, at] = value[j * size:(j + 1) * size].astype(out_ref.dtype)


def send_kernel(plain, dz_ref, w2_ref, n_ref, inv_ref, xt_ref, at_ref, dh_ref, g_ref):
    i = pl.program_id(0)
    rows = dz_ref.shape[0]
    dz = dz_ref[...]
    normed = n_ref[...]
    d_norm = jnp.where(normed > 0.0, dot_t(dz, w2_ref[...]), 0.0)
    mean = jnp.sum(d_norm, axis=0, keepdims=True) / rows
    slope = jnp.sum(d_norm * normed, axis=0, keepdims=True) / rows
    d_hidden = (inv_ref[...] * (d_norm - mean - normed * slope)).astype(jnp.bfloat16)
    dh_ref[...] = d_hidden
    g = dot(xt_ref[...], d_hidden)
    at = pl.ds(pl.multiple_of(i * TILE, TILE), TILE)

    @pl.when(i < plain)
    def _():
        store_rows(g_ref, at, g, False)

    @pl.when(i >= plain)
    def _():
        store_rows(g_ref, at, g, True)

    if at_ref is not None:
        @pl.when(i == pl.num_programs(0) - 1)
        def _():
            end = g_ref.shape[1]
            store_rows(g_ref, pl.ds(end - dz.shape[1], dz.shape[1]), dot(at_ref[...], dz), True)


def send_half(dz, w2, normed, inv, xt, at, first, tiles, plain):
    rows, emb = dz.shape
    half = xt.shape[0] // 2
    extra = 0 if at is None else emb
    operands = [dz, w2, normed, inv, xt]
    in_specs = [
        whole((rows, emb)),
        pl.BlockSpec((TILE, emb), lambda i: (first + i, 0)),
        pl.BlockSpec((rows, TILE), lambda i: (0, first + i)),
        pl.BlockSpec((1, TILE), lambda i: (0, first + i)),
        pl.BlockSpec((half, rows), lambda i: (1, 0)),
    ]
    if at is None:
        kernel = lambda a, b, c, d, e, f, g: send_kernel(plain, a, b, c, d, e, None, f, g)
    else:
        kernel = lambda *refs: send_kernel(plain, *refs)
        operands.append(at)
        in_specs.append(pl.BlockSpec((half, rows), lambda i: (1, 0)))
    return pl.pallas_call(
        kernel,
        grid=(tiles,),
        in_specs=in_specs,
        out_specs=[
            pl.BlockSpec((rows, TILE), lambda i: (0, i)),
            whole((half, tiles * TILE + extra)),
        ],
        out_shape=[
            jax.ShapeDtypeStruct((rows, tiles * TILE), jnp.bfloat16),
            jax.ShapeDtypeStruct((half, tiles * TILE + extra), jnp.bfloat16),
        ],
        cost_estimate=pl.CostEstimate(
            flops=2 * rows * half * tiles * TILE, bytes_accessed=8 * rows * half, transcendentals=0
        ),
        compiler_params=params(),
        name="send_half",
    )(*operands)


def keep_kernel(plain, dz_ref, dh_ref, xt_ref, at_ref, g_ref):
    i = pl.program_id(0)
    g = dot(xt_ref[...], dh_ref[...])
    at = pl.ds(pl.multiple_of(i * TILE, TILE), TILE)

    @pl.when(i < plain)
    def _():
        store_rows(g_ref, at, g, False)

    @pl.when(i >= plain)
    def _():
        store_rows(g_ref, at, g, True)

    if at_ref is not None:
        @pl.when(i == pl.num_programs(0) - 1)
        def _():
            dz = dz_ref[...]
            end = g_ref.shape[1]
            store_rows(g_ref, pl.ds(end - dz.shape[1], dz.shape[1]), dot(at_ref[...], dz), True)


def keep_half(dz, dh, xt, at, plain):
    rows, emb = dz.shape
    half = xt.shape[0] // 2
    tiles = dh.shape[1] // TILE
    extra = 0 if at is None else emb
    operands = [dz, dh, xt]
    in_specs = [
        whole((rows, emb)),
        pl.BlockSpec((rows, TILE), lambda i: (0, i)),
        whole((half, rows)),
    ]
    if at is None:
        kernel = lambda a, b, c, d: keep_kernel(plain, a, b, c, None, d)
    else:
        kernel = lambda *refs: keep_kernel(plain, *refs)
        operands.append(at)
        in_specs.append(whole((half, rows)))
    return pl.pallas_call(
        kernel,
        grid=(tiles,),
        in_specs=in_specs,
        out_specs=whole((half, tiles * TILE + extra)),
        out_shape=jax.ShapeDtypeStruct((half, tiles * TILE + extra), jnp.float32),
        cost_estimate=pl.CostEstimate(
            flops=2 * rows * half * tiles * TILE, bytes_accessed=8 * rows * half, transcendentals=0
        ),
        compiler_params=params(),
        name="keep_half",
    )(*operands)


def swap(x, axis, bit):
    size = lax.axis_size(axis)
    return lax.ppermute(x, axis, [(i, i ^ bit) for i in range(size)])


def total(parts, rows, cols):
    parts = [p[rows, cols].astype(jnp.float32) for p in parts]
    out = parts[0]
    for p in parts[1:]:
        out = out + p
    return out


def scatter_pair(keep, sent, split):
    n_dp = lax.axis_size("dp")
    length = n_dp // 2
    half = keep.shape[0]
    quarter, eighth = half // 2, half // 4
    rows = eighth // length
    every = slice(None)
    came = swap(sent, "crop", 1)
    sides = []
    for side, (first, second) in enumerate(
        ((("dp", 1), ("crop", 2)), (("crop", 2), ("dp", 1)))
    ):
        cols = slice(0, split) if side == 0 else slice(split, None)
        held = [keep[:, cols], came[:, cols]]
        out = total(held, slice(quarter, half), every).astype(jnp.bfloat16)
        held.append(swap(out, *first))
        out = total(held, slice(eighth, quarter), every).astype(jnp.bfloat16)
        held.append(swap(out, *second))
        sides.append(held)
    own = jnp.concatenate([total(held, slice(0, rows), every) for held in sides], axis=1)
    for k in range(1, length):
        out = jnp.concatenate(
            [
                total(held, slice(k * rows, (k + 1) * rows), every).astype(jnp.bfloat16)
                for held in sides
            ],
            axis=1,
        )
        perm = [
            (2 * p + b, 2 * ((p + k) % length) + b) for p in range(length) for b in range(2)
        ]
        own = own + lax.ppermute(out, "dp", perm).astype(jnp.float32)
    return own


def per_device(
    query_crops, key_crops, shuffle, distractor_bank, query_inner, query_outer, key_inner, key_outer
):
    n_dp, n_crop = lax.axis_size("dp"), lax.axis_size("crop")
    group_count = n_dp * n_crop
    row_count = query_crops.shape[0]
    hid = query_inner.shape[1]
    per_peer = row_count // group_count
    all_rows = float(row_count * group_count)

    wanted = (shuffle % row_count).reshape(group_count, per_peer)
    requested = lax.all_to_all(wanted, AXES, split_axis=0, concat_axis=0, tiled=True)
    flat_req = requested.reshape(-1)

    hidden_k, sums = key_hidden(flat_req[:, None], key_crops, key_inner, group_count)
    told = batch(lax.all_to_all(sums, AXES, split_axis=0, concat_axis=0, tiled=True), row_count)
    told = lax.all_to_all(told, AXES, split_axis=0, concat_axis=0, tiled=True)

    normed, inv_q, active, q, inv_len, q_low = query_forward(query_crops, query_inner, query_outer)
    neg_sum, weighted = negatives(q_low, distractor_bank)

    length = n_dp // 2
    dp, crop = lax.axis_index("dp"), lax.axis_index("crop")
    block = lax.iota(jnp.int32, group_count // 2)
    z, x, y = block // (n_crop), (block // (n_crop // 2)) % 2, block % (n_crop // 2)
    order = ((x ^ (dp % 2)) * (n_crop // 2) + (y ^ (crop // 2))) * length
    order = order + (z + length - dp // 2) % length
    core = crop % 2
    xt = ordered(query_crops, order, core, group_count)
    at = ordered(active, order, core, group_count)

    told, neg_sum, weighted, xt, at = lax.optimization_barrier((told, neg_sum, weighted, xt, at))
    d_z = embed(
        flat_req[None, :], hidden_k, told, key_outer, q, inv_len, neg_sum, weighted, all_rows
    )

    tiles = hid // TILE
    pairs = PAIRS
    scale = tiles // sum(pairs)
    made = []
    first = 0
    for i, count in enumerate(pairs):
        last = at if i == len(pairs) - 1 else None
        dh, sent = send_half(
            d_z, query_outer, normed, inv_q, xt, last, first, count * scale, count * scale // 2
        )
        made.append((dh, sent, last, count * scale // 2))
        first += count * scale
    outs = []
    for dh, sent, last, plain in made:
        keep = keep_half(d_z, dh, xt, last, plain)
        outs.append(scatter_pair(keep, sent, plain * TILE))
    grad = jnp.concatenate(outs, axis=1)
    return (grad[:, :hid], grad[:, hid:])


def solution(mesh):
    placed = (
        P(AXES, None),
        P(AXES, None),
        P(AXES),
        P(),
        P(),
        P(),
        P(),
        P(),
    )
    return jax.shard_map(
        per_device,
        mesh=mesh,
        in_specs=placed,
        out_specs=(P(AXES, None), P(AXES, None)),
        check_vma=False,
    )
```

```python
import math
import jax
import jax.numpy as jnp
from jax import lax
from jax.experimental import pallas as pl
from jax.experimental.pallas import tpu as pltpu
from jax.sharding import PartitionSpec as P

sharpness_divisor = 0.2
loss_scale = 4096.0
bn_eps = 1e-05
norm_eps = 1e-06
AXES = ("dp", "crop")
QUARTER = 0.25


def neg_kernel(q_ref, bank_ref, out_ref):
    rows, emb = q_ref.shape

    @pl.when(pl.program_id(0) == 0)
    def _():
        out_ref[...] = jnp.zeros_like(out_ref)

    q = q_ref[...]
    step = 512
    for j in range(bank_ref.shape[0] // step):
        bank = bank_ref[j * step:(j + 1) * step, :]
        s = lax.dot_general(q, bank, (((1,), (1,)), ((), ())), preferred_element_type=jnp.float32)
        e = jnp.exp2(s * (1.0 / (sharpness_divisor * math.log(2.0))) - 2.0)
        total = e[:, :128]
        for i in range(1, step // 128):
            total = total + e[:, i * 128:(i + 1) * 128]
        out_ref[:, emb:] += total
        out_ref[:, :emb] += jnp.dot(
            e.astype(jnp.bfloat16), bank, preferred_element_type=jnp.float32
        )


def negatives(q, bank):
    rows, emb = q.shape
    tile = 2048
    return pl.pallas_call(
        neg_kernel,
        grid=(bank.shape[0] // tile,),
        in_specs=[
            pl.BlockSpec((rows, emb), lambda i: (0, 0)),
            pl.BlockSpec((tile, emb), lambda i: (i, 0)),
        ],
        out_specs=pl.BlockSpec((rows, emb + 128), lambda i: (0, 0)),
        out_shape=jax.ShapeDtypeStruct((rows, emb + 128), jnp.float32),
        cost_estimate=pl.CostEstimate(
            flops=4 * rows * bank.shape[0] * emb,
            bytes_accessed=bank.shape[0] * emb * 2,
            transcendentals=rows * bank.shape[0],
        ),
        compiler_params=pltpu.CompilerParams(vmem_limit_bytes=32 * 1024 * 1024),
        name="negatives",
    )(q, bank)


TILE = 256
STEP = 512
VMEM_LIMIT = 48 * 1024 * 1024


def params():
    return pltpu.CompilerParams(
        dimension_semantics=("arbitrary",), vmem_limit_bytes=VMEM_LIMIT
    )


def dot(a, b):
    return jnp.dot(a, b, preferred_element_type=jnp.float32)


def dot_t(a, b):
    return lax.dot_general(a, b, (((1,), (1,)), ((), ())), preferred_element_type=jnp.float32)


def whole(shape):
    return pl.BlockSpec(shape, lambda *_: (0,) * len(shape))


def group_rows(groups, per_peer):
    rows = groups * per_peer
    row = lax.broadcasted_iota(jnp.int32, (groups, rows), 1)
    group = lax.broadcasted_iota(jnp.int32, (groups, rows), 0)
    inside = (row >= group * per_peer) & (row < (group + 1) * per_peer)
    return jnp.where(inside, 1.0, 0.0).astype(jnp.float32)


def group_sum(h, groups):
    rows, cols = h.shape
    per_peer = rows // groups
    if per_peer % 8 == 0:
        return jnp.sum(h.reshape(groups, per_peer, cols), axis=1)
    return jnp.dot(
        group_rows(groups, per_peer),
        h,
        precision=lax.Precision.HIGHEST,
        preferred_element_type=jnp.float32,
    )


def group_spread(v, rows):
    groups, cols = v.shape
    per_peer = rows // groups
    if per_peer % 8 == 0:
        return jnp.broadcast_to(v[:, None, :], (groups, per_peer, cols)).reshape(rows, cols)
    return lax.dot_general(
        group_rows(groups, per_peer),
        v,
        (((0,), (0,)), ((), ())),
        precision=lax.Precision.HIGHEST,
        preferred_element_type=jnp.float32,
    )


def key_hidden_kernel(groups, flat_ref, k_ref, w_ref, h_ref, sums_ref, sorted_ref):
    rows = k_ref.shape[0]

    @pl.when(pl.program_id(0) == 0)
    def _():
        cols = lax.broadcasted_iota(jnp.int32, (rows, rows), 1)
        pick = jnp.where(flat_ref[...] == cols, 1.0, 0.0).astype(jnp.bfloat16)
        for i in range(0, k_ref.shape[1], 512):
            sorted_ref[:, i:i + 512] = dot(pick, k_ref[:, i:i + 512]).astype(jnp.bfloat16)

    x = sorted_ref[...]
    for t in range(0, STEP, TILE):
        h = dot(x, w_ref[:, t:t + TILE])
        h_ref[:, t:t + TILE] = h
        sums_ref[:, 0, 2 * t:2 * t + TILE] = group_sum(h, groups)
        sums_ref[:, 0, 2 * t + TILE:2 * t + 2 * TILE] = group_sum(h * h, groups)


def key_hidden(flat_col, k, w, groups):
    rows, d = k.shape
    hid = w.shape[1]
    return pl.pallas_call(
        lambda *refs: key_hidden_kernel(groups, *refs),
        grid=(hid // STEP,),
        in_specs=[
            whole((rows, 1)),
            whole((rows, d)),
            pl.BlockSpec((d, STEP), lambda i: (0, i)),
        ],
        out_specs=[
            pl.BlockSpec((rows, STEP), lambda i: (0, i)),
            pl.BlockSpec((groups, 1, 2 * STEP), lambda i: (0, 0, i)),
        ],
        out_shape=[
            jax.ShapeDtypeStruct((rows, hid), jnp.float32),
            jax.ShapeDtypeStruct((groups, 1, 2 * hid), jnp.float32),
        ],
        scratch_shapes=[pltpu.VMEM((rows, d), jnp.bfloat16)],
        cost_estimate=pl.CostEstimate(
            flops=2 * rows * d * (hid + rows), bytes_accessed=2 * d * hid, transcendentals=0
        ),
        compiler_params=params(),
        name="key_hidden",
    )(flat_col, k, w)


def batch_kernel(rows, part_ref, told_ref):
    groups, _, size = part_ref.shape
    for t in range(0, size, 2 * TILE):
        total = jnp.sum(part_ref[:, 0, t:t + 2 * TILE], axis=0, keepdims=True) / rows
        mu = total[:, :TILE]
        inv = lax.rsqrt(total[:, TILE:] - mu * mu + bn_eps)
        told = jnp.concatenate([mu, inv], axis=1)
        told_ref[:, 0, t:t + 2 * TILE] = jnp.broadcast_to(told, (groups, 2 * TILE))


def batch(part, rows):
    return pl.pallas_call(
        lambda *refs: batch_kernel(rows, *refs),
        grid=(1,),
        in_specs=[whole(part.shape)],
        out_specs=whole(part.shape),
        out_shape=jax.ShapeDtypeStruct(part.shape, jnp.float32),
        compiler_params=params(),
        name="batch",
    )(part)


def query_kernel(x_ref, w_ref, w2_ref, n_ref, inv_ref, z_ref, q_ref, sum_ref):
    i = pl.program_id(0)
    rows = x_ref.shape[0]

    @pl.when(i == 0)
    def _():
        sum_ref[...] = jnp.zeros_like(sum_ref)

    x = x_ref[...]
    z = None
    for t in range(0, STEP, TILE):
        h = dot(x, w_ref[:, t:t + TILE])
        mu = jnp.sum(h, axis=0, keepdims=True) / rows
        inv = lax.rsqrt(jnp.sum(h * h, axis=0, keepdims=True) / rows - mu * mu + bn_eps)
        normed = ((h - mu) * inv).astype(jnp.bfloat16)
        n_ref[:, t:t + TILE] = normed
        inv_ref[:, t:t + TILE] = inv
        term = dot(jnp.maximum(normed, 0), w2_ref[t:t + TILE, :])
        z = term if z is None else z + term
    sum_ref[...] += z

    @pl.when(i == pl.num_programs(0) - 1)
    def _():
        z = sum_ref[...]
        z_ref[...] = z
        q = z * lax.rsqrt(jnp.sum(z * z, axis=-1, keepdims=True) + norm_eps)
        q_ref[...] = q.astype(jnp.bfloat16)


def query_forward(x, w, w2):
    rows, d = x.shape
    hid, emb = w2.shape
    return pl.pallas_call(
        query_kernel,
        grid=(hid // STEP,),
        in_specs=[
            whole((rows, d)),
            pl.BlockSpec((d, STEP), lambda i: (0, i)),
            pl.BlockSpec((STEP, emb), lambda i: (i, 0)),
        ],
        out_specs=[
            pl.BlockSpec((rows, STEP), lambda i: (0, i)),
            pl.BlockSpec((1, STEP), lambda i: (0, i)),
            whole((rows, emb)),
            whole((rows, emb)),
        ],
        out_shape=[
            jax.ShapeDtypeStruct((rows, hid), jnp.bfloat16),
            jax.ShapeDtypeStruct((1, hid), jnp.float32),
            jax.ShapeDtypeStruct((rows, emb), jnp.float32),
            jax.ShapeDtypeStruct((rows, emb), jnp.bfloat16),
        ],
        scratch_shapes=[pltpu.VMEM((rows, emb), jnp.float32)],
        cost_estimate=pl.CostEstimate(
            flops=2 * rows * hid * (d + emb), bytes_accessed=2 * d * hid, transcendentals=0
        ),
        compiler_params=params(),
        name="query_forward",
    )(x, w, w2)


def order_kernel(positive, order_ref, x_ref, y_ref):
    rows = y_ref.shape[2]
    core = order_ref[pl.num_programs(0)]
    t = x_ref[...]
    if positive:
        t = jnp.maximum(t, 0)
    t = t.T
    y_ref[core, 0] = t[:rows]
    y_ref[1 - core, 0] = t[rows:]


def ordered(x, order, core, blocks, positive):
    n, d = x.shape
    half = blocks // 2
    rows = d // blocks
    width = 2 * rows
    if width % 128:
        y = (jnp.maximum(x, 0) if positive else x).T.reshape(half, 2, rows, n)
        y = jnp.zeros_like(y).at[order].set(y)
        return jnp.moveaxis(jnp.where(core == 0, y, y[:, ::-1]), 1, 0).reshape(d, n)
    return pl.pallas_call(
        lambda *refs: order_kernel(positive, *refs),
        grid_spec=pltpu.PrefetchScalarGridSpec(
            num_scalar_prefetch=1,
            grid=(half,),
            in_specs=[pl.BlockSpec((n, width), lambda i, o: (0, i))],
            out_specs=pl.BlockSpec((2, 1, rows, n), lambda i, o: (0, o[i], 0, 0)),
        ),
        out_shape=jax.ShapeDtypeStruct((2, half, rows, n), x.dtype),
        cost_estimate=pl.CostEstimate(flops=0, bytes_accessed=8 * n * d, transcendentals=0),
        compiler_params=params(),
        name="ordered",
    )(jnp.append(order, core), x).reshape(d, n)


def embed_kernel(all_rows, flat_ref, h_ref, told_ref, w2_ref, zq_ref, neg_ref, dz_ref, z_ref):
    i = pl.program_id(0)
    rows, emb = zq_ref.shape

    @pl.when(i == 0)
    def _():
        z_ref[...] = jnp.zeros_like(z_ref)

    z = None
    for t in range(0, STEP, TILE):
        mu = group_spread(told_ref[:, 0, 2 * t:2 * t + TILE], rows)
        inv = group_spread(told_ref[:, 0, 2 * t + TILE:2 * t + 2 * TILE], rows)
        active = jnp.maximum((h_ref[:, t:t + TILE] - mu) * inv, 0.0).astype(jnp.bfloat16)
        term = dot(active, w2_ref[t:t + TILE, :])
        z = term if z is None else z + term
    z_ref[...] += z

    @pl.when(i == pl.num_programs(0) - 1)
    def _():
        z = z_ref[...]
        z = z * lax.rsqrt(jnp.sum(z * z, axis=-1, keepdims=True) + norm_eps)
        back = jnp.where(
            flat_ref[...] == lax.broadcasted_iota(jnp.int32, (rows, rows), 0), 1.0, 0.0
        ).astype(jnp.bfloat16)
        high = z.astype(jnp.bfloat16)
        rest = z - high.astype(jnp.float32)
        mid = rest.astype(jnp.bfloat16)
        low = (rest - mid.astype(jnp.float32)).astype(jnp.bfloat16)
        positives = dot(back, high) + dot(back, mid) + dot(back, low)
        zq = zq_ref[...]
        inv_len = lax.rsqrt(jnp.sum(zq * zq, axis=-1, keepdims=True) + norm_eps)
        q = zq * inv_len
        scale_coef = loss_scale / all_rows
        pos = jnp.sum(q * positives, axis=-1, keepdims=True) / sharpness_divisor
        exp_pos = jnp.exp(pos) * QUARTER
        total = exp_pos + jnp.sum(neg_ref[:, emb:], axis=-1, keepdims=True)
        d_pos = scale_coef * (exp_pos / total - 1.0)
        weighted = neg_ref[:, :emb] * (scale_coef / total)
        d_q = (d_pos * positives + weighted) / sharpness_divisor
        d_z = (d_q - q * jnp.sum(d_q * q, axis=-1, keepdims=True)) * inv_len
        dz_ref[...] = d_z.astype(jnp.bfloat16)


def embed(flat_row, h, told, w2, zq, negs, all_rows):
    rows, hid = h.shape
    emb = w2.shape[1]
    groups = told.shape[0]
    return pl.pallas_call(
        lambda *refs: embed_kernel(all_rows, *refs),
        grid=(hid // STEP,),
        in_specs=[
            whole((1, rows)),
            pl.BlockSpec((rows, STEP), lambda i: (0, i)),
            pl.BlockSpec((groups, 1, 2 * STEP), lambda i: (0, 0, i)),
            pl.BlockSpec((STEP, emb), lambda i: (i, 0)),
            whole((rows, emb)),
            whole(negs.shape),
        ],
        out_specs=whole((rows, emb)),
        out_shape=jax.ShapeDtypeStruct((rows, emb), jnp.bfloat16),
        scratch_shapes=[pltpu.VMEM((rows, emb), jnp.float32)],
        cost_estimate=pl.CostEstimate(
            flops=2 * rows * hid * emb, bytes_accessed=4 * rows * hid, transcendentals=0
        ),
        compiler_params=params(),
        name="embed",
    )(flat_row, h, told, w2, zq, negs)


def store_rows(out_ref, at, value, crossed):
    size = value.shape[0] // 4
    for i, j in enumerate((0, 2, 1, 3)):
        j = j if crossed else i
        out_ref[i * size:(i + 1) * size, at] = value[j * size:(j + 1) * size].astype(out_ref.dtype)


def send_kernel(plain, dz_ref, w2_ref, n_ref, inv_ref, xt_ref, at_ref, dh_ref, g_ref):
    rows = dz_ref.shape[0]
    dz = dz_ref[...]
    xt = xt_ref[...]
    cols = dh_ref.shape[1]
    for t in range(0, cols, TILE):
        normed = n_ref[:, t:t + TILE].astype(jnp.float32)
        d_norm = jnp.where(normed > 0.0, dot_t(dz, w2_ref[t:t + TILE, :]), 0.0)
        mean = jnp.sum(d_norm, axis=0, keepdims=True) / rows
        slope = jnp.sum(d_norm * normed, axis=0, keepdims=True) / rows
        d_hidden = inv_ref[:, t:t + TILE] * (d_norm - mean - normed * slope)
        d_hidden = d_hidden.astype(jnp.bfloat16)
        dh_ref[:, t:t + TILE] = d_hidden
        store_rows(g_ref, slice(t, t + TILE), dot(xt, d_hidden), t >= plain)
    if at_ref is not None:
        store_rows(g_ref, slice(cols, None), dot(at_ref[...], dz), True)


def send_half(dz, w2, normed, inv, xt, at, place, cols, plain):
    rows, emb = dz.shape
    half = xt.shape[0] // 2
    extra = 0 if at is None else emb
    operands = [dz, w2, normed, inv, xt]
    in_specs = [
        whole((rows, emb)),
        pl.BlockSpec((cols, emb), lambda i: (place, 0)),
        pl.BlockSpec((rows, cols), lambda i: (0, place)),
        pl.BlockSpec((1, cols), lambda i: (0, place)),
        pl.BlockSpec((half, rows), lambda i: (1, 0)),
    ]
    if at is None:
        kernel = lambda a, b, c, d, e, f, g: send_kernel(plain, a, b, c, d, e, None, f, g)
    else:
        kernel = lambda *refs: send_kernel(plain, *refs)
        operands.append(at)
        in_specs.append(pl.BlockSpec((half, rows), lambda i: (1, 0)))
    return pl.pallas_call(
        kernel,
        grid=(1,),
        in_specs=in_specs,
        out_specs=[whole((rows, cols)), whole((half, cols + extra))],
        out_shape=[
            jax.ShapeDtypeStruct((rows, cols), jnp.bfloat16),
            jax.ShapeDtypeStruct((half, cols + extra), jnp.bfloat16),
        ],
        cost_estimate=pl.CostEstimate(
            flops=2 * rows * half * cols, bytes_accessed=8 * rows * half, transcendentals=0
        ),
        compiler_params=params(),
        name="send_half",
    )(*operands)


def keep_kernel(plain, dz_ref, dh_ref, xt_ref, at_ref, g_ref):
    xt = xt_ref[...]
    cols = dh_ref.shape[1]
    for t in range(0, cols, TILE):
        g = dot(xt, dh_ref[:, t:t + TILE])
        store_rows(g_ref, slice(t, t + TILE), g, t >= plain)
    if at_ref is not None:
        store_rows(g_ref, slice(cols, None), dot(at_ref[...], dz_ref[...]), True)


def keep_half(dz, dh, xt, at, plain):
    rows, emb = dz.shape
    half = xt.shape[0] // 2
    cols = dh.shape[1]
    extra = 0 if at is None else emb
    operands = [dz, dh, xt]
    in_specs = [whole((rows, emb)), whole((rows, cols)), whole((half, rows))]
    if at is None:
        kernel = lambda a, b, c, d: keep_kernel(plain, a, b, c, None, d)
    else:
        kernel = lambda *refs: keep_kernel(plain, *refs)
        operands.append(at)
        in_specs.append(whole((half, rows)))
    return pl.pallas_call(
        kernel,
        grid=(1,),
        in_specs=in_specs,
        out_specs=whole((half, cols + extra)),
        out_shape=jax.ShapeDtypeStruct((half, cols + extra), jnp.float32),
        cost_estimate=pl.CostEstimate(
            flops=2 * rows * half * cols, bytes_accessed=8 * rows * half, transcendentals=0
        ),
        compiler_params=params(),
        name="keep_half",
    )(*operands)


def swap(x, axis, bit):
    size = lax.axis_size(axis)
    return lax.ppermute(x, axis, [(i, i ^ bit) for i in range(size)])


def total(parts, rows, cols):
    parts = [p[rows, cols].astype(jnp.float32) for p in parts]
    out = parts[0]
    for p in parts[1:]:
        out = out + p
    return out


def scatter_pair(keep, sent, split):
    n_dp = lax.axis_size("dp")
    length = n_dp // 2
    half = keep.shape[0]
    quarter, eighth = half // 2, half // 4
    rows = eighth // length
    every = slice(None)
    came = swap(sent, "crop", 1)
    sides = []
    for side, (first, second) in enumerate(
        ((("dp", 1), ("crop", 2)), (("crop", 2), ("dp", 1)))
    ):
        cols = slice(0, split) if side == 0 else slice(split, None)
        held = [keep[:, cols], came[:, cols]]
        out = total(held, slice(quarter, half), every).astype(jnp.bfloat16)
        held.append(swap(out, *first))
        out = total(held, slice(eighth, quarter), every).astype(jnp.bfloat16)
        held.append(swap(out, *second))
        sides.append(held)
    own = jnp.concatenate([total(held, slice(0, rows), every) for held in sides], axis=1)
    for k in range(1, length):
        out = jnp.concatenate(
            [
                total(held, slice(k * rows, (k + 1) * rows), every).astype(jnp.bfloat16)
                for held in sides
            ],
            axis=1,
        )
        own = own + swap(out, "dp", 2 * k).astype(jnp.float32)
    return own


def per_device(
    query_crops, key_crops, shuffle, distractor_bank, query_inner, query_outer, key_inner, key_outer
):
    n_dp, n_crop = lax.axis_size("dp"), lax.axis_size("crop")
    group_count = n_dp * n_crop
    row_count = query_crops.shape[0]
    hid = query_inner.shape[1]
    per_peer = row_count // group_count
    all_rows = float(row_count * group_count)

    wanted = (shuffle % row_count).reshape(group_count, per_peer)
    requested = lax.all_to_all(wanted, AXES, split_axis=0, concat_axis=0, tiled=True)
    flat_req = requested.reshape(-1)

    flat_col, flat_row = flat_req[:, None], flat_req[None, :]
    hidden_k, sums = key_hidden(flat_col, key_crops, key_inner, group_count)
    came = lax.all_to_all(sums, AXES, split_axis=0, concat_axis=0, tiled=True)

    normed, inv_q, z_q, q_low = query_forward(query_crops, query_inner, query_outer)
    came, q_low, flat_row = lax.optimization_barrier((came, q_low, flat_row))
    told = batch(came, row_count)
    told = lax.all_to_all(told, AXES, split_axis=0, concat_axis=0, tiled=True)

    negs = negatives(q_low, distractor_bank)

    length = n_dp // 2
    dp, crop = lax.axis_index("dp"), lax.axis_index("crop")
    block = lax.iota(jnp.int32, group_count // 2)
    z, x, y = block // n_crop, (block // (n_crop // 2)) % 2, block % (n_crop // 2)
    order = ((x ^ (dp % 2)) * (n_crop // 2) + (y ^ (crop // 2))) * length + (z ^ (dp // 2))
    core = crop % 2
    xt = ordered(query_crops, order, core, group_count, False)
    at = ordered(normed, order, core, group_count, True)

    told, negs, xt, at = lax.optimization_barrier((told, negs, xt, at))
    d_z = embed(flat_row, hidden_k, told, key_outer, z_q, negs, all_rows)

    outs, made = [], []
    parts = 2
    cols = hid // parts
    plain = cols // (2 * TILE) * TILE
    for i in range(parts):
        last = at if i == parts - 1 else None
        dh, sent = send_half(d_z, query_outer, normed, inv_q, xt, last, i, cols, plain)
        made.append((dh, sent, last))
    for dh, sent, last in made:
        keep = keep_half(d_z, dh, xt, last, plain)
        outs.append(scatter_pair(keep, sent, plain))
    grad = jnp.concatenate(outs, axis=1)
    return (grad[:, :hid], grad[:, hid:])


def solution(mesh):
    placed = (
        P(AXES, None),
        P(AXES, None),
        P(AXES),
        P(),
        P(),
        P(),
        P(),
        P(),
    )
    return jax.shard_map(
        per_device,
        mesh=mesh,
        in_specs=placed,
        out_specs=(P(AXES, None), P(AXES, None)),
        check_vma=False,
    )
```

```python
import math
import jax
import jax.numpy as jnp
from jax import lax
from jax.experimental import pallas as pl
from jax.experimental.pallas import tpu as pltpu
from jax.sharding import PartitionSpec as P

sharpness_divisor = 0.2
loss_scale = 4096.0
bn_eps = 1e-05
norm_eps = 1e-06
AXES = ("dp", "crop")
QUARTER = 0.25


def neg_kernel(q_ref, bank_ref, out_ref):
    rows, emb = q_ref.shape

    @pl.when(pl.program_id(0) == 0)
    def _():
        out_ref[...] = jnp.zeros_like(out_ref)

    q = q_ref[...]
    step = 512
    for j in range(bank_ref.shape[0] // step):
        bank = bank_ref[j * step:(j + 1) * step, :]
        s = lax.dot_general(q, bank, (((1,), (1,)), ((), ())), preferred_element_type=jnp.float32)
        e = jnp.exp2(s * (1.0 / (sharpness_divisor * math.log(2.0))) - 2.0)
        total = e[:, :128]
        for i in range(1, step // 128):
            total = total + e[:, i * 128:(i + 1) * 128]
        out_ref[:, emb:] += total
        out_ref[:, :emb] += jnp.dot(
            e.astype(jnp.bfloat16), bank, preferred_element_type=jnp.float32
        )


def negatives(q, bank):
    rows, emb = q.shape
    tile = 2048
    return pl.pallas_call(
        neg_kernel,
        grid=(bank.shape[0] // tile,),
        in_specs=[
            pl.BlockSpec((rows, emb), lambda i: (0, 0)),
            pl.BlockSpec((tile, emb), lambda i: (i, 0)),
        ],
        out_specs=pl.BlockSpec((rows, emb + 128), lambda i: (0, 0)),
        out_shape=jax.ShapeDtypeStruct((rows, emb + 128), jnp.float32),
        cost_estimate=pl.CostEstimate(
            flops=4 * rows * bank.shape[0] * emb,
            bytes_accessed=bank.shape[0] * emb * 2,
            transcendentals=rows * bank.shape[0],
        ),
        compiler_params=params(),
        name="negatives",
    )(q, bank)


TILE = 256
STEP = 512
MIB = 1024 * 1024
SOON = pl.CostEstimate(flops=1, bytes_accessed=1, transcendentals=0)


def params(limit=56):
    return pltpu.CompilerParams(
        dimension_semantics=("arbitrary",), vmem_limit_bytes=limit * MIB
    )


def dot(a, b):
    return jnp.dot(a, b, preferred_element_type=jnp.float32)


def dot_t(a, b):
    return lax.dot_general(a, b, (((1,), (1,)), ((), ())), preferred_element_type=jnp.float32)


def whole(shape):
    return pl.BlockSpec(shape, lambda *_: (0,) * len(shape))


def group_rows(groups, per_peer):
    rows = groups * per_peer
    row = lax.broadcasted_iota(jnp.int32, (groups, rows), 1)
    group = lax.broadcasted_iota(jnp.int32, (groups, rows), 0)
    inside = (row >= group * per_peer) & (row < (group + 1) * per_peer)
    return jnp.where(inside, 1.0, 0.0).astype(jnp.float32)


def group_sum(h, groups):
    rows, cols = h.shape
    per_peer = rows // groups
    if per_peer % 8 == 0:
        return jnp.sum(h.reshape(groups, per_peer, cols), axis=1)
    return jnp.dot(
        group_rows(groups, per_peer),
        h,
        precision=lax.Precision.HIGHEST,
        preferred_element_type=jnp.float32,
    )


def group_spread(v, rows):
    groups, cols = v.shape
    per_peer = rows // groups
    if per_peer % 8 == 0:
        return jnp.broadcast_to(v[:, None, :], (groups, per_peer, cols)).reshape(rows, cols)
    return lax.dot_general(
        group_rows(groups, per_peer),
        v,
        (((0,), (0,)), ((), ())),
        precision=lax.Precision.HIGHEST,
        preferred_element_type=jnp.float32,
    )


def key_hidden_kernel(groups, flat_ref, k_ref, w_ref, h_ref, sums_ref, sorted_ref):
    rows = k_ref.shape[0]

    @pl.when(pl.program_id(0) == 0)
    def _():
        cols = lax.broadcasted_iota(jnp.int32, (rows, rows), 1)
        pick = jnp.where(flat_ref[...] == cols, 1.0, 0.0).astype(jnp.bfloat16)
        for i in range(0, k_ref.shape[1], 512):
            sorted_ref[:, i:i + 512] = dot(pick, k_ref[:, i:i + 512]).astype(jnp.bfloat16)

    x = sorted_ref[...]
    for t in range(0, STEP, TILE):
        h = dot(x, w_ref[:, t:t + TILE])
        h_ref[:, t:t + TILE] = h
        sums_ref[:, 0, 2 * t:2 * t + TILE] = group_sum(h, groups)
        sums_ref[:, 0, 2 * t + TILE:2 * t + 2 * TILE] = group_sum(h * h, groups)


def key_hidden(flat_col, k, w, groups):
    rows, d = k.shape
    hid = w.shape[1]
    return pl.pallas_call(
        lambda *refs: key_hidden_kernel(groups, *refs),
        grid=(hid // STEP,),
        in_specs=[
            whole((rows, 1)),
            whole((rows, d)),
            pl.BlockSpec((d, STEP), lambda i: (0, i)),
        ],
        out_specs=[
            pl.BlockSpec((rows, STEP), lambda i: (0, i)),
            pl.BlockSpec((groups, 1, 2 * STEP), lambda i: (0, 0, i)),
        ],
        out_shape=[
            jax.ShapeDtypeStruct((rows, hid), jnp.float32),
            jax.ShapeDtypeStruct((groups, 1, 2 * hid), jnp.float32),
        ],
        scratch_shapes=[pltpu.VMEM((rows, d), jnp.bfloat16)],
        cost_estimate=pl.CostEstimate(
            flops=2 * rows * d * (hid + rows), bytes_accessed=2 * d * hid, transcendentals=0
        ),
        compiler_params=params(),
        name="key_hidden",
    )(flat_col, k, w)


def batch_kernel(rows, part_ref, told_ref):
    groups, _, size = part_ref.shape
    for t in range(0, size, 2 * TILE):
        total = jnp.sum(part_ref[:, 0, t:t + 2 * TILE], axis=0, keepdims=True) / rows
        mu = total[:, :TILE]
        inv = lax.rsqrt(total[:, TILE:] - mu * mu + bn_eps)
        told = jnp.concatenate([mu, inv], axis=1)
        told_ref[:, 0, t:t + 2 * TILE] = jnp.broadcast_to(told, (groups, 2 * TILE))


def batch(part, rows):
    return pl.pallas_call(
        lambda *refs: batch_kernel(rows, *refs),
        grid=(1,),
        in_specs=[whole(part.shape)],
        out_specs=whole(part.shape),
        out_shape=jax.ShapeDtypeStruct(part.shape, jnp.float32),
        compiler_params=params(),
        name="batch",
    )(part)


def query_kernel(x_ref, w_ref, w2_ref, n_ref, inv_ref, z_ref, q_ref, sum_ref):
    i = pl.program_id(0)
    rows = x_ref.shape[0]

    @pl.when(i == 0)
    def _():
        sum_ref[...] = jnp.zeros_like(sum_ref)

    x = x_ref[...]
    z = None
    for t in range(0, STEP, TILE):
        h = dot(x, w_ref[:, t:t + TILE])
        mu = jnp.sum(h, axis=0, keepdims=True) / rows
        inv = lax.rsqrt(jnp.sum(h * h, axis=0, keepdims=True) / rows - mu * mu + bn_eps)
        normed = ((h - mu) * inv).astype(jnp.bfloat16)
        n_ref[:, t:t + TILE] = normed
        inv_ref[:, t:t + TILE] = inv
        term = dot(jnp.maximum(normed, 0), w2_ref[t:t + TILE, :])
        z = term if z is None else z + term
    sum_ref[...] += z

    @pl.when(i == pl.num_programs(0) - 1)
    def _():
        z = sum_ref[...]
        z_ref[...] = z
        q = z * lax.rsqrt(jnp.sum(z * z, axis=-1, keepdims=True) + norm_eps)
        q_ref[...] = q.astype(jnp.bfloat16)


def query_forward(x, w, w2):
    rows, d = x.shape
    hid, emb = w2.shape
    return pl.pallas_call(
        query_kernel,
        grid=(hid // STEP,),
        in_specs=[
            whole((rows, d)),
            pl.BlockSpec((d, STEP), lambda i: (0, i)),
            pl.BlockSpec((STEP, emb), lambda i: (i, 0)),
        ],
        out_specs=[
            pl.BlockSpec((rows, STEP), lambda i: (0, i)),
            pl.BlockSpec((1, STEP), lambda i: (0, i)),
            whole((rows, emb)),
            whole((rows, emb)),
        ],
        out_shape=[
            jax.ShapeDtypeStruct((rows, hid), jnp.bfloat16),
            jax.ShapeDtypeStruct((1, hid), jnp.float32),
            jax.ShapeDtypeStruct((rows, emb), jnp.float32),
            jax.ShapeDtypeStruct((rows, emb), jnp.bfloat16),
        ],
        scratch_shapes=[pltpu.VMEM((rows, emb), jnp.float32)],
        cost_estimate=pl.CostEstimate(
            flops=2 * rows * hid * (d + emb), bytes_accessed=2 * d * hid, transcendentals=0
        ),
        compiler_params=params(),
        name="query_forward",
    )(x, w, w2)


def order_kernel(positive, order_ref, x_ref, y_ref):
    rows = y_ref.shape[2]
    core = order_ref[pl.num_programs(0)]
    t = x_ref[...]
    if positive:
        t = jnp.maximum(t, 0)
    t = t.T
    y_ref[core, 0] = t[:rows]
    y_ref[1 - core, 0] = t[rows:]


def ordered(x, order, core, blocks, positive):
    n, d = x.shape
    half = blocks // 2
    rows = d // blocks
    width = 2 * rows
    if width % 128:
        y = (jnp.maximum(x, 0) if positive else x).T.reshape(half, 2, rows, n)
        y = jnp.zeros_like(y).at[order].set(y)
        return jnp.moveaxis(jnp.where(core == 0, y, y[:, ::-1]), 1, 0).reshape(d, n)
    return pl.pallas_call(
        lambda *refs: order_kernel(positive, *refs),
        grid_spec=pltpu.PrefetchScalarGridSpec(
            num_scalar_prefetch=1,
            grid=(half,),
            in_specs=[pl.BlockSpec((n, width), lambda i, o: (0, i))],
            out_specs=pl.BlockSpec((2, 1, rows, n), lambda i, o: (0, o[i], 0, 0)),
        ),
        out_shape=jax.ShapeDtypeStruct((2, half, rows, n), x.dtype),
        cost_estimate=pl.CostEstimate(flops=0, bytes_accessed=8 * n * d, transcendentals=0),
        compiler_params=params(),
        name="ordered",
    )(jnp.append(order, core), x).reshape(d, n)


def embed_kernel(all_rows, flat_ref, h_ref, told_ref, w2_ref, zq_ref, neg_ref, dz_ref, z_ref):
    i = pl.program_id(0)
    rows, emb = zq_ref.shape

    @pl.when(i == 0)
    def _():
        z_ref[...] = jnp.zeros_like(z_ref)

    z = None
    for t in range(0, STEP, TILE):
        mu = group_spread(told_ref[:, 0, 2 * t:2 * t + TILE], rows)
        inv = group_spread(told_ref[:, 0, 2 * t + TILE:2 * t + 2 * TILE], rows)
        active = jnp.maximum((h_ref[:, t:t + TILE] - mu) * inv, 0.0).astype(jnp.bfloat16)
        term = dot(active, w2_ref[t:t + TILE, :])
        z = term if z is None else z + term
    z_ref[...] += z

    @pl.when(i == pl.num_programs(0) - 1)
    def _():
        z = z_ref[...]
        z = z * lax.rsqrt(jnp.sum(z * z, axis=-1, keepdims=True) + norm_eps)
        back = jnp.where(
            flat_ref[...] == lax.broadcasted_iota(jnp.int32, (rows, rows), 0), 1.0, 0.0
        ).astype(jnp.bfloat16)
        high = z.astype(jnp.bfloat16)
        rest = z - high.astype(jnp.float32)
        mid = rest.astype(jnp.bfloat16)
        low = (rest - mid.astype(jnp.float32)).astype(jnp.bfloat16)
        positives = dot(back, high) + dot(back, mid) + dot(back, low)
        zq = zq_ref[...]
        inv_len = lax.rsqrt(jnp.sum(zq * zq, axis=-1, keepdims=True) + norm_eps)
        q = zq * inv_len
        scale_coef = loss_scale / all_rows
        pos = jnp.sum(q * positives, axis=-1, keepdims=True) / sharpness_divisor
        exp_pos = jnp.exp(pos) * QUARTER
        total = exp_pos + jnp.sum(neg_ref[:, emb:], axis=-1, keepdims=True)
        d_pos = scale_coef * (exp_pos / total - 1.0)
        weighted = neg_ref[:, :emb] * (scale_coef / total)
        d_q = (d_pos * positives + weighted) / sharpness_divisor
        d_z = (d_q - q * jnp.sum(d_q * q, axis=-1, keepdims=True)) * inv_len
        dz_ref[...] = d_z.astype(jnp.bfloat16)


def embed(flat_row, h, told, w2, zq, negs, all_rows):
    rows, hid = h.shape
    emb = w2.shape[1]
    groups = told.shape[0]
    return pl.pallas_call(
        lambda *refs: embed_kernel(all_rows, *refs),
        grid=(hid // STEP,),
        in_specs=[
            whole((1, rows)),
            pl.BlockSpec((rows, STEP), lambda i: (0, i)),
            pl.BlockSpec((groups, 1, 2 * STEP), lambda i: (0, 0, i)),
            pl.BlockSpec((STEP, emb), lambda i: (i, 0)),
            whole((rows, emb)),
            whole(negs.shape),
        ],
        out_specs=whole((rows, emb)),
        out_shape=jax.ShapeDtypeStruct((rows, emb), jnp.bfloat16),
        scratch_shapes=[pltpu.VMEM((rows, emb), jnp.float32)],
        cost_estimate=pl.CostEstimate(
            flops=2 * rows * hid * emb, bytes_accessed=4 * rows * hid, transcendentals=0
        ),
        compiler_params=params(),
        name="embed",
    )(flat_row, h, told, w2, zq, negs)


def store_rows(out_ref, at, value, crossed):
    size = value.shape[0] // 4
    for i, j in enumerate((0, 2, 1, 3)):
        j = j if crossed else i
        out_ref[i * size:(i + 1) * size, at] = value[j * size:(j + 1) * size].astype(out_ref.dtype)


def column_tiles(cols):
    plain = cols // 2
    for start, end in ((0, plain), (plain, cols)):
        for t in range(start, end, TILE):
            yield slice(t, min(t + TILE, end)), start > 0


def keep_rows(keep_ref, xt_ref, dh_ref, at_ref, dz_ref):
    cols = dh_ref.shape[1]
    for at, crossed in column_tiles(cols):
        store_rows(keep_ref, at, dot(xt_ref[...], dh_ref[:, at]), crossed)
    if at_ref is not None:
        store_rows(keep_ref, slice(cols, None), dot(at_ref[...], dz_ref[...]), True)


def send_kernel(has_old, has_at, count, *refs):
    refs = list(refs)
    dz_ref, xt_ref = refs[:2]
    refs = refs[2:]
    at_ref = refs.pop(0) if has_at else None
    dz = dz_ref[...]
    rows = dz.shape[0]
    if has_old:
        old_xt_ref, old_ref = refs[:2]
        refs = refs[2:]
    ins, outs = refs[:3 * count], refs[3 * count:]
    if has_old:
        keep_rows(outs.pop(0), old_xt_ref, old_ref, None, None)
    for p in range(count):
        w2_ref, n_ref, inv_ref = ins[3 * p:3 * p + 3]
        dh_ref, sent_ref = outs[2 * p:2 * p + 2]
        cols = n_ref.shape[1]
        for at, crossed in column_tiles(cols):
            normed = n_ref[:, at].astype(jnp.float32)
            d_norm = jnp.where(normed > 0.0, dot_t(dz, w2_ref[at, :]), 0.0)
            mean = jnp.sum(d_norm, axis=0, keepdims=True) / rows
            slope = jnp.sum(d_norm * normed, axis=0, keepdims=True) / rows
            d_hidden = inv_ref[:, at] * (d_norm - mean - normed * slope)
            d_hidden = d_hidden.astype(jnp.bfloat16)
            dh_ref[:, at] = d_hidden
            store_rows(sent_ref, at, dot(xt_ref[...], d_hidden), crossed)
        if has_at and p == count - 1:
            store_rows(sent_ref, slice(cols, None), dot(at_ref[...], dz), True)


def send_half(dz, xt, at, old, w2, normed, inv, pairs):
    rows, emb = dz.shape
    half = xt.shape[0] // 2
    operands, in_specs = [dz, xt], [whole(dz.shape), pl.BlockSpec((half, rows), lambda i: (1, 0))]
    shapes = []
    if at is not None:
        operands.append(at)
        in_specs.append(pl.BlockSpec((half, rows), lambda i: (1, 0)))
    if old is not None:
        operands += [xt, old]
        in_specs += [whole((half, rows)), whole(old.shape)]
        shapes.append(jax.ShapeDtypeStruct((half, old.shape[1]), jnp.float32))
    for p, (place, cols) in enumerate(pairs):
        operands += [w2, normed, inv]
        in_specs += [
            pl.BlockSpec((cols, emb), lambda i, place=place: (place, 0)),
            pl.BlockSpec((rows, cols), lambda i, place=place: (0, place)),
            pl.BlockSpec((1, cols), lambda i, place=place: (0, place)),
        ]
        extra = emb if at is not None and p == len(pairs) - 1 else 0
        shapes.append(jax.ShapeDtypeStruct((rows, cols), jnp.bfloat16))
        shapes.append(jax.ShapeDtypeStruct((half, cols + extra), jnp.bfloat16))
    return pl.pallas_call(
        lambda *refs: send_kernel(old is not None, at is not None, len(pairs), *refs),
        grid=(1,),
        in_specs=in_specs,
        out_specs=[whole(shape.shape) for shape in shapes],
        out_shape=shapes,
        cost_estimate=pl.CostEstimate(
            flops=2 * rows * half * sum(cols for _, cols in pairs),
            bytes_accessed=8 * rows * half,
            transcendentals=0,
        ),
        compiler_params=params(36),
        name="send_half",
    )(*operands)


def keep_half(dz, dh, xt, at):
    rows, emb = dz.shape
    half = xt.shape[0] // 2
    cols = dh.shape[1]
    operands = [xt, dh]
    in_specs = [whole((half, rows)), whole((rows, cols))]
    if at is None:
        kernel = lambda x, d, g: keep_rows(g, x, d, None, None)
    else:
        kernel = lambda x, d, a, z, g: keep_rows(g, x, d, a, z)
        operands += [at, dz]
        in_specs += [whole((half, rows)), whole((rows, emb))]
        cols += emb
    return pl.pallas_call(
        kernel,
        grid=(1,),
        in_specs=in_specs,
        out_specs=whole((half, cols)),
        out_shape=jax.ShapeDtypeStruct((half, cols), jnp.float32),
        cost_estimate=pl.CostEstimate(
            flops=2 * rows * half * cols, bytes_accessed=8 * rows * half, transcendentals=0
        ),
        compiler_params=params(28),
        name="keep_half",
    )(*operands)


def swap(x, axis, bit):
    size = lax.axis_size(axis)
    return lax.ppermute(x, axis, [(i, i ^ bit) for i in range(size)])


def after(x, *others):
    return lax.optimization_barrier((x,) + others)[0]


def fold_kernel(split, joined, *refs):
    keep_ref, came_ref = refs[:2]
    count = len(refs) - 4
    sides = (refs[2:2 + count // 2], refs[2 + count // 2:2 + count])
    outs = refs[-2:]
    for side, cols in enumerate((slice(0, split), slice(split, keep_ref.shape[1]))):
        v = keep_ref[:, cols] + came_ref[:, cols].astype(jnp.float32)
        for ref in sides[side]:
            v = v + ref[...].astype(jnp.float32)
        if joined:
            half = v.shape[0] // 2
            outs[0][:, cols] = v[:half]
            outs[1][:, cols] = v[half:].astype(jnp.bfloat16)
        else:
            outs[side][...] = v.astype(jnp.bfloat16)


def fold(keep, came, left, right, split, rows, place, joined):
    cols = keep.shape[1]

    def spec(width):
        return pl.BlockSpec((rows, width), lambda i: (place, 0))

    if joined:
        shapes = [
            jax.ShapeDtypeStruct((rows // 2, cols), jnp.float32),
            jax.ShapeDtypeStruct((rows // 2, cols), jnp.bfloat16),
        ]
    else:
        shapes = [
            jax.ShapeDtypeStruct((rows, split), jnp.bfloat16),
            jax.ShapeDtypeStruct((rows, cols - split), jnp.bfloat16),
        ]
    return pl.pallas_call(
        lambda *refs: fold_kernel(split, joined, *refs),
        grid=(1,),
        in_specs=[spec(cols)] * 2 + [spec(split)] * len(left) + [spec(cols - split)] * len(right),
        out_specs=[whole(shape.shape) for shape in shapes],
        out_shape=shapes,
        cost_estimate=SOON,
        compiler_params=params(16),
        name="fold",
    )(keep, came, *left, *right)


class Pair:
    def __init__(self, keep, came, split):
        self.keep, self.came, self.split = keep, came, split
        self.left, self.right = [], []
        self.half = keep.shape[0]

    def first(self):
        rows = self.half // 2
        out = fold(self.keep, self.came, [], [], self.split, rows, 1, False)
        return out

    def cross_first(self, out):
        self.left.append(swap(out[0], "dp", 1))
        self.right.append(swap(out[1], "crop", 2))

    def second(self):
        rows = self.half // 4
        return fold(self.keep, self.came, self.left, self.right, self.split, rows, 1, False)

    def cross_second(self, out):
        self.left.append(swap(out[0], "crop", 2))
        self.right.append(swap(out[1], "dp", 1))

    def third(self):
        rows = self.half // 4
        return fold(self.keep, self.came, self.left, self.right, self.split, rows, 0, True)

    def cross_third(self, out):
        own, send = out
        length = lax.axis_size("dp") // 2
        bit = 1
        own = own + swap(send, "dp", 2 * bit).astype(jnp.float32)
        while 2 * bit < length:
            bit *= 2
            half = own.shape[0] // 2
            own, send = own[:half], own[half:].astype(jnp.bfloat16)
            own = own + swap(send, "dp", 2 * bit).astype(jnp.float32)
        return own


def per_device(
    query_crops, key_crops, shuffle, distractor_bank, query_inner, query_outer, key_inner, key_outer
):
    n_dp, n_crop = lax.axis_size("dp"), lax.axis_size("crop")
    group_count = n_dp * n_crop
    row_count = query_crops.shape[0]
    hid = query_inner.shape[1]
    per_peer = row_count // group_count
    all_rows = float(row_count * group_count)

    wanted = (shuffle % row_count).reshape(group_count, per_peer)
    requested = lax.all_to_all(wanted, AXES, split_axis=0, concat_axis=0, tiled=True)
    flat_req = requested.reshape(-1)

    flat_col, flat_row = flat_req[:, None], flat_req[None, :]
    hidden_k, sums = key_hidden(flat_col, key_crops, key_inner, group_count)
    came = lax.all_to_all(sums, AXES, split_axis=0, concat_axis=0, tiled=True)

    length = n_dp // 2
    bits = length.bit_length() - 1
    dp, crop = lax.axis_index("dp"), lax.axis_index("crop")
    block = lax.iota(jnp.int32, group_count // 2)
    z, x, y = block // n_crop, (block // (n_crop // 2)) % 2, block % (n_crop // 2)
    order = (x ^ (dp % 2)) * (n_crop // 2) + (y ^ (crop // 2))
    for bit in range(bits):
        order = order * 2 + (((z ^ (dp // 2)) >> bit) & 1)
    core = crop % 2

    normed, inv_q, z_q, q_low = query_forward(
        after(query_crops, sums), query_inner, query_outer
    )
    xt = ordered(query_crops, order, core, group_count, False)
    came, q_low, flat_row, xt = lax.optimization_barrier((came, q_low, flat_row, xt))
    told = batch(came, row_count)
    told = lax.all_to_all(told, AXES, split_axis=0, concat_axis=0, tiled=True)

    negs = negatives(q_low, distractor_bank)
    at = ordered(normed, order, core, group_count, True)

    told, negs, at = lax.optimization_barrier((told, negs, at))
    d_z = embed(flat_row, hidden_k, told, key_outer, z_q, negs, all_rows)

    def send(last, old, pairs):
        return send_half(d_z, xt, last, old, query_outer, normed, inv_q, pairs)

    large = hid // 8 * 3
    small = hid - 2 * large
    dh_1, sent_1 = send(None, None, [(0, large)])
    came_1 = swap(sent_1, "crop", 1)
    keep_1, dh_2, sent_2, dh_3, sent_3 = send(
        at, dh_1, [(1, large), (2 * large // small, small)]
    )
    came_2 = swap(sent_2, "crop", 1)
    came_3 = swap(sent_3, "crop", 1)
    one = Pair(keep_1, came_1, large // 2)
    a_1 = lax.optimization_barrier(one.first())
    one.cross_first(a_1)
    keep_2 = keep_half(d_z, after(dh_2, *a_1), xt, None)
    two = Pair(keep_2, came_2, large // 2)
    a_2 = lax.optimization_barrier(two.first())
    two.cross_first(a_2)
    keep_3 = keep_half(d_z, after(dh_3, *a_2), xt, at)
    one.left[0] = after(one.left[0], keep_3)
    b_1 = lax.optimization_barrier(one.second())
    one.cross_second(b_1)
    three = Pair(keep_3, after(came_3, *b_1), small // 2)
    a_3 = lax.optimization_barrier(three.first())
    three.cross_first(a_3)
    two.left[0] = after(two.left[0], *a_3)
    b_2 = lax.optimization_barrier(two.second())
    two.cross_second(b_2)
    one.left[1] = after(one.left[1], *b_2)
    c_1 = lax.optimization_barrier(one.third())
    three.left[0] = after(three.left[0], *c_1)
    b_3 = lax.optimization_barrier(three.second())
    three.cross_second(b_3)
    own_1 = one.cross_third(c_1)
    two.left[1] = after(two.left[1], *b_3)
    own_2 = two.cross_third(two.third())
    own_3 = three.cross_third(three.third())
    grad_inner = jnp.concatenate([own_1, own_2, own_3[:, :small]], axis=1)
    return (grad_inner, own_3[:, small:])


def solution(mesh):
    placed = (
        P(AXES, None),
        P(AXES, None),
        P(AXES),
        P(),
        P(),
        P(),
        P(),
        P(),
    )
    return jax.shard_map(
        per_device,
        mesh=mesh,
        in_specs=placed,
        out_specs=(P(AXES, None), P(AXES, None)),
        check_vma=False,
    )
```

```python
import math
import jax
import jax.numpy as jnp
from jax import lax
from jax.experimental import pallas as pl
from jax.experimental.pallas import tpu as pltpu
from jax.sharding import PartitionSpec as P

sharpness_divisor = 0.2
loss_scale = 4096.0
bn_eps = 1e-05
norm_eps = 1e-06
AXES = ("dp", "crop")
QUARTER = 0.25


def neg_kernel(q_ref, bank_ref, out_ref):
    rows, emb = q_ref.shape

    @pl.when(pl.program_id(0) == 0)
    def _():
        out_ref[...] = jnp.zeros_like(out_ref)

    q = q_ref[...]
    step = 512
    for j in range(bank_ref.shape[0] // step):
        bank = bank_ref[j * step:(j + 1) * step, :]
        s = lax.dot_general(q, bank, (((1,), (1,)), ((), ())), preferred_element_type=jnp.float32)
        e = jnp.exp2(s * (1.0 / (sharpness_divisor * math.log(2.0))) - 2.0)
        total = e[:, :128]
        for i in range(1, step // 128):
            total = total + e[:, i * 128:(i + 1) * 128]
        out_ref[:, emb:] += total
        out_ref[:, :emb] += jnp.dot(
            e.astype(jnp.bfloat16), bank, preferred_element_type=jnp.float32
        )


def negatives(q, bank):
    rows, emb = q.shape
    tile = 2048
    return pl.pallas_call(
        neg_kernel,
        grid=(bank.shape[0] // tile,),
        in_specs=[
            pl.BlockSpec((rows, emb), lambda i: (0, 0)),
            pl.BlockSpec((tile, emb), lambda i: (i, 0)),
        ],
        out_specs=pl.BlockSpec((rows, emb + 128), lambda i: (0, 0)),
        out_shape=jax.ShapeDtypeStruct((rows, emb + 128), jnp.float32),
        cost_estimate=pl.CostEstimate(
            flops=4 * rows * bank.shape[0] * emb,
            bytes_accessed=bank.shape[0] * emb * 2,
            transcendentals=rows * bank.shape[0],
        ),
        compiler_params=params(),
        name="negatives",
    )(q, bank)


TILE = 256
STEP = 512
MIB = 1024 * 1024
SOON = pl.CostEstimate(flops=1, bytes_accessed=1, transcendentals=0)


def params(limit=24):
    return pltpu.CompilerParams(
        dimension_semantics=("arbitrary",), vmem_limit_bytes=limit * MIB
    )


def dot(a, b):
    return jnp.dot(a, b, preferred_element_type=jnp.float32)


def dot_t(a, b):
    return lax.dot_general(a, b, (((1,), (1,)), ((), ())), preferred_element_type=jnp.float32)


def whole(shape):
    return pl.BlockSpec(shape, lambda *_: (0,) * len(shape))


def group_rows(groups, per_peer):
    rows = groups * per_peer
    row = lax.broadcasted_iota(jnp.int32, (groups, rows), 1)
    group = lax.broadcasted_iota(jnp.int32, (groups, rows), 0)
    inside = (row >= group * per_peer) & (row < (group + 1) * per_peer)
    return jnp.where(inside, 1.0, 0.0).astype(jnp.float32)


def group_sum(h, groups):
    rows, cols = h.shape
    per_peer = rows // groups
    if per_peer % 8 == 0:
        return jnp.sum(h.reshape(groups, per_peer, cols), axis=1)
    return jnp.dot(
        group_rows(groups, per_peer),
        h,
        precision=lax.Precision.HIGHEST,
        preferred_element_type=jnp.float32,
    )


def group_spread(v, rows):
    groups, cols = v.shape
    per_peer = rows // groups
    if per_peer % 8 == 0:
        return jnp.broadcast_to(v[:, None, :], (groups, per_peer, cols)).reshape(rows, cols)
    return lax.dot_general(
        group_rows(groups, per_peer),
        v,
        (((0,), (0,)), ((), ())),
        precision=lax.Precision.HIGHEST,
        preferred_element_type=jnp.float32,
    )


def key_hidden_kernel(groups, flat_ref, k_ref, w_ref, h_ref, sums_ref, sorted_ref):
    rows = k_ref.shape[0]

    @pl.when(pl.program_id(0) == 0)
    def _():
        cols = lax.broadcasted_iota(jnp.int32, (rows, rows), 1)
        pick = jnp.where(flat_ref[...] == cols, 1.0, 0.0).astype(jnp.bfloat16)
        for i in range(0, k_ref.shape[1], 512):
            sorted_ref[:, i:i + 512] = dot(pick, k_ref[:, i:i + 512]).astype(jnp.bfloat16)

    x = sorted_ref[...]
    for t in range(0, STEP, TILE):
        h = dot(x, w_ref[:, t:t + TILE])
        h_ref[:, t:t + TILE] = h
        sums_ref[:, 0, 2 * t:2 * t + TILE] = group_sum(h, groups)
        sums_ref[:, 0, 2 * t + TILE:2 * t + 2 * TILE] = group_sum(h * h, groups)


def key_hidden(flat_col, k, w, groups):
    rows, d = k.shape
    hid = w.shape[1]
    return pl.pallas_call(
        lambda *refs: key_hidden_kernel(groups, *refs),
        grid=(hid // STEP,),
        in_specs=[
            whole((rows, 1)),
            whole((rows, d)),
            pl.BlockSpec((d, STEP), lambda i: (0, i)),
        ],
        out_specs=[
            pl.BlockSpec((rows, STEP), lambda i: (0, i)),
            pl.BlockSpec((groups, 1, 2 * STEP), lambda i: (0, 0, i)),
        ],
        out_shape=[
            jax.ShapeDtypeStruct((rows, hid), jnp.float32),
            jax.ShapeDtypeStruct((groups, 1, 2 * hid), jnp.float32),
        ],
        scratch_shapes=[pltpu.VMEM((rows, d), jnp.bfloat16)],
        cost_estimate=pl.CostEstimate(
            flops=2 * rows * d * (hid + rows), bytes_accessed=2 * d * hid, transcendentals=0
        ),
        compiler_params=params(),
        name="key_hidden",
    )(flat_col, k, w)


def batch_kernel(rows, part_ref, told_ref):
    groups, _, size = part_ref.shape
    for t in range(0, size, 2 * TILE):
        total = jnp.sum(part_ref[:, 0, t:t + 2 * TILE], axis=0, keepdims=True) / rows
        mu = total[:, :TILE]
        inv = lax.rsqrt(total[:, TILE:] - mu * mu + bn_eps)
        told = jnp.concatenate([mu, inv], axis=1)
        told_ref[:, 0, t:t + 2 * TILE] = jnp.broadcast_to(told, (groups, 2 * TILE))


def batch(part, rows):
    return pl.pallas_call(
        lambda *refs: batch_kernel(rows, *refs),
        grid=(1,),
        in_specs=[whole(part.shape)],
        out_specs=whole(part.shape),
        out_shape=jax.ShapeDtypeStruct(part.shape, jnp.float32),
        compiler_params=params(),
        name="batch",
    )(part)


def query_kernel(x_ref, w_ref, w2_ref, n_ref, inv_ref, z_ref, q_ref, sum_ref):
    i = pl.program_id(0)
    rows = x_ref.shape[0]

    @pl.when(i == 0)
    def _():
        sum_ref[...] = jnp.zeros_like(sum_ref)

    x = x_ref[...]
    z = None
    for t in range(0, STEP, TILE):
        h = dot(x, w_ref[:, t:t + TILE])
        mu = jnp.sum(h, axis=0, keepdims=True) / rows
        inv = lax.rsqrt(jnp.sum(h * h, axis=0, keepdims=True) / rows - mu * mu + bn_eps)
        normed = ((h - mu) * inv).astype(jnp.bfloat16)
        n_ref[:, t:t + TILE] = normed
        inv_ref[:, t:t + TILE] = inv
        term = dot(jnp.maximum(normed, 0), w2_ref[t:t + TILE, :])
        z = term if z is None else z + term
    sum_ref[...] += z

    @pl.when(i == pl.num_programs(0) - 1)
    def _():
        z = sum_ref[...]
        z_ref[...] = z
        q = z * lax.rsqrt(jnp.sum(z * z, axis=-1, keepdims=True) + norm_eps)
        q_ref[...] = q.astype(jnp.bfloat16)


def query_forward(x, w, w2):
    rows, d = x.shape
    hid, emb = w2.shape
    return pl.pallas_call(
        query_kernel,
        grid=(hid // STEP,),
        in_specs=[
            whole((rows, d)),
            pl.BlockSpec((d, STEP), lambda i: (0, i)),
            pl.BlockSpec((STEP, emb), lambda i: (i, 0)),
        ],
        out_specs=[
            pl.BlockSpec((rows, STEP), lambda i: (0, i)),
            pl.BlockSpec((1, STEP), lambda i: (0, i)),
            whole((rows, emb)),
            whole((rows, emb)),
        ],
        out_shape=[
            jax.ShapeDtypeStruct((rows, hid), jnp.bfloat16),
            jax.ShapeDtypeStruct((1, hid), jnp.float32),
            jax.ShapeDtypeStruct((rows, emb), jnp.float32),
            jax.ShapeDtypeStruct((rows, emb), jnp.bfloat16),
        ],
        scratch_shapes=[pltpu.VMEM((rows, emb), jnp.float32)],
        cost_estimate=pl.CostEstimate(
            flops=2 * rows * hid * (d + emb), bytes_accessed=2 * d * hid, transcendentals=0
        ),
        compiler_params=params(),
        name="query_forward",
    )(x, w, w2)


def order_kernel(positive, order_ref, x_ref, y_ref):
    rows = y_ref.shape[2]
    core = order_ref[pl.num_programs(0)]
    t = x_ref[...]
    if positive:
        t = jnp.maximum(t, 0)
    t = t.T
    y_ref[core, 0] = t[:rows]
    y_ref[1 - core, 0] = t[rows:]


def ordered(x, order, core, blocks, positive):
    n, d = x.shape
    half = blocks // 2
    rows = d // blocks
    width = 2 * rows
    if width % 128:
        y = (jnp.maximum(x, 0) if positive else x).T.reshape(half, 2, rows, n)
        y = jnp.zeros_like(y).at[order].set(y)
        return jnp.moveaxis(jnp.where(core == 0, y, y[:, ::-1]), 1, 0).reshape(d, n)
    return pl.pallas_call(
        lambda *refs: order_kernel(positive, *refs),
        grid_spec=pltpu.PrefetchScalarGridSpec(
            num_scalar_prefetch=1,
            grid=(half,),
            in_specs=[pl.BlockSpec((n, width), lambda i, o: (0, i))],
            out_specs=pl.BlockSpec((2, 1, rows, n), lambda i, o: (0, o[i], 0, 0)),
        ),
        out_shape=jax.ShapeDtypeStruct((2, half, rows, n), x.dtype),
        cost_estimate=pl.CostEstimate(flops=0, bytes_accessed=8 * n * d, transcendentals=0),
        compiler_params=params(),
        name="ordered",
    )(jnp.append(order, core), x).reshape(d, n)


def embed_kernel(all_rows, flat_ref, h_ref, told_ref, w2_ref, zq_ref, neg_ref, dz_ref, z_ref):
    i = pl.program_id(0)
    rows, emb = zq_ref.shape

    @pl.when(i == 0)
    def _():
        z_ref[...] = jnp.zeros_like(z_ref)

    z = None
    for t in range(0, STEP, TILE):
        mu = group_spread(told_ref[:, 0, 2 * t:2 * t + TILE], rows)
        inv = group_spread(told_ref[:, 0, 2 * t + TILE:2 * t + 2 * TILE], rows)
        active = jnp.maximum((h_ref[:, t:t + TILE] - mu) * inv, 0.0).astype(jnp.bfloat16)
        term = dot(active, w2_ref[t:t + TILE, :])
        z = term if z is None else z + term
    z_ref[...] += z

    @pl.when(i == pl.num_programs(0) - 1)
    def _():
        z = z_ref[...]
        z = z * lax.rsqrt(jnp.sum(z * z, axis=-1, keepdims=True) + norm_eps)
        back = jnp.where(
            flat_ref[...] == lax.broadcasted_iota(jnp.int32, (rows, rows), 0), 1.0, 0.0
        ).astype(jnp.bfloat16)
        high = z.astype(jnp.bfloat16)
        rest = z - high.astype(jnp.float32)
        mid = rest.astype(jnp.bfloat16)
        low = (rest - mid.astype(jnp.float32)).astype(jnp.bfloat16)
        positives = dot(back, high) + dot(back, mid) + dot(back, low)
        zq = zq_ref[...]
        inv_len = lax.rsqrt(jnp.sum(zq * zq, axis=-1, keepdims=True) + norm_eps)
        q = zq * inv_len
        scale_coef = loss_scale / all_rows
        pos = jnp.sum(q * positives, axis=-1, keepdims=True) / sharpness_divisor
        exp_pos = jnp.exp(pos) * QUARTER
        total = exp_pos + jnp.sum(neg_ref[:, emb:], axis=-1, keepdims=True)
        d_pos = scale_coef * (exp_pos / total - 1.0)
        weighted = neg_ref[:, :emb] * (scale_coef / total)
        d_q = (d_pos * positives + weighted) / sharpness_divisor
        d_z = (d_q - q * jnp.sum(d_q * q, axis=-1, keepdims=True)) * inv_len
        dz_ref[...] = d_z.astype(jnp.bfloat16)


def embed(flat_row, h, told, w2, zq, negs, all_rows):
    rows, hid = h.shape
    emb = w2.shape[1]
    groups = told.shape[0]
    return pl.pallas_call(
        lambda *refs: embed_kernel(all_rows, *refs),
        grid=(hid // STEP,),
        in_specs=[
            whole((1, rows)),
            pl.BlockSpec((rows, STEP), lambda i: (0, i)),
            pl.BlockSpec((groups, 1, 2 * STEP), lambda i: (0, 0, i)),
            pl.BlockSpec((STEP, emb), lambda i: (i, 0)),
            whole((rows, emb)),
            whole(negs.shape),
        ],
        out_specs=whole((rows, emb)),
        out_shape=jax.ShapeDtypeStruct((rows, emb), jnp.bfloat16),
        scratch_shapes=[pltpu.VMEM((rows, emb), jnp.float32)],
        cost_estimate=pl.CostEstimate(
            flops=2 * rows * hid * emb, bytes_accessed=4 * rows * hid, transcendentals=0
        ),
        compiler_params=params(),
        name="embed",
    )(flat_row, h, told, w2, zq, negs)


def store_rows(out_ref, at, value, crossed):
    size = value.shape[0] // 4
    for i, j in enumerate((0, 2, 1, 3)):
        j = j if crossed else i
        out_ref[i * size:(i + 1) * size, at] = value[j * size:(j + 1) * size].astype(out_ref.dtype)


def column_tiles(cols):
    plain = cols // 2
    for start, end in ((0, plain), (plain, cols)):
        for t in range(start, end, TILE):
            yield slice(t, min(t + TILE, end)), start > 0


def keep_rows(keep_ref, xt_ref, dh_ref, at_ref, dz_ref):
    cols = dh_ref.shape[1]
    for at, crossed in column_tiles(cols):
        store_rows(keep_ref, at, dot(xt_ref[...], dh_ref[:, at]), crossed)
    if at_ref is not None:
        store_rows(keep_ref, slice(cols, None), dot(at_ref[...], dz_ref[...]), True)


def keep_some(quarters, keep_ref, xt_ref, dh_ref, at_ref, dz_ref):
    cols = dh_ref.shape[1]
    size = xt_ref.shape[0] // 4

    def make(at, ref, other, crossed):
        for i, quarter in enumerate(quarters):
            j = (0, 2, 1, 3)[quarter] if crossed else quarter
            keep_ref[i * size:(i + 1) * size, at] = dot(ref[j * size:(j + 1) * size, :], other)

    for at, crossed in column_tiles(cols):
        make(at, xt_ref, dh_ref[:, at], crossed)
    make(slice(cols, None), at_ref, dz_ref[...], True)


def send_kernel(has_old, has_at, count, *refs):
    refs = list(refs)
    dz_ref, xt_ref = refs[:2]
    refs = refs[2:]
    at_ref = refs.pop(0) if has_at else None
    dz = dz_ref[...]
    rows = dz.shape[0]
    if has_old:
        old_xt_ref, old_ref = refs[:2]
        refs = refs[2:]
    ins, outs = refs[:3 * count], refs[3 * count:]
    if has_old:
        keep_rows(outs.pop(0), old_xt_ref, old_ref, None, None)
    for p in range(count):
        w2_ref, n_ref, inv_ref = ins[3 * p:3 * p + 3]
        dh_ref, sent_ref = outs[2 * p:2 * p + 2]
        cols = n_ref.shape[1]
        for at, crossed in column_tiles(cols):
            normed = n_ref[:, at].astype(jnp.float32)
            d_norm = jnp.where(normed > 0.0, dot_t(dz, w2_ref[at, :]), 0.0)
            mean = jnp.sum(d_norm, axis=0, keepdims=True) / rows
            slope = jnp.sum(d_norm * normed, axis=0, keepdims=True) / rows
            d_hidden = inv_ref[:, at] * (d_norm - mean - normed * slope)
            d_hidden = d_hidden.astype(jnp.bfloat16)
            dh_ref[:, at] = d_hidden
            store_rows(sent_ref, at, dot(xt_ref[...], d_hidden), crossed)
        if has_at and p == count - 1:
            store_rows(sent_ref, slice(cols, None), dot(at_ref[...], dz), True)


def send_half(dz, xt, at, old, w2, normed, inv, pairs):
    rows, emb = dz.shape
    half = xt.shape[0] // 2
    operands, in_specs = [dz, xt], [whole(dz.shape), pl.BlockSpec((half, rows), lambda i: (1, 0))]
    shapes = []
    if at is not None:
        operands.append(at)
        in_specs.append(pl.BlockSpec((half, rows), lambda i: (1, 0)))
    if old is not None:
        operands += [xt, old]
        in_specs += [whole((half, rows)), whole(old.shape)]
        shapes.append(jax.ShapeDtypeStruct((half, old.shape[1]), jnp.float32))
    for p, (place, cols) in enumerate(pairs):
        operands += [w2, normed, inv]
        in_specs += [
            pl.BlockSpec((cols, emb), lambda i, place=place: (place, 0)),
            pl.BlockSpec((rows, cols), lambda i, place=place: (0, place)),
            pl.BlockSpec((1, cols), lambda i, place=place: (0, place)),
        ]
        extra = emb if at is not None and p == len(pairs) - 1 else 0
        shapes.append(jax.ShapeDtypeStruct((rows, cols), jnp.bfloat16))
        shapes.append(jax.ShapeDtypeStruct((half, cols + extra), jnp.bfloat16))
    return pl.pallas_call(
        lambda *refs: send_kernel(old is not None, at is not None, len(pairs), *refs),
        grid=(1,),
        in_specs=in_specs,
        out_specs=[whole(shape.shape) for shape in shapes],
        out_shape=shapes,
        cost_estimate=pl.CostEstimate(
            flops=2 * rows * half * sum(cols for _, cols in pairs),
            bytes_accessed=8 * rows * half,
            transcendentals=0,
        ),
        compiler_params=params(36),
        name="send_half",
    )(*operands)


def keep_half(dz, dh, xt, at, quarters):
    rows, emb = dz.shape
    half = xt.shape[0] // 2
    cols = dh.shape[1]
    operands = [xt, dh]
    in_specs = [whole((half, rows)), whole((rows, cols))]
    made = half
    if at is None:
        kernel = lambda x, d, g: keep_rows(g, x, d, None, None)
    else:
        kernel = lambda x, d, a, z, g: keep_some(quarters, g, x, d, a, z)
        operands += [at, dz]
        in_specs += [whole((half, rows)), whole((rows, emb))]
        cols += emb
        made = half // 4 * len(quarters)
    return pl.pallas_call(
        kernel,
        grid=(1,),
        in_specs=in_specs,
        out_specs=whole((made, cols)),
        out_shape=jax.ShapeDtypeStruct((made, cols), jnp.float32),
        cost_estimate=pl.CostEstimate(
            flops=2 * rows * made * cols, bytes_accessed=8 * rows * half, transcendentals=0
        ),
        compiler_params=params(28),
        name="keep_half",
    )(*operands)


def swap(x, axis, bit):
    size = lax.axis_size(axis)
    return lax.ppermute(x, axis, [(i, i ^ bit) for i in range(size)])


def after(x, *others):
    return lax.optimization_barrier((x,) + others)[0]


def fold_kernel(split, joined, *refs):
    keep_ref, came_ref = refs[:2]
    count = len(refs) - 4
    sides = (refs[2:2 + count // 2], refs[2 + count // 2:2 + count])
    outs = refs[-2:]
    for side, cols in enumerate((slice(0, split), slice(split, keep_ref.shape[1]))):
        v = keep_ref[:, cols] + came_ref[:, cols].astype(jnp.float32)
        for ref in sides[side]:
            v = v + ref[...].astype(jnp.float32)
        if joined:
            half = v.shape[0] // 2
            outs[0][:, cols] = v[:half]
            outs[1][:, cols] = v[half:].astype(jnp.bfloat16)
        else:
            outs[side][...] = v.astype(jnp.bfloat16)


def fold(keep, came, left, right, split, rows, place, joined, keep_place):
    cols = keep.shape[1]

    def spec(width, place=place):
        return pl.BlockSpec((rows, width), lambda i: (place, 0))

    if joined:
        shapes = [
            jax.ShapeDtypeStruct((rows // 2, cols), jnp.float32),
            jax.ShapeDtypeStruct((rows // 2, cols), jnp.bfloat16),
        ]
    else:
        shapes = [
            jax.ShapeDtypeStruct((rows, split), jnp.bfloat16),
            jax.ShapeDtypeStruct((rows, cols - split), jnp.bfloat16),
        ]
    return pl.pallas_call(
        lambda *refs: fold_kernel(split, joined, *refs),
        grid=(1,),
        in_specs=[spec(cols, keep_place), spec(cols)] + [spec(split)] * len(left) + [spec(cols - split)] * len(right),
        out_specs=[whole(shape.shape) for shape in shapes],
        out_shape=shapes,
        cost_estimate=SOON,
        compiler_params=params(16),
        name="fold",
    )(keep, came, *left, *right)


class Pair:
    def __init__(self, keep, came, split):
        self.keep, self.came, self.split = keep, came, split
        self.left, self.right = [], []
        self.half = came.shape[0]

    def add(self, rows, place, joined):
        keep, keep_place = self.keep, place
        if isinstance(keep, list):
            keep, keep_place = keep[len(self.left)], 0
        return fold(
            keep, self.came, self.left, self.right, self.split, rows, place, joined, keep_place
        )

    def hold(self, *others):
        self.left[-1], self.right[-1] = lax.optimization_barrier(
            (self.left[-1], self.right[-1]) + others
        )[:2]

    def first(self):
        return self.add(self.half // 2, 1, False)

    def cross_first(self, out):
        self.left.append(swap(out[0], "dp", 1))
        self.right.append(swap(out[1], "crop", 2))

    def second(self):
        return self.add(self.half // 4, 1, False)

    def cross_second(self, out):
        self.left.append(swap(out[0], "crop", 2))
        self.right.append(swap(out[1], "dp", 1))

    def third(self):
        return self.add(self.half // 4, 0, True)

    def cross_third(self, out):
        own, send = out
        return own + swap(send, "dp", 2).astype(jnp.float32)

    def cross_rest(self, own):
        length = lax.axis_size("dp") // 2
        bit = 1
        while 2 * bit < length:
            bit *= 2
            half = own.shape[0] // 2
            own, send = own[:half], own[half:].astype(jnp.bfloat16)
            own = own + swap(send, "dp", 2 * bit).astype(jnp.float32)
        return own


def per_device(
    query_crops, key_crops, shuffle, distractor_bank, query_inner, query_outer, key_inner, key_outer
):
    n_dp, n_crop = lax.axis_size("dp"), lax.axis_size("crop")
    group_count = n_dp * n_crop
    row_count = query_crops.shape[0]
    hid = query_inner.shape[1]
    per_peer = row_count // group_count
    all_rows = float(row_count * group_count)

    wanted = (shuffle % row_count).reshape(group_count, per_peer)
    requested = lax.all_to_all(wanted, AXES, split_axis=0, concat_axis=0, tiled=True)
    flat_req = requested.reshape(-1)

    flat_col, flat_row = flat_req[:, None], flat_req[None, :]
    hidden_k, sums = key_hidden(flat_col, key_crops, key_inner, group_count)
    came = lax.all_to_all(sums, AXES, split_axis=0, concat_axis=0, tiled=True)

    length = n_dp // 2
    bits = length.bit_length() - 1
    dp, crop = lax.axis_index("dp"), lax.axis_index("crop")
    block = lax.iota(jnp.int32, group_count // 2)
    z, x, y = block // n_crop, (block // (n_crop // 2)) % 2, block % (n_crop // 2)
    order = (x ^ (dp % 2)) * (n_crop // 2) + (y ^ (crop // 2))
    for bit in range(bits):
        order = order * 2 + (((z ^ (dp // 2)) >> bit) & 1)
    core = crop % 2

    normed, inv_q, z_q, q_low = query_forward(
        after(query_crops, sums), query_inner, query_outer
    )
    xt = ordered(query_crops, order, core, group_count, False)
    came, q_low, flat_row, xt = lax.optimization_barrier((came, q_low, flat_row, xt))
    told = batch(came, row_count)
    told = lax.all_to_all(told, AXES, split_axis=0, concat_axis=0, tiled=True)

    negs = negatives(q_low, distractor_bank)
    at = ordered(normed, order, core, group_count, True)

    told, negs, at = lax.optimization_barrier((told, negs, at))
    d_z = embed(flat_row, hidden_k, told, key_outer, z_q, negs, all_rows)

    def send(last, old, pairs):
        return send_half(d_z, xt, last, old, query_outer, normed, inv_q, pairs)

    large = hid // 8 * 3
    small = hid - 2 * large
    dh_1, sent_1 = send(None, None, [(0, large)])
    came_1 = swap(sent_1, "crop", 1)
    keep_1, dh_2, sent_2, dh_3, sent_3 = send(
        at, dh_1, [(1, large), (2 * large // small, small)]
    )
    came_2 = swap(sent_2, "crop", 1)
    came_3 = swap(sent_3, "crop", 1)
    one = Pair(keep_1, came_1, large // 2)
    a_1 = lax.optimization_barrier(one.first())
    one.cross_first(a_1)
    keep_2 = keep_half(d_z, after(dh_2, *a_1), xt, None, None)
    two = Pair(keep_2, came_2, large // 2)
    a_2 = lax.optimization_barrier(two.first())
    two.cross_first(a_2)
    three = Pair([keep_half(d_z, after(dh_3, *a_2), xt, at, (2, 3))], came_3, small // 2)
    a_3 = lax.optimization_barrier(three.first())
    three.cross_first(a_3)
    three.keep.append(keep_half(d_z, after(dh_3, *a_3), xt, at, (1,)))
    one.hold(three.keep[1])
    b_1 = lax.optimization_barrier(one.second())
    one.cross_second(b_1)
    three.keep.append(keep_half(d_z, after(dh_3, *b_1), xt, at, (0,)))
    two.hold(three.keep[2])
    b_2 = lax.optimization_barrier(two.second())
    two.cross_second(b_2)
    three.hold(*b_2)
    b_3 = lax.optimization_barrier(three.second())
    three.cross_second(b_3)
    one.hold(*b_3)
    c_1 = lax.optimization_barrier(one.third())
    two.hold(*c_1)
    c_2 = lax.optimization_barrier(two.third())
    own_1 = lax.optimization_barrier(one.cross_third(c_1))
    three.hold(own_1, *c_2)
    c_3 = lax.optimization_barrier(three.third())
    own_1 = one.cross_rest(own_1)
    own_2 = two.cross_rest(two.cross_third(c_2))
    own_3 = three.cross_rest(three.cross_third(c_3))
    grad_inner = jnp.concatenate([own_1, own_2, own_3[:, :small]], axis=1)
    return (grad_inner, own_3[:, small:])


def solution(mesh):
    placed = (
        P(AXES, None),
        P(AXES, None),
        P(AXES),
        P(),
        P(),
        P(),
        P(),
        P(),
    )
    return jax.shard_map(
        per_device,
        mesh=mesh,
        in_specs=placed,
        out_specs=(P(AXES, None), P(AXES, None)),
        check_vma=False,
    )
```

```python
import math
import jax
import jax.numpy as jnp
from jax import lax
from jax.experimental import pallas as pl
from jax.experimental.pallas import tpu as pltpu
from jax.sharding import PartitionSpec as P

sharpness_divisor = 0.2
loss_scale = 4096.0
bn_eps = 1e-05
norm_eps = 1e-06
AXES = ("dp", "crop")
QUARTER = 0.25


def neg_kernel(q_ref, bank_ref, out_ref):
    rows, emb = q_ref.shape

    @pl.when(pl.program_id(0) == 0)
    def _():
        out_ref[...] = jnp.zeros_like(out_ref)

    q = q_ref[...]
    step = 512
    for j in range(bank_ref.shape[0] // step):
        bank = bank_ref[j * step:(j + 1) * step, :]
        s = lax.dot_general(q, bank, (((1,), (1,)), ((), ())), preferred_element_type=jnp.float32)
        e = jnp.exp2(s * (1.0 / (sharpness_divisor * math.log(2.0))) - 2.0)
        total = e[:, :128]
        for i in range(1, step // 128):
            total = total + e[:, i * 128:(i + 1) * 128]
        out_ref[:, emb:] += total
        out_ref[:, :emb] += jnp.dot(
            e.astype(jnp.bfloat16), bank, preferred_element_type=jnp.float32
        )


def negatives(q, bank):
    rows, emb = q.shape
    tile = 2048
    return pl.pallas_call(
        neg_kernel,
        grid=(bank.shape[0] // tile,),
        in_specs=[
            pl.BlockSpec((rows, emb), lambda i: (0, 0)),
            pl.BlockSpec((tile, emb), lambda i: (i, 0)),
        ],
        out_specs=pl.BlockSpec((rows, emb + 128), lambda i: (0, 0)),
        out_shape=jax.ShapeDtypeStruct((rows, emb + 128), jnp.float32),
        cost_estimate=pl.CostEstimate(
            flops=4 * rows * bank.shape[0] * emb,
            bytes_accessed=bank.shape[0] * emb * 2,
            transcendentals=rows * bank.shape[0],
        ),
        compiler_params=params(44),
        name="negatives",
    )(q, bank)


TILE = 256
STEP = 512
MIB = 1024 * 1024
SOON = pl.CostEstimate(flops=1, bytes_accessed=1, transcendentals=0)


def params(limit=24):
    return pltpu.CompilerParams(
        dimension_semantics=("arbitrary",), vmem_limit_bytes=limit * MIB
    )


def dot(a, b):
    return jnp.dot(a, b, preferred_element_type=jnp.float32)


def dot_t(a, b):
    return lax.dot_general(a, b, (((1,), (1,)), ((), ())), preferred_element_type=jnp.float32)


def whole(shape):
    return pl.BlockSpec(shape, lambda *_: (0,) * len(shape))


def group_rows(groups, per_peer):
    rows = groups * per_peer
    row = lax.broadcasted_iota(jnp.int32, (groups, rows), 1)
    group = lax.broadcasted_iota(jnp.int32, (groups, rows), 0)
    inside = (row >= group * per_peer) & (row < (group + 1) * per_peer)
    return jnp.where(inside, 1.0, 0.0).astype(jnp.float32)


def group_sum(h, groups):
    rows, cols = h.shape
    per_peer = rows // groups
    if per_peer % 8 == 0:
        return jnp.sum(h.reshape(groups, per_peer, cols), axis=1)
    return jnp.dot(
        group_rows(groups, per_peer),
        h,
        precision=lax.Precision.HIGHEST,
        preferred_element_type=jnp.float32,
    )


def group_spread(v, rows):
    groups, cols = v.shape
    per_peer = rows // groups
    if per_peer % 8 == 0:
        return jnp.broadcast_to(v[:, None, :], (groups, per_peer, cols)).reshape(rows, cols)
    return lax.dot_general(
        group_rows(groups, per_peer),
        v,
        (((0,), (0,)), ((), ())),
        precision=lax.Precision.HIGHEST,
        preferred_element_type=jnp.float32,
    )


def key_hidden_kernel(groups, flat_ref, k_ref, w_ref, h_ref, sums_ref, sorted_ref):
    rows = k_ref.shape[0]

    @pl.when(pl.program_id(0) == 0)
    def _():
        cols = lax.broadcasted_iota(jnp.int32, (rows, rows), 1)
        pick = jnp.where(flat_ref[...] == cols, 1.0, 0.0).astype(jnp.bfloat16)
        for i in range(0, k_ref.shape[1], 512):
            sorted_ref[:, i:i + 512] = dot(pick, k_ref[:, i:i + 512]).astype(jnp.bfloat16)

    x = sorted_ref[...]
    for t in range(0, STEP, TILE):
        h = dot(x, w_ref[:, t:t + TILE])
        h_ref[:, t:t + TILE] = h
        sums_ref[:, 0, 2 * t:2 * t + TILE] = group_sum(h, groups)
        sums_ref[:, 0, 2 * t + TILE:2 * t + 2 * TILE] = group_sum(h * h, groups)


def key_hidden(flat_col, k, w, groups):
    rows, d = k.shape
    hid = w.shape[1]
    return pl.pallas_call(
        lambda *refs: key_hidden_kernel(groups, *refs),
        grid=(hid // STEP,),
        in_specs=[
            whole((rows, 1)),
            whole((rows, d)),
            pl.BlockSpec((d, STEP), lambda i: (0, i)),
        ],
        out_specs=[
            pl.BlockSpec((rows, STEP), lambda i: (0, i)),
            pl.BlockSpec((groups, 1, 2 * STEP), lambda i: (0, 0, i)),
        ],
        out_shape=[
            jax.ShapeDtypeStruct((rows, hid), jnp.float32),
            jax.ShapeDtypeStruct((groups, 1, 2 * hid), jnp.float32),
        ],
        scratch_shapes=[pltpu.VMEM((rows, d), jnp.bfloat16)],
        cost_estimate=pl.CostEstimate(
            flops=2 * rows * d * (hid + rows), bytes_accessed=2 * d * hid, transcendentals=0
        ),
        compiler_params=params(50),
        name="key_hidden",
    )(flat_col, k, w)


def batch_kernel(rows, part_ref, told_ref):
    groups, _, size = part_ref.shape
    for t in range(0, size, 2 * TILE):
        total = jnp.sum(part_ref[:, 0, t:t + 2 * TILE], axis=0, keepdims=True) / rows
        mu = total[:, :TILE]
        inv = lax.rsqrt(total[:, TILE:] - mu * mu + bn_eps)
        told = jnp.concatenate([mu, inv], axis=1)
        told_ref[:, 0, t:t + 2 * TILE] = jnp.broadcast_to(told, (groups, 2 * TILE))


def batch(part, rows):
    return pl.pallas_call(
        lambda *refs: batch_kernel(rows, *refs),
        grid=(1,),
        in_specs=[whole(part.shape)],
        out_specs=whole(part.shape),
        out_shape=jax.ShapeDtypeStruct(part.shape, jnp.float32),
        compiler_params=params(),
        name="batch",
    )(part)


def place_rows(order_ref, which, first, rows, t, out_ref):
    for i in range(t.shape[0] // (2 * rows)):
        at = order_ref[which, first + i]
        core = order_ref[2, 0]
        out_ref[core, at] = t[2 * i * rows:(2 * i + 1) * rows]
        out_ref[1 - core, at] = t[(2 * i + 1) * rows:(2 * i + 2) * rows]


def query_kernel(
    rows_of_block, order_ref, x_ref, w_ref, w2_ref,
    n_ref, inv_ref, z_ref, q_ref, xt_ref, xt3_ref, at3_ref, sum_ref,
):
    i = pl.program_id(0)
    rows = x_ref.shape[0]

    @pl.when(i == 0)
    def _():
        sum_ref[...] = jnp.zeros_like(sum_ref)

    x = x_ref[...]
    z = None
    for t in range(0, STEP, TILE):
        h = dot(x, w_ref[:, t:t + TILE])
        mu = jnp.sum(h, axis=0, keepdims=True) / rows
        inv = lax.rsqrt(jnp.sum(h * h, axis=0, keepdims=True) / rows - mu * mu + bn_eps)
        normed = ((h - mu) * inv).astype(jnp.bfloat16)
        n_ref[:, t:t + TILE] = normed
        inv_ref[:, t:t + TILE] = inv
        active = jnp.maximum(normed, 0)
        term = dot(active, w2_ref[t:t + TILE, :])
        z = term if z is None else z + term
        block = (i * STEP + t) // (2 * rows_of_block)
        own = x_ref[:, pl.ds(pl.multiple_of(i * STEP + t, TILE), TILE)].T
        place_rows(order_ref, 0, block, rows_of_block, own, xt_ref)
        place_rows(order_ref, 1, block, rows_of_block, own, xt3_ref)
        place_rows(order_ref, 1, block, rows_of_block, active.T, at3_ref)
    sum_ref[...] += z

    @pl.when(i == pl.num_programs(0) - 1)
    def _():
        z = sum_ref[...]
        z_ref[...] = z
        q = z * lax.rsqrt(jnp.sum(z * z, axis=-1, keepdims=True) + norm_eps)
        q_ref[...] = q.astype(jnp.bfloat16)


def query_forward(order, blocks, x, w, w2):
    rows, d = x.shape
    hid, emb = w2.shape
    half, size = blocks // 2, d // blocks
    turned = jax.ShapeDtypeStruct((2, half, size, rows), jnp.bfloat16)
    out = pl.pallas_call(
        lambda *refs: query_kernel(size, *refs),
        grid_spec=pltpu.PrefetchScalarGridSpec(
            num_scalar_prefetch=1,
            grid=(hid // STEP,),
            in_specs=[
                whole((rows, d)),
                pl.BlockSpec((d, STEP), lambda i, o: (0, i)),
                pl.BlockSpec((STEP, emb), lambda i, o: (i, 0)),
            ],
            out_specs=[
                pl.BlockSpec((rows, STEP), lambda i, o: (0, i)),
                pl.BlockSpec((1, STEP), lambda i, o: (0, i)),
                whole((rows, emb)),
                whole((rows, emb)),
                whole(turned.shape),
                whole(turned.shape),
                whole(turned.shape),
            ],
            scratch_shapes=[pltpu.VMEM((rows, emb), jnp.float32)],
        ),
        out_shape=[
            jax.ShapeDtypeStruct((rows, hid), jnp.bfloat16),
            jax.ShapeDtypeStruct((1, hid), jnp.float32),
            jax.ShapeDtypeStruct((rows, emb), jnp.float32),
            jax.ShapeDtypeStruct((rows, emb), jnp.bfloat16),
            turned,
            turned,
            turned,
        ],
        cost_estimate=pl.CostEstimate(
            flops=2 * rows * hid * (d + emb), bytes_accessed=2 * d * hid, transcendentals=0
        ),
        compiler_params=params(44),
        name="query_forward",
    )(order, x, w, w2)
    return (*out[:4], *(t.reshape(d, rows) for t in out[4:]))


def embed_kernel(all_rows, flat_ref, h_ref, told_ref, w2_ref, zq_ref, neg_ref, dz_ref, z_ref):
    i = pl.program_id(0)
    rows, emb = zq_ref.shape

    @pl.when(i == 0)
    def _():
        z_ref[...] = jnp.zeros_like(z_ref)

    z = None
    for t in range(0, STEP, TILE):
        mu = group_spread(told_ref[:, 0, 2 * t:2 * t + TILE], rows)
        inv = group_spread(told_ref[:, 0, 2 * t + TILE:2 * t + 2 * TILE], rows)
        active = jnp.maximum((h_ref[:, t:t + TILE] - mu) * inv, 0.0).astype(jnp.bfloat16)
        term = dot(active, w2_ref[t:t + TILE, :])
        z = term if z is None else z + term
    z_ref[...] += z

    @pl.when(i == pl.num_programs(0) - 1)
    def _():
        z = z_ref[...]
        z = z * lax.rsqrt(jnp.sum(z * z, axis=-1, keepdims=True) + norm_eps)
        back = jnp.where(
            flat_ref[...] == lax.broadcasted_iota(jnp.int32, (rows, rows), 0), 1.0, 0.0
        ).astype(jnp.bfloat16)
        high = z.astype(jnp.bfloat16)
        rest = z - high.astype(jnp.float32)
        mid = rest.astype(jnp.bfloat16)
        low = (rest - mid.astype(jnp.float32)).astype(jnp.bfloat16)
        positives = dot(back, high) + dot(back, mid) + dot(back, low)
        zq = zq_ref[...]
        inv_len = lax.rsqrt(jnp.sum(zq * zq, axis=-1, keepdims=True) + norm_eps)
        q = zq * inv_len
        scale_coef = loss_scale / all_rows
        pos = jnp.sum(q * positives, axis=-1, keepdims=True) / sharpness_divisor
        exp_pos = jnp.exp(pos) * QUARTER
        total = exp_pos + jnp.sum(neg_ref[:, emb:], axis=-1, keepdims=True)
        d_pos = scale_coef * (exp_pos / total - 1.0)
        weighted = neg_ref[:, :emb] * (scale_coef / total)
        d_q = (d_pos * positives + weighted) / sharpness_divisor
        d_z = (d_q - q * jnp.sum(d_q * q, axis=-1, keepdims=True)) * inv_len
        dz_ref[...] = d_z.astype(jnp.bfloat16)


def embed(flat_row, h, told, w2, zq, negs, all_rows):
    rows, hid = h.shape
    emb = w2.shape[1]
    groups = told.shape[0]
    return pl.pallas_call(
        lambda *refs: embed_kernel(all_rows, *refs),
        grid=(hid // STEP,),
        in_specs=[
            whole((1, rows)),
            pl.BlockSpec((rows, STEP), lambda i: (0, i)),
            pl.BlockSpec((groups, 1, 2 * STEP), lambda i: (0, 0, i)),
            pl.BlockSpec((STEP, emb), lambda i: (i, 0)),
            whole((rows, emb)),
            whole(negs.shape),
        ],
        out_specs=whole((rows, emb)),
        out_shape=jax.ShapeDtypeStruct((rows, emb), jnp.bfloat16),
        scratch_shapes=[pltpu.VMEM((rows, emb), jnp.float32)],
        cost_estimate=pl.CostEstimate(
            flops=2 * rows * hid * emb, bytes_accessed=4 * rows * hid, transcendentals=0
        ),
        compiler_params=params(30),
        name="embed",
    )(flat_row, h, told, w2, zq, negs)


def store_rows(out_ref, at, value, crossed, size):
    if not crossed:
        out_ref[:, at] = value.astype(out_ref.dtype)
        return
    for four in range(0, value.shape[0], 4 * size):
        for i, j in enumerate((0, 2, 1, 3)):
            i, j = four + i * size, four + j * size
            out_ref[i:i + size, at] = value[j:j + size].astype(out_ref.dtype)


def column_tiles(cols):
    plain = cols // 2
    for start, end in ((0, plain), (plain, cols)):
        for t in range(start, end, TILE):
            yield slice(t, min(t + TILE, end)), start > 0


def keep_rows(keep_ref, xt_ref, dh_ref, size, at_ref=None, dz_ref=None):
    cols = dh_ref.shape[1]
    for at, crossed in column_tiles(cols):
        store_rows(keep_ref, at, dot(xt_ref[...], dh_ref[:, at]), crossed, size)
    if at_ref is not None:
        store_rows(keep_ref, slice(cols, None), dot(at_ref[...], dz_ref[...]), True, size)


def send_kernel(sizes, has_old, has_at, *refs):
    refs = list(refs)
    count = len(sizes)
    dz_ref = refs.pop(0)
    at_ref = refs.pop(0) if has_at else None
    dz = dz_ref[...]
    rows = dz.shape[0]
    if has_old:
        old_xt_ref, old_ref = refs[:2]
        refs = refs[2:]
    ins, outs = refs[:4 * count], refs[4 * count:]
    if has_old:
        keep_rows(outs.pop(0), old_xt_ref, old_ref, sizes[0])
    for p in range(count):
        xt_ref, w2_ref, n_ref, inv_ref = ins[4 * p:4 * p + 4]
        dh_ref, sent_ref = outs[2 * p:2 * p + 2]
        cols = n_ref.shape[1]
        for at, crossed in column_tiles(cols):
            normed = n_ref[:, at].astype(jnp.float32)
            d_norm = jnp.where(normed > 0.0, dot_t(dz, w2_ref[at, :]), 0.0)
            mean = jnp.sum(d_norm, axis=0, keepdims=True) / rows
            slope = jnp.sum(d_norm * normed, axis=0, keepdims=True) / rows
            d_hidden = inv_ref[:, at] * (d_norm - mean - normed * slope)
            d_hidden = d_hidden.astype(jnp.bfloat16)
            dh_ref[:, at] = d_hidden
            store_rows(sent_ref, at, dot(xt_ref[...], d_hidden), crossed, sizes[p])
        if has_at and p == count - 1:
            store_rows(sent_ref, slice(cols, None), dot(at_ref[...], dz), True, sizes[p])


def send_half(dz, at, old, w2, normed, inv, pairs):
    rows, emb = dz.shape
    operands, in_specs, shapes = [dz], [whole(dz.shape)], []
    if at is not None:
        half = at.shape[0] // 2
        operands.append(at)
        in_specs.append(pl.BlockSpec((half, rows), lambda i: (1, 0)))
    if old is not None:
        half = old[0].shape[0] // 2
        operands += list(old)
        in_specs += [whole((half, rows)), whole(old[1].shape)]
        shapes.append(jax.ShapeDtypeStruct((half, old[1].shape[1]), jnp.float32))
    for p, (xt, place, cols, _) in enumerate(pairs):
        half = xt.shape[0] // 2
        operands += [xt, w2, normed, inv]
        in_specs += [
            pl.BlockSpec((half, rows), lambda i: (1, 0)),
            pl.BlockSpec((cols, emb), lambda i, place=place: (place, 0)),
            pl.BlockSpec((rows, cols), lambda i, place=place: (0, place)),
            pl.BlockSpec((1, cols), lambda i, place=place: (0, place)),
        ]
        extra = emb if at is not None and p == len(pairs) - 1 else 0
        shapes.append(jax.ShapeDtypeStruct((rows, cols), jnp.bfloat16))
        shapes.append(jax.ShapeDtypeStruct((half, cols + extra), jnp.bfloat16))
    sizes = [size for *_, size in pairs]
    return pl.pallas_call(
        lambda *refs: send_kernel(sizes, old is not None, at is not None, *refs),
        grid=(1,),
        in_specs=in_specs,
        out_specs=[whole(shape.shape) for shape in shapes],
        out_shape=shapes,
        cost_estimate=pl.CostEstimate(
            flops=2 * rows * half * sum(cols for _, _, cols, _ in pairs),
            bytes_accessed=8 * rows * half,
            transcendentals=0,
        ),
        compiler_params=params(36),
        name="send_half",
    )(*operands)


def keep_half(dz, dh, xt, at, size, made, place):
    rows, emb = dz.shape
    cols = dh.shape[1]
    block = pl.BlockSpec((made, rows), lambda i: (place, 0))
    operands = [xt, dh]
    in_specs = [block, whole((rows, cols))]
    if at is None:
        kernel = lambda x, d, g: keep_rows(g, x, d, size)
    else:
        kernel = lambda x, d, a, z, g: keep_rows(g, x, d, size, a, z)
        operands += [at, dz]
        in_specs += [block, whole((rows, emb))]
        cols += emb
    return pl.pallas_call(
        kernel,
        grid=(1,),
        in_specs=in_specs,
        out_specs=whole((made, cols)),
        out_shape=jax.ShapeDtypeStruct((made, cols), jnp.float32),
        cost_estimate=pl.CostEstimate(
            flops=2 * rows * made * cols, bytes_accessed=8 * rows * made, transcendentals=0
        ),
        compiler_params=params(28),
        name="keep_half",
    )(*operands)


def swap(x, axis, bit):
    size = lax.axis_size(axis)
    return lax.ppermute(x, axis, [(i, i ^ bit) for i in range(size)])


def after(x, *others):
    return lax.optimization_barrier((x,) + others)[0]


def fold_kernel(split, form, counts, *refs):
    both, left, right = counts
    joined = refs[:both]
    sides = (refs[both:both + left], refs[both + left:both + left + right])
    outs = refs[both + left + right:]
    for side, cols in enumerate((slice(0, split), slice(split, refs[0].shape[1]))):
        v = joined[0][:, cols].astype(jnp.float32)
        for ref in joined[1:]:
            v = v + ref[:, cols].astype(jnp.float32)
        for ref in sides[side]:
            v = v + ref[...].astype(jnp.float32)
        if form == "halves":
            half = v.shape[0] // 2
            outs[0][:, cols] = v[:half]
            outs[1][:, cols] = v[half:].astype(jnp.bfloat16)
        elif form == "sides":
            outs[side][...] = v.astype(jnp.bfloat16)
        else:
            outs[0][:, cols] = v.astype(outs[0].dtype)


def fold(keep, keep_place, both, left, right, split, rows, place, form):
    cols = keep.shape[1]

    def spec(width, place=place):
        return pl.BlockSpec((rows, width), lambda i: (place, 0))

    low, full = jnp.bfloat16, jnp.float32
    shapes = {
        "halves": [((rows // 2, cols), full), ((rows // 2, cols), low)],
        "sides": [((rows, split), low), ((rows, cols - split), low)],
        "send": [((rows, cols), low)],
        "own": [((rows, cols), full)],
    }[form]
    in_specs = [spec(cols, keep_place)] + [spec(cols)] * len(both)
    in_specs += [spec(split)] * len(left) + [spec(cols - split)] * len(right)
    return pl.pallas_call(
        lambda *refs: fold_kernel(split, form, (1 + len(both), len(left), len(right)), *refs),
        grid=(1,),
        in_specs=in_specs,
        out_specs=[whole(shape) for shape, _ in shapes],
        out_shape=[jax.ShapeDtypeStruct(*shape) for shape in shapes],
        cost_estimate=SOON,
        compiler_params=params(16),
        name="fold",
    )(keep, *both, *left, *right)


class Pair:
    def __init__(self, keep, came, split):
        self.keep, self.both, self.split = keep, [came], split
        self.left, self.right = [], []

    def hold(self, *others):
        for came in (self.both, self.left, self.right):
            if came:
                came[-1] = after(came[-1], *others)

    def add(self, rows, place, form):
        keep, keep_place = self.keep, place
        if isinstance(keep, list):
            keep, start = keep[-1]
            keep_place = (place * rows - start) // rows
        out = fold(
            keep, keep_place, self.both, self.left, self.right, self.split, rows, place, form
        )
        return lax.optimization_barrier(out)

    def cross_first(self, out):
        self.left.append(swap(out[0], "dp", 1))
        self.right.append(swap(out[1], "crop", 2))

    def cross_second(self, out):
        self.left.append(swap(out[0], "crop", 2))
        self.right.append(swap(out[1], "dp", 1))

    def cross_line_apart(self, out):
        self.left.append(swap(out[0], "dp", 2))
        self.right.append(swap(out[1], "dp", 2))

    def cross_line(self, out, bit):
        self.both.append(swap(out[0], "dp", 2 * bit))

    def cross_third(self, out):
        own, send = out
        return own + swap(send, "dp", 2).astype(jnp.float32)

    def cross_rest(self, own):
        length = lax.axis_size("dp") // 2
        bit = 1
        while 2 * bit < length:
            bit *= 2
            half = own.shape[0] // 2
            own, send = own[:half], own[half:].astype(jnp.bfloat16)
            own = own + swap(send, "dp", 2 * bit).astype(jnp.float32)
        return own


def per_device(
    query_crops, key_crops, shuffle, distractor_bank, query_inner, query_outer, key_inner, key_outer
):
    n_dp, n_crop = lax.axis_size("dp"), lax.axis_size("crop")
    group_count = n_dp * n_crop
    row_count = query_crops.shape[0]
    hid = query_inner.shape[1]
    per_peer = row_count // group_count
    all_rows = float(row_count * group_count)

    wanted = (shuffle % row_count).reshape(group_count, per_peer)
    requested = lax.all_to_all(wanted, AXES, split_axis=0, concat_axis=0, tiled=True)
    flat_req = requested.reshape(-1)

    flat_col, flat_row = flat_req[:, None], flat_req[None, :]
    hidden_k, sums = key_hidden(flat_col, key_crops, key_inner, group_count)
    came = lax.all_to_all(sums, AXES, split_axis=0, concat_axis=0, tiled=True)

    length = n_dp // 2
    bits = length.bit_length() - 1
    dp, crop = lax.axis_index("dp"), lax.axis_index("crop")
    block = lax.iota(jnp.int32, group_count // 2)
    z, x, y = block // n_crop, (block // (n_crop // 2)) % 2, block % (n_crop // 2)
    plane = (x ^ (dp % 2)) * (n_crop // 2) + (y ^ (crop // 2))
    line = jnp.zeros_like(block)
    for bit in range(bits):
        line = line * 2 + (((z ^ (dp // 2)) >> bit) & 1)
    order = jnp.stack(
        [plane * length + line, line * n_crop + plane, jnp.full_like(block, crop % 2)]
    )

    normed, inv_q, z_q, q_low, xt, xt3, at3 = query_forward(
        order, group_count, after(query_crops, sums), query_inner, query_outer
    )
    came, q_low, flat_row = lax.optimization_barrier((came, q_low, flat_row))
    told = batch(came, row_count)
    told = lax.all_to_all(told, AXES, split_axis=0, concat_axis=0, tiled=True)

    negs = negatives(q_low, distractor_bank)
    told, negs = lax.optimization_barrier((told, negs))
    d_z = embed(flat_row, hidden_k, told, key_outer, z_q, negs, all_rows)

    def send(last, old, pairs):
        return send_half(d_z, last, old, query_outer, normed, inv_q, pairs)

    large = hid // 8 * 3
    small = hid - 2 * large
    half = xt.shape[0] // 2
    size, size_3 = half // 4, half // (4 * length)
    dh_1, sent_1 = send(None, None, [(xt, 0, large, size)])
    came_1 = swap(sent_1, "crop", 1)
    keep_1, dh_2, sent_2, dh_3, sent_3 = send(
        at3, (xt, dh_1), [(xt, 1, large, size), (xt3, 2 * large // small, small, size_3)]
    )
    came_2 = swap(sent_2, "crop", 1)
    came_3 = swap(sent_3, "crop", 1)
    one = Pair(keep_1, came_1, large // 2)
    a_1 = one.add(half // 2, 1, "sides")
    one.cross_first(a_1)
    keep_2 = keep_half(d_z, after(dh_2, *a_1), xt, None, size, half, 0)
    two = Pair(keep_2, came_2, large // 2)
    a_2 = two.add(half // 2, 1, "sides")
    two.cross_first(a_2)
    upper = keep_half(d_z, after(dh_3, *a_2), xt3, at3, size_3, half // 2, 1)
    three = Pair([(upper, half // 2)], came_3, small // 2)
    rows = half // 2
    l_3 = three.add(rows, 1, "sides")
    three.cross_line_apart(l_3)
    lower = keep_half(d_z, after(dh_3, *l_3), xt3, at3, size_3, half // 4, 1)
    one.hold(lower)
    b_1 = one.add(half // 4, 1, "sides")
    one.cross_second(b_1)
    lowest = keep_half(d_z, after(dh_3, *b_1), xt3, at3, size_3, half // 4, 0)
    two.hold(lowest)
    b_2 = two.add(half // 4, 1, "sides")
    two.cross_second(b_2)
    held = b_2
    for bit in range(1, bits):
        rows //= 2
        three.hold(*held)
        three.keep = [(lower, half // 4) if bit == 1 else (lowest, 0)]
        held = three.add(rows, 1, "send")
        three.cross_line(held, 2 ** bit)
    one.hold(*held)
    c_1 = one.add(half // 4, 0, "halves")
    two.hold(*c_1)
    c_2 = two.add(half // 4, 0, "halves")
    own_1 = lax.optimization_barrier(one.cross_third(c_1))
    own_2 = lax.optimization_barrier(two.cross_third(c_2))
    three.keep = [(lowest, 0)]
    three.hold(own_1, own_2)
    rows //= 2
    e_3 = three.add(rows, 1, "sides")
    three.cross_first(e_3)
    rows //= 2
    f_3 = three.add(rows, 1, "sides")
    three.cross_second(f_3)
    own_1 = one.cross_rest(own_1)
    own_2 = two.cross_rest(own_2)
    own_3 = three.add(rows, 0, "own")[0]
    grad_inner = jnp.concatenate([own_1, own_2, own_3[:, :small]], axis=1)
    return (grad_inner, own_3[:, small:])


def solution(mesh):
    placed = (
        P(AXES, None),
        P(AXES, None),
        P(AXES),
        P(),
        P(),
        P(),
        P(),
        P(),
    )
    return jax.shard_map(
        per_device,
        mesh=mesh,
        in_specs=placed,
        out_specs=(P(AXES, None), P(AXES, None)),
        check_vma=False,
    )
```

```python
import math
import jax
import jax.numpy as jnp
from jax import lax
from jax.experimental import pallas as pl
from jax.experimental.pallas import tpu as pltpu
from jax.sharding import PartitionSpec as P

sharpness_divisor = 0.2
loss_scale = 4096.0
bn_eps = 1e-05
norm_eps = 1e-06
AXES = ("dp", "crop")
QUARTER = 0.25


def neg_kernel(q_ref, bank_ref, out_ref):
    rows, emb = q_ref.shape

    @pl.when(pl.program_id(0) == 0)
    def _():
        out_ref[...] = jnp.zeros_like(out_ref)

    q = q_ref[...]
    step = 512
    for j in range(bank_ref.shape[0] // step):
        bank = bank_ref[j * step:(j + 1) * step, :]
        s = lax.dot_general(q, bank, (((1,), (1,)), ((), ())), preferred_element_type=jnp.float32)
        e = jnp.exp2(s * (1.0 / (sharpness_divisor * math.log(2.0))) - 2.0)
        total = e[:, :128]
        for i in range(1, step // 128):
            total = total + e[:, i * 128:(i + 1) * 128]
        out_ref[:, emb:] += total
        out_ref[:, :emb] += jnp.dot(
            e.astype(jnp.bfloat16), bank, preferred_element_type=jnp.float32
        )


def negatives(q, bank):
    rows, emb = q.shape
    tile = 2048
    return pl.pallas_call(
        neg_kernel,
        grid=(bank.shape[0] // tile,),
        in_specs=[
            pl.BlockSpec((rows, emb), lambda i: (0, 0)),
            pl.BlockSpec((tile, emb), lambda i: (i, 0)),
        ],
        out_specs=pl.BlockSpec((rows, emb + 128), lambda i: (0, 0)),
        out_shape=jax.ShapeDtypeStruct((rows, emb + 128), jnp.float32),
        cost_estimate=pl.CostEstimate(
            flops=4 * rows * bank.shape[0] * emb,
            bytes_accessed=bank.shape[0] * emb * 2,
            transcendentals=rows * bank.shape[0],
        ),
        compiler_params=params(44),
        name="negatives",
    )(q, bank)


TILE = 256
STEP = 512
MIB = 1024 * 1024
SOON = pl.CostEstimate(flops=1, bytes_accessed=1, transcendentals=0)


def params(limit=24):
    return pltpu.CompilerParams(
        dimension_semantics=("arbitrary",), vmem_limit_bytes=limit * MIB
    )


def dot(a, b):
    return jnp.dot(a, b, preferred_element_type=jnp.float32)


def dot_t(a, b):
    return lax.dot_general(a, b, (((1,), (1,)), ((), ())), preferred_element_type=jnp.float32)


def whole(shape):
    return pl.BlockSpec(shape, lambda *_: (0,) * len(shape))


def group_rows(groups, per_peer):
    rows = groups * per_peer
    row = lax.broadcasted_iota(jnp.int32, (groups, rows), 1)
    group = lax.broadcasted_iota(jnp.int32, (groups, rows), 0)
    inside = (row >= group * per_peer) & (row < (group + 1) * per_peer)
    return jnp.where(inside, 1.0, 0.0).astype(jnp.float32)


def group_sum(h, groups):
    rows, cols = h.shape
    per_peer = rows // groups
    if per_peer % 8 == 0:
        return jnp.sum(h.reshape(groups, per_peer, cols), axis=1)
    return jnp.dot(
        group_rows(groups, per_peer),
        h,
        precision=lax.Precision.HIGHEST,
        preferred_element_type=jnp.float32,
    )


def group_spread(v, rows):
    groups, cols = v.shape
    per_peer = rows // groups
    if per_peer % 8 == 0:
        return jnp.broadcast_to(v[:, None, :], (groups, per_peer, cols)).reshape(rows, cols)
    return lax.dot_general(
        group_rows(groups, per_peer),
        v,
        (((0,), (0,)), ((), ())),
        precision=lax.Precision.HIGHEST,
        preferred_element_type=jnp.float32,
    )


def key_hidden_kernel(groups, flat_ref, k_ref, w_ref, h_ref, sums_ref, sorted_ref):
    rows = k_ref.shape[0]

    @pl.when(pl.program_id(0) == 0)
    def _():
        cols = lax.broadcasted_iota(jnp.int32, (rows, rows), 1)
        pick = jnp.where(flat_ref[...] == cols, 1.0, 0.0).astype(jnp.bfloat16)
        for i in range(0, k_ref.shape[1], 512):
            sorted_ref[:, i:i + 512] = dot(pick, k_ref[:, i:i + 512]).astype(jnp.bfloat16)

    x = sorted_ref[...]
    for t in range(0, STEP, TILE):
        h = dot(x, w_ref[:, t:t + TILE])
        h_ref[:, t:t + TILE] = h
        sums_ref[:, 0, 2 * t:2 * t + TILE] = group_sum(h, groups)
        sums_ref[:, 0, 2 * t + TILE:2 * t + 2 * TILE] = group_sum(h * h, groups)


def key_hidden(flat_col, k, w, groups):
    rows, d = k.shape
    hid = w.shape[1]
    return pl.pallas_call(
        lambda *refs: key_hidden_kernel(groups, *refs),
        grid=(hid // STEP,),
        in_specs=[
            whole((rows, 1)),
            whole((rows, d)),
            pl.BlockSpec((d, STEP), lambda i: (0, i)),
        ],
        out_specs=[
            pl.BlockSpec((rows, STEP), lambda i: (0, i)),
            pl.BlockSpec((groups, 1, 2 * STEP), lambda i: (0, 0, i)),
        ],
        out_shape=[
            jax.ShapeDtypeStruct((rows, hid), jnp.float32),
            jax.ShapeDtypeStruct((groups, 1, 2 * hid), jnp.float32),
        ],
        scratch_shapes=[pltpu.VMEM((rows, d), jnp.bfloat16)],
        cost_estimate=pl.CostEstimate(
            flops=2 * rows * d * (hid + rows), bytes_accessed=2 * d * hid, transcendentals=0
        ),
        compiler_params=params(50),
        name="key_hidden",
    )(flat_col, k, w)


def batch_kernel(rows, part_ref, told_ref):
    groups, _, size = part_ref.shape
    for t in range(0, size, 2 * TILE):
        total = jnp.sum(part_ref[:, 0, t:t + 2 * TILE], axis=0, keepdims=True) / rows
        mu = total[:, :TILE]
        inv = lax.rsqrt(total[:, TILE:] - mu * mu + bn_eps)
        told = jnp.concatenate([mu, inv], axis=1)
        told_ref[:, 0, t:t + 2 * TILE] = jnp.broadcast_to(told, (groups, 2 * TILE))


def batch(part, rows):
    return pl.pallas_call(
        lambda *refs: batch_kernel(rows, *refs),
        grid=(1,),
        in_specs=[whole(part.shape)],
        out_specs=whole(part.shape),
        out_shape=jax.ShapeDtypeStruct(part.shape, jnp.float32),
        compiler_params=params(),
        name="batch",
    )(part)


def place_rows(order_ref, which, first, rows, t, out_ref):
    for i in range(t.shape[0] // (2 * rows)):
        at = order_ref[which, first + i]
        core = order_ref[2, 0]
        out_ref[core, at] = t[2 * i * rows:(2 * i + 1) * rows]
        out_ref[1 - core, at] = t[(2 * i + 1) * rows:(2 * i + 2) * rows]


def query_kernel(
    rows_of_block, order_ref, x_ref, w_ref, w2_ref,
    n_ref, inv_ref, z_ref, q_ref, xt_ref, xt3_ref, at3_ref, sum_ref,
):
    i = pl.program_id(0)
    rows = x_ref.shape[0]

    @pl.when(i == 0)
    def _():
        sum_ref[...] = jnp.zeros_like(sum_ref)

    x = x_ref[...]
    z = None
    for t in range(0, STEP, TILE):
        h = dot(x, w_ref[:, t:t + TILE])
        mu = jnp.sum(h, axis=0, keepdims=True) / rows
        inv = lax.rsqrt(jnp.sum(h * h, axis=0, keepdims=True) / rows - mu * mu + bn_eps)
        normed = ((h - mu) * inv).astype(jnp.bfloat16)
        n_ref[:, t:t + TILE] = normed
        inv_ref[:, t:t + TILE] = inv
        active = jnp.maximum(normed, 0)
        term = dot(active, w2_ref[t:t + TILE, :])
        z = term if z is None else z + term
        block = (i * STEP + t) // (2 * rows_of_block)
        own = x_ref[:, pl.ds(pl.multiple_of(i * STEP + t, TILE), TILE)].T
        place_rows(order_ref, 0, block, rows_of_block, own, xt_ref)
        place_rows(order_ref, 1, block, rows_of_block, own, xt3_ref)
        place_rows(order_ref, 1, block, rows_of_block, active.T, at3_ref)
    sum_ref[...] += z

    @pl.when(i == pl.num_programs(0) - 1)
    def _():
        z = sum_ref[...]
        z_ref[...] = z
        q = z * lax.rsqrt(jnp.sum(z * z, axis=-1, keepdims=True) + norm_eps)
        q_ref[...] = q.astype(jnp.bfloat16)


def query_forward(order, blocks, x, w, w2):
    rows, d = x.shape
    hid, emb = w2.shape
    half, size = blocks // 2, d // blocks
    turned = jax.ShapeDtypeStruct((2, half, size, rows), jnp.bfloat16)
    out = pl.pallas_call(
        lambda *refs: query_kernel(size, *refs),
        grid_spec=pltpu.PrefetchScalarGridSpec(
            num_scalar_prefetch=1,
            grid=(hid // STEP,),
            in_specs=[
                whole((rows, d)),
                pl.BlockSpec((d, STEP), lambda i, o: (0, i)),
                pl.BlockSpec((STEP, emb), lambda i, o: (i, 0)),
            ],
            out_specs=[
                pl.BlockSpec((rows, STEP), lambda i, o: (0, i)),
                pl.BlockSpec((1, STEP), lambda i, o: (0, i)),
                whole((rows, emb)),
                whole((rows, emb)),
                whole(turned.shape),
                whole(turned.shape),
                whole(turned.shape),
            ],
            scratch_shapes=[pltpu.VMEM((rows, emb), jnp.float32)],
        ),
        out_shape=[
            jax.ShapeDtypeStruct((rows, hid), jnp.bfloat16),
            jax.ShapeDtypeStruct((1, hid), jnp.float32),
            jax.ShapeDtypeStruct((rows, emb), jnp.float32),
            jax.ShapeDtypeStruct((rows, emb), jnp.bfloat16),
            turned,
            turned,
            turned,
        ],
        cost_estimate=pl.CostEstimate(
            flops=2 * rows * hid * (d + emb), bytes_accessed=2 * d * hid, transcendentals=0
        ),
        compiler_params=params(44),
        name="query_forward",
    )(order, x, w, w2)
    return (*out[:4], *(t.reshape(d, rows) for t in out[4:]))


def embed_kernel(all_rows, flat_ref, h_ref, told_ref, w2_ref, zq_ref, neg_ref, dz_ref, z_ref):
    i = pl.program_id(0)
    rows, emb = zq_ref.shape

    @pl.when(i == 0)
    def _():
        z_ref[...] = jnp.zeros_like(z_ref)

    z = None
    for t in range(0, STEP, TILE):
        mu = group_spread(told_ref[:, 0, 2 * t:2 * t + TILE], rows)
        inv = group_spread(told_ref[:, 0, 2 * t + TILE:2 * t + 2 * TILE], rows)
        active = jnp.maximum((h_ref[:, t:t + TILE] - mu) * inv, 0.0).astype(jnp.bfloat16)
        term = dot(active, w2_ref[t:t + TILE, :])
        z = term if z is None else z + term
    z_ref[...] += z

    @pl.when(i == pl.num_programs(0) - 1)
    def _():
        z = z_ref[...]
        z = z * lax.rsqrt(jnp.sum(z * z, axis=-1, keepdims=True) + norm_eps)
        back = jnp.where(
            flat_ref[...] == lax.broadcasted_iota(jnp.int32, (rows, rows), 0), 1.0, 0.0
        ).astype(jnp.bfloat16)
        high = z.astype(jnp.bfloat16)
        rest = z - high.astype(jnp.float32)
        mid = rest.astype(jnp.bfloat16)
        low = (rest - mid.astype(jnp.float32)).astype(jnp.bfloat16)
        positives = dot(back, high) + dot(back, mid) + dot(back, low)
        zq = zq_ref[...]
        inv_len = lax.rsqrt(jnp.sum(zq * zq, axis=-1, keepdims=True) + norm_eps)
        q = zq * inv_len
        scale_coef = loss_scale / all_rows
        pos = jnp.sum(q * positives, axis=-1, keepdims=True) / sharpness_divisor
        exp_pos = jnp.exp(pos) * QUARTER
        total = exp_pos + jnp.sum(neg_ref[:, emb:], axis=-1, keepdims=True)
        d_pos = scale_coef * (exp_pos / total - 1.0)
        weighted = neg_ref[:, :emb] * (scale_coef / total)
        d_q = (d_pos * positives + weighted) / sharpness_divisor
        d_z = (d_q - q * jnp.sum(d_q * q, axis=-1, keepdims=True)) * inv_len
        dz_ref[...] = d_z.astype(jnp.bfloat16)


def embed(flat_row, h, told, w2, zq, negs, all_rows):
    rows, hid = h.shape
    emb = w2.shape[1]
    groups = told.shape[0]
    return pl.pallas_call(
        lambda *refs: embed_kernel(all_rows, *refs),
        grid=(hid // STEP,),
        in_specs=[
            whole((1, rows)),
            pl.BlockSpec((rows, STEP), lambda i: (0, i)),
            pl.BlockSpec((groups, 1, 2 * STEP), lambda i: (0, 0, i)),
            pl.BlockSpec((STEP, emb), lambda i: (i, 0)),
            whole((rows, emb)),
            whole(negs.shape),
        ],
        out_specs=whole((rows, emb)),
        out_shape=jax.ShapeDtypeStruct((rows, emb), jnp.bfloat16),
        scratch_shapes=[pltpu.VMEM((rows, emb), jnp.float32)],
        cost_estimate=pl.CostEstimate(
            flops=2 * rows * hid * emb, bytes_accessed=4 * rows * hid, transcendentals=0
        ),
        compiler_params=params(30),
        name="embed",
    )(flat_row, h, told, w2, zq, negs)


def store_rows(out_ref, at, value, crossed, size):
    if not crossed:
        out_ref[:, at] = value.astype(out_ref.dtype)
        return
    for four in range(0, value.shape[0], 4 * size):
        for i, j in enumerate((0, 2, 1, 3)):
            i, j = four + i * size, four + j * size
            out_ref[i:i + size, at] = value[j:j + size].astype(out_ref.dtype)


def column_tiles(cols, plain):
    for start, end in ((0, plain), (plain, cols)):
        for t in range(start, end, TILE):
            yield slice(t, min(t + TILE, end)), start > 0


def keep_rows(keep_ref, xt_ref, dh_ref, plain, size, at_ref=None, dz_ref=None):
    cols = dh_ref.shape[1]
    for at, crossed in column_tiles(cols, plain):
        store_rows(keep_ref, at, dot(xt_ref[...], dh_ref[:, at]), crossed, size)
    if at_ref is not None:
        store_rows(keep_ref, slice(cols, None), dot(at_ref[...], dz_ref[...]), True, size)


def keep_blocks(keep_ref, xt_ref, dh_ref, plain, size, blocks):
    for at, crossed in column_tiles(dh_ref.shape[1], plain):
        for i, block in enumerate(blocks):
            j = (0, 2, 1, 3)[block] if crossed else block
            keep_ref[i * size:(i + 1) * size, at] = dot(
                xt_ref[j * size:(j + 1) * size, :], dh_ref[:, at]
            )


def send_kernel(sizes, old_plain, has_at, *refs):
    refs = list(refs)
    count = len(sizes)
    dz_ref = refs.pop(0)
    at_ref = refs.pop(0) if has_at else None
    dz = dz_ref[...]
    rows = dz.shape[0]
    if old_plain:
        old_xt_ref, old_ref = refs[:2]
        refs = refs[2:]
    ins, outs = refs[:4 * count], refs[4 * count:]
    if old_plain:
        keep_blocks(outs.pop(0), old_xt_ref, old_ref, old_plain, sizes[0][1], (2, 3))
    for p in range(count):
        xt_ref, w2_ref, n_ref, inv_ref = ins[4 * p:4 * p + 4]
        dh_ref, sent_ref = outs[2 * p:2 * p + 2]
        cols = n_ref.shape[1]
        plain, size = sizes[p]
        for at, crossed in column_tiles(cols, plain):
            normed = n_ref[:, at].astype(jnp.float32)
            d_norm = jnp.where(normed > 0.0, dot_t(dz, w2_ref[at, :]), 0.0)
            mean = jnp.sum(d_norm, axis=0, keepdims=True) / rows
            slope = jnp.sum(d_norm * normed, axis=0, keepdims=True) / rows
            d_hidden = inv_ref[:, at] * (d_norm - mean - normed * slope)
            d_hidden = d_hidden.astype(jnp.bfloat16)
            dh_ref[:, at] = d_hidden
            store_rows(sent_ref, at, dot(xt_ref[...], d_hidden), crossed, size)
        if has_at and p == count - 1:
            store_rows(sent_ref, slice(cols, None), dot(at_ref[...], dz), True, size)


def send_half(dz, at, old, w2, normed, inv, pairs):
    rows, emb = dz.shape
    operands, in_specs, shapes = [dz], [whole(dz.shape)], []
    if at is not None:
        half = at.shape[0] // 2
        operands.append(at)
        in_specs.append(pl.BlockSpec((half, rows), lambda i: (1, 0)))
    if old is not None:
        half = old[0].shape[0] // 2
        operands += old[:2]
        in_specs += [whole((half, rows)), whole(old[1].shape)]
        shapes.append(jax.ShapeDtypeStruct((half // 2, old[1].shape[1]), jnp.float32))
    for p, (xt, place, cols, *_) in enumerate(pairs):
        half = xt.shape[0] // 2
        operands += [xt, w2, normed, inv]
        in_specs += [
            pl.BlockSpec((half, rows), lambda i: (1, 0)),
            pl.BlockSpec((cols, emb), lambda i, place=place: (place, 0)),
            pl.BlockSpec((rows, cols), lambda i, place=place: (0, place)),
            pl.BlockSpec((1, cols), lambda i, place=place: (0, place)),
        ]
        extra = emb if at is not None and p == len(pairs) - 1 else 0
        shapes.append(jax.ShapeDtypeStruct((rows, cols), jnp.bfloat16))
        shapes.append(jax.ShapeDtypeStruct((half, cols + extra), jnp.bfloat16))
    sizes = [pair[3:] for pair in pairs]
    old_plain = 0 if old is None else old[2]
    return pl.pallas_call(
        lambda *refs: send_kernel(sizes, old_plain, at is not None, *refs),
        grid=(1,),
        in_specs=in_specs,
        out_specs=[whole(shape.shape) for shape in shapes],
        out_shape=shapes,
        cost_estimate=pl.CostEstimate(
            flops=2 * rows * half * sum(pair[2] for pair in pairs),
            bytes_accessed=8 * rows * half,
            transcendentals=0,
        ),
        compiler_params=params(36),
        name="send_half",
    )(*operands)


def keep_half(dz, dh, xt, at, plain, size, made, place):
    rows, emb = dz.shape
    cols = dh.shape[1]
    block = pl.BlockSpec((made, rows), lambda i: (place, 0))
    operands = [xt, dh]
    in_specs = [block, whole((rows, cols))]
    if at is None:
        blocks = tuple(range(made // size * place, made // size * (place + 1)))
        kernel = lambda x, d, g: keep_blocks(g, x, d, plain, size, blocks)
        in_specs[0] = whole((4 * size, rows))
    else:
        kernel = lambda x, d, a, z, g: keep_rows(g, x, d, plain, size, a, z)
        operands += [at, dz]
        in_specs += [block, whole((rows, emb))]
        cols += emb
    return pl.pallas_call(
        kernel,
        grid=(1,),
        in_specs=in_specs,
        out_specs=whole((made, cols)),
        out_shape=jax.ShapeDtypeStruct((made, cols), jnp.float32),
        cost_estimate=pl.CostEstimate(
            flops=2 * rows * made * cols, bytes_accessed=8 * rows * made, transcendentals=0
        ),
        compiler_params=params(28),
        name="keep_half",
    )(*operands)


def swap(x, axis, bit):
    size = lax.axis_size(axis)
    return lax.ppermute(x, axis, [(i, i ^ bit) for i in range(size)])


def after(x, *others):
    return lax.optimization_barrier((x,) + others)[0]


def fold_kernel(split, form, counts, *refs):
    both, left, right = counts
    joined = refs[:both]
    sides = (refs[both:both + left], refs[both + left:both + left + right])
    outs = refs[both + left + right:]
    for side, cols in enumerate((slice(0, split), slice(split, refs[0].shape[1]))):
        v = joined[0][:, cols].astype(jnp.float32)
        for ref in joined[1:]:
            v = v + ref[:, cols].astype(jnp.float32)
        for ref in sides[side]:
            v = v + ref[...].astype(jnp.float32)
        if form == "halves":
            half = v.shape[0] // 2
            outs[0][:, cols] = v[:half]
            outs[1][:, cols] = v[half:].astype(jnp.bfloat16)
        elif form == "sides":
            outs[side][...] = v.astype(jnp.bfloat16)
        else:
            outs[0][:, cols] = v.astype(outs[0].dtype)


def fold(keep, keep_place, both, left, right, split, rows, place, form):
    cols = keep.shape[1]

    def spec(width, place=place):
        return pl.BlockSpec((rows, width), lambda i: (place, 0))

    low, full = jnp.bfloat16, jnp.float32
    shapes = {
        "halves": [((rows // 2, cols), full), ((rows // 2, cols), low)],
        "sides": [((rows, split), low), ((rows, cols - split), low)],
        "send": [((rows, cols), low)],
        "own": [((rows, cols), full)],
    }[form]
    in_specs = [spec(cols, keep_place)] + [spec(cols)] * len(both)
    in_specs += [spec(split)] * len(left) + [spec(cols - split)] * len(right)
    return pl.pallas_call(
        lambda *refs: fold_kernel(split, form, (1 + len(both), len(left), len(right)), *refs),
        grid=(1,),
        in_specs=in_specs,
        out_specs=[whole(shape) for shape, _ in shapes],
        out_shape=[jax.ShapeDtypeStruct(*shape) for shape in shapes],
        cost_estimate=SOON,
        compiler_params=params(16),
        name="fold",
    )(keep, *both, *left, *right)


class Pair:
    def __init__(self, keep, came, split):
        self.keep, self.both, self.split = keep, [came], split
        self.left, self.right = [], []

    def hold(self, *others):
        for came in (self.both, self.left, self.right):
            if came:
                came[-1] = after(came[-1], *others)

    def add(self, rows, place, form):
        keep, start = self.keep
        keep_place = (place * rows - start) // rows
        out = fold(
            keep, keep_place, self.both, self.left, self.right, self.split, rows, place, form
        )
        return lax.optimization_barrier(out)

    def cross_first(self, out):
        self.left.append(swap(out[0], "dp", 1))
        self.right.append(swap(out[1], "crop", 2))

    def cross_second(self, out):
        self.left.append(swap(out[0], "crop", 2))
        self.right.append(swap(out[1], "dp", 1))

    def cross_line(self, out, bit):
        self.both.append(swap(out[0], "dp", 2 * bit))

    def cross_third(self, out):
        own, send = out
        return own + swap(send, "dp", 2).astype(jnp.float32)

    def cross_rest(self, own):
        length = lax.axis_size("dp") // 2
        bit = 1
        while 2 * bit < length:
            bit *= 2
            half = own.shape[0] // 2
            own, send = own[:half], own[half:].astype(jnp.bfloat16)
            own = own + swap(send, "dp", 2 * bit).astype(jnp.float32)
        return own


def per_device(
    query_crops, key_crops, shuffle, distractor_bank, query_inner, query_outer, key_inner, key_outer
):
    n_dp, n_crop = lax.axis_size("dp"), lax.axis_size("crop")
    group_count = n_dp * n_crop
    row_count = query_crops.shape[0]
    hid = query_inner.shape[1]
    per_peer = row_count // group_count
    all_rows = float(row_count * group_count)

    wanted = (shuffle % row_count).reshape(group_count, per_peer)
    wanted = jnp.pad(wanted.astype(jnp.float32), ((0, 0), (0, 128 - per_peer)))
    requested = lax.all_to_all(wanted, AXES, split_axis=0, concat_axis=0, tiled=True)
    flat_req = requested[:, :per_peer].astype(jnp.int32).reshape(-1)

    flat_col, flat_row = flat_req[:, None], flat_req[None, :]
    hidden_k, sums = key_hidden(flat_col, key_crops, key_inner, group_count)
    came = lax.all_to_all(sums, AXES, split_axis=0, concat_axis=0, tiled=True)

    length = n_dp // 2
    bits = length.bit_length() - 1
    dp, crop = lax.axis_index("dp"), lax.axis_index("crop")
    block = lax.iota(jnp.int32, group_count // 2)
    z, x, y = block // n_crop, (block // (n_crop // 2)) % 2, block % (n_crop // 2)
    plane = (x ^ (dp % 2)) * (n_crop // 2) + (y ^ (crop // 2))
    line = jnp.zeros_like(block)
    for bit in range(bits):
        line = line * 2 + (((z ^ (dp // 2)) >> bit) & 1)
    order = jnp.stack(
        [plane * length + line, line * n_crop + plane, jnp.full_like(block, crop % 2)]
    )

    normed, inv_q, z_q, q_low, xt, xt3, at3 = query_forward(
        order, group_count, after(query_crops, sums), query_inner, query_outer
    )
    came, q_low, flat_row = lax.optimization_barrier((came, q_low, flat_row))
    told = batch(came, row_count)
    told = lax.all_to_all(told, AXES, split_axis=0, concat_axis=0, tiled=True)

    negs = negatives(q_low, distractor_bank)
    told, negs = lax.optimization_barrier((told, negs))
    d_z = embed(flat_row, hidden_k, told, key_outer, z_q, negs, all_rows)

    def send(last, old, pairs):
        return send_half(d_z, last, old, query_outer, normed, inv_q, pairs)

    large = hid // 16 * 7
    small = hid - 2 * large
    wide = hid // 4
    narrow = large - wide
    half = xt.shape[0] // 2
    size, size_3 = half // 4, half // (4 * length)
    dh_1, sent_1 = send(None, None, [(xt, 0, large, wide, size)])
    came_1 = swap(sent_1, "crop", 1)
    keep_1, dh_2, sent_2, dh_3, sent_3 = send(
        at3,
        (xt, dh_1, wide),
        [
            (xt, 1, large, narrow, size),
            (xt3, 2 * large // small, small, small // 2, size_3),
        ],
    )
    came_2 = swap(sent_2, "crop", 1)
    came_3 = swap(sent_3, "crop", 1)

    def piece(part, rows, place, *others):
        if part == 3:
            dh = after(dh_3, *others)
            keep = keep_half(d_z, dh, xt3, at3, small // 2, size_3, rows, place)
        else:
            dh = after(dh_1 if part == 1 else dh_2, *others)
            plain = wide if part == 1 else narrow
            keep = keep_half(d_z, dh, xt, None, plain, size, rows, place)
        return keep, rows * place

    half_rows, rows = half // 2, half // 4
    one = Pair((keep_1, half_rows), came_1, wide)
    out = one.add(half_rows, 1, "sides")
    one.cross_first(out)
    two = Pair(piece(2, half_rows, 1, *out), came_2, narrow)
    out = two.add(half_rows, 1, "sides")
    two.cross_first(out)
    three = Pair(piece(3, half_rows, 1, *out), came_3, small // 2)
    out = three.add(half_rows, 1, "send")
    three.cross_line(out, 1)
    one.keep = piece(1, rows, 1, *out)
    one.hold(one.keep[0])
    out = one.add(rows, 1, "sides")
    one.cross_second(out)
    two.keep = piece(2, half_rows, 0, *out)
    three.keep = piece(3, half_rows, 0, two.keep[0])
    two.hold(three.keep[0])
    out = two.add(rows, 1, "sides")
    two.cross_second(out)
    line_rows = half_rows
    for bit in range(1, bits):
        line_rows //= 2
        three.hold(*out)
        out = three.add(line_rows, 1, "send")
        three.cross_line(out, 2 ** bit)
    one.keep = piece(1, rows, 0, *out)
    one.hold(one.keep[0])
    c_1 = one.add(rows, 0, "halves")
    two.hold(*c_1)
    c_2 = two.add(rows, 0, "halves")
    own_1 = lax.optimization_barrier(one.cross_third(c_1))
    three.hold(*c_2)
    line_rows //= 2
    out = three.add(line_rows, 1, "sides")
    three.cross_first(out)
    own_2 = lax.optimization_barrier(two.cross_third(c_2))
    three.hold(own_1)
    line_rows //= 2
    out = three.add(line_rows, 1, "sides")
    three.cross_second(out)
    own_1 = one.cross_rest(own_1)
    own_2 = two.cross_rest(own_2)
    own_3 = three.add(line_rows, 0, "own")[0]
    grad_inner = jnp.concatenate([own_1, own_2, own_3[:, :small]], axis=1)
    return (grad_inner, own_3[:, small:])


def solution(mesh):
    placed = (
        P(AXES, None),
        P(AXES, None),
        P(AXES),
        P(),
        P(),
        P(),
        P(),
        P(),
    )
    return jax.shard_map(
        per_device,
        mesh=mesh,
        in_specs=placed,
        out_specs=(P(AXES, None), P(AXES, None)),
        check_vma=False,
    )
```

```python
import math
import jax
import jax.numpy as jnp
from jax import lax
from jax.experimental import pallas as pl
from jax.experimental.pallas import tpu as pltpu
from jax.sharding import PartitionSpec as P

sharpness_divisor = 0.2
loss_scale = 4096.0
bn_eps = 1e-05
norm_eps = 1e-06
AXES = ("dp", "crop")
QUARTER = 0.25


def neg_kernel(q_ref, bank_ref, out_ref):
    rows, emb = q_ref.shape

    @pl.when(pl.program_id(0) == 0)
    def _():
        out_ref[...] = jnp.zeros_like(out_ref)

    q = q_ref[...]
    step = 512
    for j in range(bank_ref.shape[0] // step):
        bank = bank_ref[j * step:(j + 1) * step, :]
        s = lax.dot_general(q, bank, (((1,), (1,)), ((), ())), preferred_element_type=jnp.float32)
        e = jnp.exp2(s * (1.0 / (sharpness_divisor * math.log(2.0))) - 2.0)
        total = e[:, :128]
        for i in range(1, step // 128):
            total = total + e[:, i * 128:(i + 1) * 128]
        out_ref[:, emb:] += total
        out_ref[:, :emb] += jnp.dot(
            e.astype(jnp.bfloat16), bank, preferred_element_type=jnp.float32
        )


def negatives(q, bank):
    rows, emb = q.shape
    tile = 2048
    return pl.pallas_call(
        neg_kernel,
        grid=(bank.shape[0] // tile,),
        in_specs=[
            pl.BlockSpec((rows, emb), lambda i: (0, 0)),
            pl.BlockSpec((tile, emb), lambda i: (i, 0)),
        ],
        out_specs=pl.BlockSpec((rows, emb + 128), lambda i: (0, 0)),
        out_shape=jax.ShapeDtypeStruct((rows, emb + 128), jnp.float32),
        cost_estimate=pl.CostEstimate(
            flops=4 * rows * bank.shape[0] * emb,
            bytes_accessed=bank.shape[0] * emb * 2,
            transcendentals=rows * bank.shape[0],
        ),
        compiler_params=params(20),
        name="negatives",
    )(q, bank)


TILE = 256
STEP = 512
MIB = 1024 * 1024
SOON = pl.CostEstimate(flops=1, bytes_accessed=1, transcendentals=0)


def params(limit=24):
    return pltpu.CompilerParams(
        dimension_semantics=("arbitrary",), vmem_limit_bytes=limit * MIB
    )


def dot(a, b):
    return jnp.dot(a, b, preferred_element_type=jnp.float32)


def dot_t(a, b):
    return lax.dot_general(a, b, (((1,), (1,)), ((), ())), preferred_element_type=jnp.float32)


def whole(shape):
    return pl.BlockSpec(shape, lambda *_: (0,) * len(shape))


def group_rows(groups, per_peer):
    rows = groups * per_peer
    row = lax.broadcasted_iota(jnp.int32, (groups, rows), 1)
    group = lax.broadcasted_iota(jnp.int32, (groups, rows), 0)
    inside = (row >= group * per_peer) & (row < (group + 1) * per_peer)
    return jnp.where(inside, 1.0, 0.0).astype(jnp.float32)


def group_sum(h, groups):
    rows, cols = h.shape
    per_peer = rows // groups
    if per_peer % 8 == 0:
        return jnp.sum(h.reshape(groups, per_peer, cols), axis=1)
    return jnp.dot(
        group_rows(groups, per_peer),
        h,
        precision=lax.Precision.HIGHEST,
        preferred_element_type=jnp.float32,
    )


def group_spread(v, rows):
    groups, cols = v.shape
    per_peer = rows // groups
    if per_peer % 8 == 0:
        return jnp.broadcast_to(v[:, None, :], (groups, per_peer, cols)).reshape(rows, cols)
    return lax.dot_general(
        group_rows(groups, per_peer),
        v,
        (((0,), (0,)), ((), ())),
        precision=lax.Precision.HIGHEST,
        preferred_element_type=jnp.float32,
    )


def key_hidden_kernel(groups, flat_ref, k_ref, w_ref, h_ref, sums_ref, sorted_ref):
    rows = k_ref.shape[0]

    @pl.when(pl.program_id(0) == 0)
    def _():
        cols = lax.broadcasted_iota(jnp.int32, (rows, rows), 1)
        pick = jnp.where(flat_ref[...] == cols, 1.0, 0.0).astype(jnp.bfloat16)
        for i in range(0, k_ref.shape[1], 512):
            sorted_ref[:, i:i + 512] = dot(pick, k_ref[:, i:i + 512]).astype(jnp.bfloat16)

    x = sorted_ref[...]
    for t in range(0, STEP, TILE):
        h = dot(x, w_ref[:, t:t + TILE])
        h_ref[:, t:t + TILE] = h
        sums_ref[:, 0, 2 * t:2 * t + TILE] = group_sum(h, groups)
        sums_ref[:, 0, 2 * t + TILE:2 * t + 2 * TILE] = group_sum(h * h, groups)


def key_hidden(flat_col, k, w, groups):
    rows, d = k.shape
    hid = w.shape[1]
    return pl.pallas_call(
        lambda *refs: key_hidden_kernel(groups, *refs),
        grid=(hid // STEP,),
        in_specs=[
            whole((rows, 1)),
            whole((rows, d)),
            pl.BlockSpec((d, STEP), lambda i: (0, i)),
        ],
        out_specs=[
            pl.BlockSpec((rows, STEP), lambda i: (0, i)),
            pl.BlockSpec((groups, 1, 2 * STEP), lambda i: (0, 0, i)),
        ],
        out_shape=[
            jax.ShapeDtypeStruct((rows, hid), jnp.float32),
            jax.ShapeDtypeStruct((groups, 1, 2 * hid), jnp.float32),
        ],
        scratch_shapes=[pltpu.VMEM((rows, d), jnp.bfloat16)],
        cost_estimate=pl.CostEstimate(
            flops=2 * rows * d * (hid + rows), bytes_accessed=2 * d * hid, transcendentals=0
        ),
        compiler_params=params(44),
        name="key_hidden",
    )(flat_col, k, w)


def batch_kernel(rows, part_ref, told_ref):
    groups, _, size = part_ref.shape
    for t in range(0, size, 2 * TILE):
        total = jnp.sum(part_ref[:, 0, t:t + 2 * TILE], axis=0, keepdims=True) / rows
        mu = total[:, :TILE]
        inv = lax.rsqrt(total[:, TILE:] - mu * mu + bn_eps)
        told = jnp.concatenate([mu, inv], axis=1)
        told_ref[:, 0, t:t + 2 * TILE] = jnp.broadcast_to(told, (groups, 2 * TILE))


def batch(part, rows):
    return pl.pallas_call(
        lambda *refs: batch_kernel(rows, *refs),
        grid=(1,),
        in_specs=[whole(part.shape)],
        out_specs=whole(part.shape),
        out_shape=jax.ShapeDtypeStruct(part.shape, jnp.float32),
        compiler_params=params(),
        name="batch",
    )(part)


def place_rows(order_ref, which, first, rows, t, out_ref):
    for i in range(t.shape[0] // (2 * rows)):
        at = order_ref[which, first + i]
        core = order_ref[2, 0]
        out_ref[core, at] = t[2 * i * rows:(2 * i + 1) * rows]
        out_ref[1 - core, at] = t[(2 * i + 1) * rows:(2 * i + 2) * rows]


def query_kernel(
    rows_of_block, order_ref, x_ref, w_ref, w2_ref,
    n_ref, inv_ref, z_ref, q_ref, xt_ref, xt3_ref, at3_ref, sum_ref,
):
    i = pl.program_id(0)
    rows = x_ref.shape[0]

    @pl.when(i == 0)
    def _():
        sum_ref[...] = jnp.zeros_like(sum_ref)

    x = x_ref[...]
    z = None
    for t in range(0, STEP, TILE):
        h = dot(x, w_ref[:, t:t + TILE])
        mu = jnp.sum(h, axis=0, keepdims=True) / rows
        inv = lax.rsqrt(jnp.sum(h * h, axis=0, keepdims=True) / rows - mu * mu + bn_eps)
        normed = ((h - mu) * inv).astype(jnp.bfloat16)
        n_ref[:, t:t + TILE] = normed
        inv_ref[:, t:t + TILE] = inv
        active = jnp.maximum(normed, 0)
        term = dot(active, w2_ref[t:t + TILE, :])
        z = term if z is None else z + term
        block = (i * STEP + t) // (2 * rows_of_block)
        own = x_ref[:, pl.ds(pl.multiple_of(i * STEP + t, TILE), TILE)].T
        place_rows(order_ref, 0, block, rows_of_block, own, xt_ref)
        place_rows(order_ref, 1, block, rows_of_block, own, xt3_ref)
        place_rows(order_ref, 1, block, rows_of_block, active.T, at3_ref)
    sum_ref[...] += z

    @pl.when(i == pl.num_programs(0) - 1)
    def _():
        z = sum_ref[...]
        z_ref[...] = z
        q = z * lax.rsqrt(jnp.sum(z * z, axis=-1, keepdims=True) + norm_eps)
        q_ref[...] = q.astype(jnp.bfloat16)


def query_forward(order, blocks, x, w, w2):
    rows, d = x.shape
    hid, emb = w2.shape
    half, size = blocks // 2, d // blocks
    turned = jax.ShapeDtypeStruct((2, half, size, rows), jnp.bfloat16)
    out = pl.pallas_call(
        lambda *refs: query_kernel(size, *refs),
        grid_spec=pltpu.PrefetchScalarGridSpec(
            num_scalar_prefetch=1,
            grid=(hid // STEP,),
            in_specs=[
                whole((rows, d)),
                pl.BlockSpec((d, STEP), lambda i, o: (0, i)),
                pl.BlockSpec((STEP, emb), lambda i, o: (i, 0)),
            ],
            out_specs=[
                pl.BlockSpec((rows, STEP), lambda i, o: (0, i)),
                pl.BlockSpec((1, STEP), lambda i, o: (0, i)),
                whole((rows, emb)),
                whole((rows, emb)),
                whole(turned.shape),
                whole(turned.shape),
                whole(turned.shape),
            ],
            scratch_shapes=[pltpu.VMEM((rows, emb), jnp.float32)],
        ),
        out_shape=[
            jax.ShapeDtypeStruct((rows, hid), jnp.bfloat16),
            jax.ShapeDtypeStruct((1, hid), jnp.float32),
            jax.ShapeDtypeStruct((rows, emb), jnp.float32),
            jax.ShapeDtypeStruct((rows, emb), jnp.bfloat16),
            turned,
            turned,
            turned,
        ],
        cost_estimate=pl.CostEstimate(
            flops=2 * rows * hid * (d + emb), bytes_accessed=2 * d * hid, transcendentals=0
        ),
        compiler_params=params(40),
        name="query_forward",
    )(order, x, w, w2)
    return (*out[:4], *(t.reshape(d, rows) for t in out[4:]))


def embed_kernel(all_rows, flat_ref, h_ref, told_ref, w2_ref, zq_ref, neg_ref, dz_ref, z_ref):
    i = pl.program_id(0)
    rows, emb = zq_ref.shape

    @pl.when(i == 0)
    def _():
        z_ref[...] = jnp.zeros_like(z_ref)

    z = None
    for t in range(0, STEP, TILE):
        mu = group_spread(told_ref[:, 0, 2 * t:2 * t + TILE], rows)
        inv = group_spread(told_ref[:, 0, 2 * t + TILE:2 * t + 2 * TILE], rows)
        active = jnp.maximum((h_ref[:, t:t + TILE] - mu) * inv, 0.0).astype(jnp.bfloat16)
        term = dot(active, w2_ref[t:t + TILE, :])
        z = term if z is None else z + term
    z_ref[...] += z

    @pl.when(i == pl.num_programs(0) - 1)
    def _():
        z = z_ref[...]
        z = z * lax.rsqrt(jnp.sum(z * z, axis=-1, keepdims=True) + norm_eps)
        back = jnp.where(
            flat_ref[...] == lax.broadcasted_iota(jnp.int32, (rows, rows), 0), 1.0, 0.0
        ).astype(jnp.bfloat16)
        high = z.astype(jnp.bfloat16)
        rest = z - high.astype(jnp.float32)
        mid = rest.astype(jnp.bfloat16)
        low = (rest - mid.astype(jnp.float32)).astype(jnp.bfloat16)
        positives = dot(back, high) + dot(back, mid) + dot(back, low)
        zq = zq_ref[...]
        inv_len = lax.rsqrt(jnp.sum(zq * zq, axis=-1, keepdims=True) + norm_eps)
        q = zq * inv_len
        scale_coef = loss_scale / all_rows
        pos = jnp.sum(q * positives, axis=-1, keepdims=True) / sharpness_divisor
        exp_pos = jnp.exp(pos) * QUARTER
        total = exp_pos + jnp.sum(neg_ref[:, emb:], axis=-1, keepdims=True)
        d_pos = scale_coef * (exp_pos / total - 1.0)
        weighted = neg_ref[:, :emb] * (scale_coef / total)
        d_q = (d_pos * positives + weighted) / sharpness_divisor
        d_z = (d_q - q * jnp.sum(d_q * q, axis=-1, keepdims=True)) * inv_len
        dz_ref[...] = d_z.astype(jnp.bfloat16)


def embed(flat_row, h, told, w2, zq, negs, all_rows):
    rows, hid = h.shape
    emb = w2.shape[1]
    groups = told.shape[0]
    return pl.pallas_call(
        lambda *refs: embed_kernel(all_rows, *refs),
        grid=(hid // STEP,),
        in_specs=[
            whole((1, rows)),
            pl.BlockSpec((rows, STEP), lambda i: (0, i)),
            pl.BlockSpec((groups, 1, 2 * STEP), lambda i: (0, 0, i)),
            pl.BlockSpec((STEP, emb), lambda i: (i, 0)),
            whole((rows, emb)),
            whole(negs.shape),
        ],
        out_specs=whole((rows, emb)),
        out_shape=jax.ShapeDtypeStruct((rows, emb), jnp.bfloat16),
        scratch_shapes=[pltpu.VMEM((rows, emb), jnp.float32)],
        cost_estimate=pl.CostEstimate(
            flops=2 * rows * hid * emb, bytes_accessed=4 * rows * hid, transcendentals=0
        ),
        compiler_params=params(20),
        name="embed",
    )(flat_row, h, told, w2, zq, negs)


def store_rows(out_ref, at, value, crossed, size):
    if not crossed:
        out_ref[:, at] = value.astype(out_ref.dtype)
        return
    for four in range(0, value.shape[0], 4 * size):
        for i, j in enumerate((0, 2, 1, 3)):
            i, j = four + i * size, four + j * size
            out_ref[i:i + size, at] = value[j:j + size].astype(out_ref.dtype)


def column_tiles(cols, plain):
    for start, end in ((0, plain), (plain, cols)):
        for t in range(start, end, TILE):
            yield slice(t, min(t + TILE, end)), start > 0


def keep_rows(keep_ref, xt_ref, dh_ref, plain, size, at_ref=None, dz_ref=None):
    cols = dh_ref.shape[1]
    for at, crossed in column_tiles(cols, plain):
        store_rows(keep_ref, at, dot(xt_ref[...], dh_ref[:, at]), crossed, size)
    if at_ref is not None:
        store_rows(keep_ref, slice(cols, None), dot(at_ref[...], dz_ref[...]), True, size)


def keep_blocks(keep_ref, xt_ref, dh_ref, plain, size, blocks):
    for at, crossed in column_tiles(dh_ref.shape[1], plain):
        for i, block in enumerate(blocks):
            j = (0, 2, 1, 3)[block] if crossed else block
            keep_ref[i * size:(i + 1) * size, at] = dot(
                xt_ref[j * size:(j + 1) * size, :], dh_ref[:, at]
            )


def send_kernel(sizes, old_plain, has_at, *refs):
    refs = list(refs)
    count = len(sizes)
    dz_ref = refs.pop(0)
    at_ref = refs.pop(0) if has_at else None
    dz = dz_ref[...]
    rows = dz.shape[0]
    if old_plain:
        old_xt_ref, old_ref = refs[:2]
        refs = refs[2:]
    ins, outs = refs[:4 * count], refs[4 * count:]
    if old_plain:
        keep_blocks(outs.pop(0), old_xt_ref, old_ref, old_plain, sizes[0][1], (2, 3))
    for p in range(count):
        xt_ref, w2_ref, n_ref, inv_ref = ins[4 * p:4 * p + 4]
        dh_ref, sent_ref = outs[2 * p:2 * p + 2]
        cols = n_ref.shape[1]
        plain, size = sizes[p]
        for at, crossed in column_tiles(cols, plain):
            normed = n_ref[:, at].astype(jnp.float32)
            d_norm = jnp.where(normed > 0.0, dot_t(dz, w2_ref[at, :]), 0.0)
            mean = jnp.sum(d_norm, axis=0, keepdims=True) / rows
            slope = jnp.sum(d_norm * normed, axis=0, keepdims=True) / rows
            d_hidden = inv_ref[:, at] * (d_norm - mean - normed * slope)
            d_hidden = d_hidden.astype(jnp.bfloat16)
            dh_ref[:, at] = d_hidden
            store_rows(sent_ref, at, dot(xt_ref[...], d_hidden), crossed, size)
        if has_at and p == count - 1:
            store_rows(sent_ref, slice(cols, None), dot(at_ref[...], dz), True, size)


def send_half(dz, at, old, w2, normed, inv, pairs):
    rows, emb = dz.shape
    operands, in_specs, shapes = [dz], [whole(dz.shape)], []
    if at is not None:
        half = at.shape[0] // 2
        operands.append(at)
        in_specs.append(pl.BlockSpec((half, rows), lambda i: (1, 0)))
    if old is not None:
        half = old[0].shape[0] // 2
        operands += old[:2]
        in_specs += [whole((half, rows)), whole(old[1].shape)]
        shapes.append(jax.ShapeDtypeStruct((half // 2, old[1].shape[1]), jnp.float32))
    for p, (xt, place, cols, *_) in enumerate(pairs):
        half = xt.shape[0] // 2
        operands += [xt, w2, normed, inv]
        in_specs += [
            pl.BlockSpec((half, rows), lambda i: (1, 0)),
            pl.BlockSpec((cols, emb), lambda i, place=place: (place, 0)),
            pl.BlockSpec((rows, cols), lambda i, place=place: (0, place)),
            pl.BlockSpec((1, cols), lambda i, place=place: (0, place)),
        ]
        extra = emb if at is not None and p == len(pairs) - 1 else 0
        shapes.append(jax.ShapeDtypeStruct((rows, cols), jnp.bfloat16))
        shapes.append(jax.ShapeDtypeStruct((half, cols + extra), jnp.bfloat16))
    sizes = [pair[3:] for pair in pairs]
    old_plain = 0 if old is None else old[2]
    return pl.pallas_call(
        lambda *refs: send_kernel(sizes, old_plain, at is not None, *refs),
        grid=(1,),
        in_specs=in_specs,
        out_specs=[whole(shape.shape) for shape in shapes],
        out_shape=shapes,
        cost_estimate=pl.CostEstimate(
            flops=2 * rows * half * sum(pair[2] for pair in pairs),
            bytes_accessed=8 * rows * half,
            transcendentals=0,
        ),
        compiler_params=params(36),
        name="send_half",
    )(*operands)


def keep_half(dz, dh, xt, at, plain, size, made, place):
    rows, emb = dz.shape
    cols = dh.shape[1]
    block = pl.BlockSpec((made, rows), lambda i: (place, 0))
    operands = [xt, dh]
    in_specs = [block, whole((rows, cols))]
    if at is None:
        blocks = tuple(range(made // size * place, made // size * (place + 1)))
        kernel = lambda x, d, g: keep_blocks(g, x, d, plain, size, blocks)
        in_specs[0] = whole((4 * size, rows))
    else:
        kernel = lambda x, d, a, z, g: keep_rows(g, x, d, plain, size, a, z)
        operands += [at, dz]
        in_specs += [block, whole((rows, emb))]
        cols += emb
    return pl.pallas_call(
        kernel,
        grid=(1,),
        in_specs=in_specs,
        out_specs=whole((made, cols)),
        out_shape=jax.ShapeDtypeStruct((made, cols), jnp.float32),
        cost_estimate=pl.CostEstimate(
            flops=2 * rows * made * cols, bytes_accessed=8 * rows * made, transcendentals=0
        ),
        compiler_params=params(28),
        name="keep_half",
    )(*operands)


def swap(x, axis, bit):
    size = lax.axis_size(axis)
    return lax.ppermute(x, axis, [(i, i ^ bit) for i in range(size)])


def after(x, *others):
    return lax.optimization_barrier((x,) + others)[0]


def fold_kernel(split, form, counts, *refs):
    both, left, right = counts
    joined = refs[:both]
    sides = (refs[both:both + left], refs[both + left:both + left + right])
    outs = refs[both + left + right:]
    for side, cols in enumerate((slice(0, split), slice(split, refs[0].shape[1]))):
        v = joined[0][:, cols].astype(jnp.float32)
        for ref in joined[1:]:
            v = v + ref[:, cols].astype(jnp.float32)
        for ref in sides[side]:
            v = v + ref[...].astype(jnp.float32)
        if form == "halves":
            half = v.shape[0] // 2
            outs[0][:, cols] = v[:half]
            outs[1][:, cols] = v[half:].astype(jnp.bfloat16)
        elif form == "sides":
            outs[side][...] = v.astype(jnp.bfloat16)
        else:
            outs[0][:, cols] = v.astype(outs[0].dtype)


def fold(keep, keep_place, both, left, right, split, rows, place, form):
    cols = keep.shape[1]

    def spec(width, place=place):
        return pl.BlockSpec((rows, width), lambda i: (place, 0))

    low, full = jnp.bfloat16, jnp.float32
    shapes = {
        "halves": [((rows // 2, cols), full), ((rows // 2, cols), low)],
        "sides": [((rows, split), low), ((rows, cols - split), low)],
        "send": [((rows, cols), low)],
        "own": [((rows, cols), full)],
    }[form]
    in_specs = [spec(cols, keep_place)] + [spec(cols)] * len(both)
    in_specs += [spec(split)] * len(left) + [spec(cols - split)] * len(right)
    return pl.pallas_call(
        lambda *refs: fold_kernel(split, form, (1 + len(both), len(left), len(right)), *refs),
        grid=(1,),
        in_specs=in_specs,
        out_specs=[whole(shape) for shape, _ in shapes],
        out_shape=[jax.ShapeDtypeStruct(*shape) for shape in shapes],
        cost_estimate=SOON,
        compiler_params=params(16),
        name="fold",
    )(keep, *both, *left, *right)


class Pair:
    def __init__(self, keep, came, split):
        self.keep, self.both, self.split = keep, [came], split
        self.left, self.right = [], []

    def hold(self, *others):
        for came in (self.both, self.left, self.right):
            if came:
                came[-1] = after(came[-1], *others)

    def add(self, rows, place, form):
        keep, start = self.keep
        keep_place = (place * rows - start) // rows
        out = fold(
            keep, keep_place, self.both, self.left, self.right, self.split, rows, place, form
        )
        return lax.optimization_barrier(out)

    def cross_first(self, out):
        self.left.append(swap(out[0], "dp", 1))
        self.right.append(swap(out[1], "crop", 2))

    def cross_second(self, out):
        self.left.append(swap(out[0], "crop", 2))
        self.right.append(swap(out[1], "dp", 1))

    def cross_line(self, out, bit):
        self.both.append(swap(out[0], "dp", 2 * bit))

    def cross_third(self, out):
        own, send = out
        return own + swap(send, "dp", 2).astype(jnp.float32)

    def cross_rest(self, own):
        length = lax.axis_size("dp") // 2
        bit = 1
        while 2 * bit < length:
            bit *= 2
            half = own.shape[0] // 2
            own, send = own[:half], own[half:].astype(jnp.bfloat16)
            own = own + swap(send, "dp", 2 * bit).astype(jnp.float32)
        return own


def per_device(
    query_crops, key_crops, shuffle, distractor_bank, query_inner, query_outer, key_inner, key_outer
):
    n_dp, n_crop = lax.axis_size("dp"), lax.axis_size("crop")
    group_count = n_dp * n_crop
    row_count = query_crops.shape[0]
    hid = query_inner.shape[1]
    per_peer = row_count // group_count
    all_rows = float(row_count * group_count)

    wanted = (shuffle % row_count).reshape(group_count, per_peer)
    wanted = jnp.pad(wanted.astype(jnp.float32), ((0, 0), (0, 128 - per_peer)))
    requested = lax.all_to_all(wanted, AXES, split_axis=0, concat_axis=0, tiled=True)
    flat_req = requested[:, :per_peer].astype(jnp.int32).reshape(-1)

    flat_col, flat_row = flat_req[:, None], flat_req[None, :]
    hidden_k, sums = key_hidden(flat_col, key_crops, key_inner, group_count)
    came = lax.all_to_all(sums, AXES, split_axis=0, concat_axis=0, tiled=True)

    length = n_dp // 2
    bits = length.bit_length() - 1
    dp, crop = lax.axis_index("dp"), lax.axis_index("crop")
    block = lax.iota(jnp.int32, group_count // 2)
    z, x, y = block // n_crop, (block // (n_crop // 2)) % 2, block % (n_crop // 2)
    plane = (x ^ (dp % 2)) * (n_crop // 2) + (y ^ (crop // 2))
    line = jnp.zeros_like(block)
    for bit in range(bits):
        line = line * 2 + (((z ^ (dp // 2)) >> bit) & 1)
    order = jnp.stack(
        [plane * length + line, line * n_crop + plane, jnp.full_like(block, crop % 2)]
    )

    normed, inv_q, z_q, q_low, xt, xt3, at3 = query_forward(
        order, group_count, after(query_crops, sums), query_inner, query_outer
    )
    came, q_low, flat_row = lax.optimization_barrier((came, q_low, flat_row))
    told = batch(came, row_count)
    told = lax.all_to_all(told, AXES, split_axis=0, concat_axis=0, tiled=True)

    negs = negatives(q_low, distractor_bank)
    told, negs = lax.optimization_barrier((told, negs))
    d_z = embed(flat_row, hidden_k, told, key_outer, z_q, negs, all_rows)

    def send(last, old, pairs):
        return send_half(d_z, last, old, query_outer, normed, inv_q, pairs)

    large = hid // 16 * 7
    small = hid - 2 * large
    wide = hid // 4
    narrow = large - wide
    half = xt.shape[0] // 2
    size, size_3 = half // 4, half // (4 * length)
    dh_1, sent_1 = send(None, None, [(xt, 0, large, wide, size)])
    came_1 = swap(sent_1, "crop", 1)
    keep_1, dh_2, sent_2, dh_3, sent_3 = send(
        at3,
        (xt, dh_1, wide),
        [
            (xt, 1, large, narrow, size),
            (xt3, 2 * large // small, small, small // 2, size_3),
        ],
    )
    came_2 = swap(sent_2, "crop", 1)
    came_3 = swap(sent_3, "crop", 1)

    def piece(part, rows, place, *others):
        if part == 3:
            dh = after(dh_3, *others)
            keep = keep_half(d_z, dh, xt3, at3, small // 2, size_3, rows, place)
        else:
            dh = after(dh_1 if part == 1 else dh_2, *others)
            plain = wide if part == 1 else narrow
            keep = keep_half(d_z, dh, xt, None, plain, size, rows, place)
        return keep, rows * place

    half_rows, rows = half // 2, half // 4
    one = Pair((keep_1, half_rows), came_1, wide)
    out = one.add(half_rows, 1, "sides")
    one.cross_first(out)
    two = Pair(piece(2, half_rows, 1, *out), came_2, narrow)
    out = two.add(half_rows, 1, "sides")
    two.cross_first(out)
    three = Pair(piece(3, half_rows, 1, *out), came_3, small // 2)
    out = three.add(half_rows, 1, "send")
    three.cross_line(out, 1)
    one.keep = piece(1, rows, 1, *out)
    three.keep = piece(3, half_rows, 0, one.keep[0])
    one.hold(three.keep[0])
    out = one.add(rows, 1, "sides")
    one.cross_second(out)
    line_rows = half_rows
    for bit in range(1, bits):
        line_rows //= 2
        three.hold(*out)
        out = three.add(line_rows, 1, "send")
        three.cross_line(out, 2 ** bit)
    two.keep = piece(2, half_rows, 0, *out)
    one.keep = piece(1, rows, 0, two.keep[0])
    two.hold(two.keep[0], one.keep[0])
    out = two.add(rows, 1, "sides")
    two.cross_second(out)
    three.hold(*out)
    line_rows //= 2
    out = three.add(line_rows, 1, "sides")
    three.cross_first(out)
    one.hold(*out)
    c_1 = one.add(rows, 0, "halves")
    two.hold(*c_1)
    c_2 = two.add(rows, 0, "halves")
    own_1 = lax.optimization_barrier(one.cross_third(c_1))
    own_2 = lax.optimization_barrier(two.cross_third(c_2))
    three.hold(own_1, own_2)
    line_rows //= 2
    out = three.add(line_rows, 1, "sides")
    three.cross_second(out)
    own_1 = one.cross_rest(own_1)
    own_2 = two.cross_rest(own_2)
    own_3 = three.add(line_rows, 0, "own")[0]
    grad_inner = jnp.concatenate([own_1, own_2, own_3[:, :small]], axis=1)
    return (grad_inner, own_3[:, small:])


def solution(mesh):
    placed = (
        P(AXES, None),
        P(AXES, None),
        P(AXES),
        P(),
        P(),
        P(),
        P(),
        P(),
    )
    return jax.shard_map(
        per_device,
        mesh=mesh,
        in_specs=placed,
        out_specs=(P(AXES, None), P(AXES, None)),
        check_vma=False,
    )
```

```python
import math
import jax
import jax.numpy as jnp
from jax import lax
from jax.experimental import pallas as pl
from jax.experimental.pallas import tpu as pltpu
from jax.sharding import PartitionSpec as P

sharpness_divisor = 0.2
loss_scale = 4096.0
bn_eps = 1e-05
norm_eps = 1e-06
AXES = ("dp", "crop")
QUARTER = 0.25


def neg_kernel(q_ref, bank_ref, out_ref):
    rows, emb = q_ref.shape

    @pl.when(pl.program_id(0) == 0)
    def _():
        out_ref[...] = jnp.zeros_like(out_ref)

    q = q_ref[...]
    step = 512
    for j in range(bank_ref.shape[0] // step):
        bank = bank_ref[j * step:(j + 1) * step, :]
        s = lax.dot_general(q, bank, (((1,), (1,)), ((), ())), preferred_element_type=jnp.float32)
        e = jnp.exp2(s * (1.0 / (sharpness_divisor * math.log(2.0))) - 2.0)
        total = e[:, :128]
        for i in range(1, step // 128):
            total = total + e[:, i * 128:(i + 1) * 128]
        out_ref[:, emb:] += total
        out_ref[:, :emb] += jnp.dot(
            e.astype(jnp.bfloat16), bank, preferred_element_type=jnp.float32
        )


def negatives(q, bank):
    rows, emb = q.shape
    tile = 2048
    return pl.pallas_call(
        neg_kernel,
        grid=(bank.shape[0] // tile,),
        in_specs=[
            pl.BlockSpec((rows, emb), lambda i: (0, 0)),
            pl.BlockSpec((tile, emb), lambda i: (i, 0)),
        ],
        out_specs=pl.BlockSpec((rows, emb + 128), lambda i: (0, 0)),
        out_shape=jax.ShapeDtypeStruct((rows, emb + 128), jnp.float32),
        cost_estimate=pl.CostEstimate(
            flops=4 * rows * bank.shape[0] * emb,
            bytes_accessed=bank.shape[0] * emb * 2,
            transcendentals=rows * bank.shape[0],
        ),
        compiler_params=params(44),
        name="negatives",
    )(q, bank)


TILE = 256
STEP = 512
MIB = 1024 * 1024
SOON = pl.CostEstimate(flops=1, bytes_accessed=1, transcendentals=0)


def params(limit=24):
    return pltpu.CompilerParams(
        dimension_semantics=("arbitrary",), vmem_limit_bytes=limit * MIB
    )


def dot(a, b):
    return jnp.dot(a, b, preferred_element_type=jnp.float32)


def dot_t(a, b):
    return lax.dot_general(a, b, (((1,), (1,)), ((), ())), preferred_element_type=jnp.float32)


def whole(shape):
    return pl.BlockSpec(shape, lambda *_: (0,) * len(shape))


def group_rows(groups, per_peer):
    rows = groups * per_peer
    row = lax.broadcasted_iota(jnp.int32, (groups, rows), 1)
    group = lax.broadcasted_iota(jnp.int32, (groups, rows), 0)
    inside = (row >= group * per_peer) & (row < (group + 1) * per_peer)
    return jnp.where(inside, 1.0, 0.0).astype(jnp.float32)


def group_sum(h, groups):
    rows, cols = h.shape
    per_peer = rows // groups
    if per_peer % 8 == 0:
        return jnp.sum(h.reshape(groups, per_peer, cols), axis=1)
    return jnp.dot(
        group_rows(groups, per_peer),
        h,
        precision=lax.Precision.HIGHEST,
        preferred_element_type=jnp.float32,
    )


def group_spread(v, rows):
    groups, cols = v.shape
    per_peer = rows // groups
    if per_peer % 8 == 0:
        return jnp.broadcast_to(v[:, None, :], (groups, per_peer, cols)).reshape(rows, cols)
    return lax.dot_general(
        group_rows(groups, per_peer),
        v,
        (((0,), (0,)), ((), ())),
        precision=lax.Precision.HIGHEST,
        preferred_element_type=jnp.float32,
    )


def key_hidden_kernel(groups, flat_ref, k_ref, w_ref, h_ref, sums_ref, sorted_ref):
    rows = k_ref.shape[0]

    @pl.when(pl.program_id(0) == 0)
    def _():
        cols = lax.broadcasted_iota(jnp.int32, (rows, rows), 1)
        pick = jnp.where(flat_ref[...] == cols, 1.0, 0.0).astype(jnp.bfloat16)
        for i in range(0, k_ref.shape[1], 512):
            sorted_ref[:, i:i + 512] = dot(pick, k_ref[:, i:i + 512]).astype(jnp.bfloat16)

    x = sorted_ref[...]
    for t in range(0, STEP, TILE):
        h = dot(x, w_ref[:, t:t + TILE])
        h_ref[:, t:t + TILE] = h
        sums_ref[:, 0, 2 * t:2 * t + TILE] = group_sum(h, groups)
        sums_ref[:, 0, 2 * t + TILE:2 * t + 2 * TILE] = group_sum(h * h, groups)


def key_hidden(flat_col, k, w, groups):
    rows, d = k.shape
    hid = w.shape[1]
    return pl.pallas_call(
        lambda *refs: key_hidden_kernel(groups, *refs),
        grid=(hid // STEP,),
        in_specs=[
            whole((rows, 1)),
            whole((rows, d)),
            pl.BlockSpec((d, STEP), lambda i: (0, i)),
        ],
        out_specs=[
            pl.BlockSpec((rows, STEP), lambda i: (0, i)),
            pl.BlockSpec((groups, 1, 2 * STEP), lambda i: (0, 0, i)),
        ],
        out_shape=[
            jax.ShapeDtypeStruct((rows, hid), jnp.float32),
            jax.ShapeDtypeStruct((groups, 1, 2 * hid), jnp.float32),
        ],
        scratch_shapes=[pltpu.VMEM((rows, d), jnp.bfloat16)],
        cost_estimate=pl.CostEstimate(
            flops=2 * rows * d * (hid + rows), bytes_accessed=2 * d * hid, transcendentals=0
        ),
        compiler_params=params(50),
        name="key_hidden",
    )(flat_col, k, w)


def batch_kernel(rows, part_ref, told_ref):
    groups, _, size = part_ref.shape
    for t in range(0, size, 2 * TILE):
        total = jnp.sum(part_ref[:, 0, t:t + 2 * TILE], axis=0, keepdims=True) / rows
        mu = total[:, :TILE]
        inv = lax.rsqrt(total[:, TILE:] - mu * mu + bn_eps)
        told = jnp.concatenate([mu, inv], axis=1)
        told_ref[:, 0, t:t + 2 * TILE] = jnp.broadcast_to(told, (groups, 2 * TILE))


def batch(part, rows):
    return pl.pallas_call(
        lambda *refs: batch_kernel(rows, *refs),
        grid=(1,),
        in_specs=[whole(part.shape)],
        out_specs=whole(part.shape),
        out_shape=jax.ShapeDtypeStruct(part.shape, jnp.float32),
        compiler_params=params(),
        name="batch",
    )(part)


def place_rows(order_ref, which, first, rows, t, out_ref):
    for i in range(t.shape[0] // (2 * rows)):
        at = order_ref[which, first + i]
        core = order_ref[2, 0]
        out_ref[core, at] = t[2 * i * rows:(2 * i + 1) * rows]
        out_ref[1 - core, at] = t[(2 * i + 1) * rows:(2 * i + 2) * rows]


def query_kernel(
    rows_of_block, order_ref, x_ref, w_ref, w2_ref,
    n_ref, inv_ref, z_ref, q_ref, xt_ref, xt3_ref, at3_ref, sum_ref,
):
    i = pl.program_id(0)
    rows = x_ref.shape[0]

    @pl.when(i == 0)
    def _():
        sum_ref[...] = jnp.zeros_like(sum_ref)

    x = x_ref[...]
    z = None
    for t in range(0, STEP, TILE):
        h = dot(x, w_ref[:, t:t + TILE])
        mu = jnp.sum(h, axis=0, keepdims=True) / rows
        inv = lax.rsqrt(jnp.sum(h * h, axis=0, keepdims=True) / rows - mu * mu + bn_eps)
        normed = ((h - mu) * inv).astype(jnp.bfloat16)
        n_ref[:, t:t + TILE] = normed
        inv_ref[:, t:t + TILE] = inv
        active = jnp.maximum(normed, 0)
        term = dot(active, w2_ref[t:t + TILE, :])
        z = term if z is None else z + term
        block = (i * STEP + t) // (2 * rows_of_block)
        own = x_ref[:, pl.ds(pl.multiple_of(i * STEP + t, TILE), TILE)].T
        place_rows(order_ref, 0, block, rows_of_block, own, xt_ref)
        place_rows(order_ref, 1, block, rows_of_block, own, xt3_ref)
        place_rows(order_ref, 1, block, rows_of_block, active.T, at3_ref)
    sum_ref[...] += z

    @pl.when(i == pl.num_programs(0) - 1)
    def _():
        z = sum_ref[...]
        z_ref[...] = z
        q = z * lax.rsqrt(jnp.sum(z * z, axis=-1, keepdims=True) + norm_eps)
        q_ref[...] = q.astype(jnp.bfloat16)


def query_forward(order, blocks, x, w, w2):
    rows, d = x.shape
    hid, emb = w2.shape
    half, size = blocks // 2, d // blocks
    turned = jax.ShapeDtypeStruct((2, half, size, rows), jnp.bfloat16)
    out = pl.pallas_call(
        lambda *refs: query_kernel(size, *refs),
        grid_spec=pltpu.PrefetchScalarGridSpec(
            num_scalar_prefetch=1,
            grid=(hid // STEP,),
            in_specs=[
                whole((rows, d)),
                pl.BlockSpec((d, STEP), lambda i, o: (0, i)),
                pl.BlockSpec((STEP, emb), lambda i, o: (i, 0)),
            ],
            out_specs=[
                pl.BlockSpec((rows, STEP), lambda i, o: (0, i)),
                pl.BlockSpec((1, STEP), lambda i, o: (0, i)),
                whole((rows, emb)),
                whole((rows, emb)),
                whole(turned.shape),
                whole(turned.shape),
                whole(turned.shape),
            ],
            scratch_shapes=[pltpu.VMEM((rows, emb), jnp.float32)],
        ),
        out_shape=[
            jax.ShapeDtypeStruct((rows, hid), jnp.bfloat16),
            jax.ShapeDtypeStruct((1, hid), jnp.float32),
            jax.ShapeDtypeStruct((rows, emb), jnp.float32),
            jax.ShapeDtypeStruct((rows, emb), jnp.bfloat16),
            turned,
            turned,
            turned,
        ],
        cost_estimate=pl.CostEstimate(
            flops=2 * rows * hid * (d + emb), bytes_accessed=2 * d * hid, transcendentals=0
        ),
        compiler_params=params(44),
        name="query_forward",
    )(order, x, w, w2)
    return (*out[:4], *(t.reshape(d, rows) for t in out[4:]))


def embed_kernel(all_rows, flat_ref, h_ref, told_ref, w2_ref, zq_ref, neg_ref, dz_ref, z_ref):
    i = pl.program_id(0)
    rows, emb = zq_ref.shape

    @pl.when(i == 0)
    def _():
        z_ref[...] = jnp.zeros_like(z_ref)

    z = None
    for t in range(0, STEP, TILE):
        mu = group_spread(told_ref[:, 0, 2 * t:2 * t + TILE], rows)
        inv = group_spread(told_ref[:, 0, 2 * t + TILE:2 * t + 2 * TILE], rows)
        active = jnp.maximum((h_ref[:, t:t + TILE] - mu) * inv, 0.0).astype(jnp.bfloat16)
        term = dot(active, w2_ref[t:t + TILE, :])
        z = term if z is None else z + term
    z_ref[...] += z

    @pl.when(i == pl.num_programs(0) - 1)
    def _():
        z = z_ref[...]
        z = z * lax.rsqrt(jnp.sum(z * z, axis=-1, keepdims=True) + norm_eps)
        back = jnp.where(
            flat_ref[...] == lax.broadcasted_iota(jnp.int32, (rows, rows), 0), 1.0, 0.0
        ).astype(jnp.bfloat16)
        high = z.astype(jnp.bfloat16)
        rest = z - high.astype(jnp.float32)
        mid = rest.astype(jnp.bfloat16)
        low = (rest - mid.astype(jnp.float32)).astype(jnp.bfloat16)
        positives = dot(back, high) + dot(back, mid) + dot(back, low)
        zq = zq_ref[...]
        inv_len = lax.rsqrt(jnp.sum(zq * zq, axis=-1, keepdims=True) + norm_eps)
        q = zq * inv_len
        scale_coef = loss_scale / all_rows
        pos = jnp.sum(q * positives, axis=-1, keepdims=True) / sharpness_divisor
        exp_pos = jnp.exp(pos) * QUARTER
        total = exp_pos + jnp.sum(neg_ref[:, emb:], axis=-1, keepdims=True)
        d_pos = scale_coef * (exp_pos / total - 1.0)
        weighted = neg_ref[:, :emb] * (scale_coef / total)
        d_q = (d_pos * positives + weighted) / sharpness_divisor
        d_z = (d_q - q * jnp.sum(d_q * q, axis=-1, keepdims=True)) * inv_len
        dz_ref[...] = d_z.astype(jnp.bfloat16)


def embed(flat_row, h, told, w2, zq, negs, all_rows):
    rows, hid = h.shape
    emb = w2.shape[1]
    groups = told.shape[0]
    return pl.pallas_call(
        lambda *refs: embed_kernel(all_rows, *refs),
        grid=(hid // STEP,),
        in_specs=[
            whole((1, rows)),
            pl.BlockSpec((rows, STEP), lambda i: (0, i)),
            pl.BlockSpec((groups, 1, 2 * STEP), lambda i: (0, 0, i)),
            pl.BlockSpec((STEP, emb), lambda i: (i, 0)),
            whole((rows, emb)),
            whole(negs.shape),
        ],
        out_specs=whole((rows, emb)),
        out_shape=jax.ShapeDtypeStruct((rows, emb), jnp.bfloat16),
        scratch_shapes=[pltpu.VMEM((rows, emb), jnp.float32)],
        cost_estimate=pl.CostEstimate(
            flops=2 * rows * hid * emb, bytes_accessed=4 * rows * hid, transcendentals=0
        ),
        compiler_params=params(30),
        name="embed",
    )(flat_row, h, told, w2, zq, negs)


def store_rows(out_ref, at, value, crossed, size):
    if not crossed:
        out_ref[:, at] = value.astype(out_ref.dtype)
        return
    for four in range(0, value.shape[0], 4 * size):
        for i, j in enumerate((0, 2, 1, 3)):
            i, j = four + i * size, four + j * size
            out_ref[i:i + size, at] = value[j:j + size].astype(out_ref.dtype)


def column_tiles(cols, plain):
    for start, end in ((0, plain), (plain, cols)):
        for t in range(start, end, TILE):
            yield slice(t, min(t + TILE, end)), start > 0


def keep_rows(keep_ref, xt_ref, dh_ref, plain, size, at_ref=None, dz_ref=None):
    cols = dh_ref.shape[1]
    for at, crossed in column_tiles(cols, plain):
        store_rows(keep_ref, at, dot(xt_ref[...], dh_ref[:, at]), crossed, size)
    if at_ref is not None:
        store_rows(keep_ref, slice(cols, None), dot(at_ref[...], dz_ref[...]), True, size)


def keep_blocks(keep_ref, xt_ref, dh_ref, plain, size, blocks):
    for at, crossed in column_tiles(dh_ref.shape[1], plain):
        for i, block in enumerate(blocks):
            j = (0, 2, 1, 3)[block] if crossed else block
            keep_ref[i * size:(i + 1) * size, at] = dot(
                xt_ref[j * size:(j + 1) * size, :], dh_ref[:, at]
            )


def send_kernel(sizes, old_plain, has_at, *refs):
    refs = list(refs)
    count = len(sizes)
    dz_ref = refs.pop(0)
    at_ref = refs.pop(0) if has_at else None
    dz = dz_ref[...]
    rows = dz.shape[0]
    if old_plain:
        old_xt_ref, old_ref = refs[:2]
        refs = refs[2:]
    ins, outs = refs[:4 * count], refs[4 * count:]
    if old_plain:
        keep_blocks(outs.pop(0), old_xt_ref, old_ref, old_plain, sizes[0][1], (2, 3))
    for p in range(count):
        xt_ref, w2_ref, n_ref, inv_ref = ins[4 * p:4 * p + 4]
        dh_ref, sent_ref = outs[2 * p:2 * p + 2]
        cols = n_ref.shape[1]
        plain, size = sizes[p]
        for at, crossed in column_tiles(cols, plain):
            normed = n_ref[:, at].astype(jnp.float32)
            d_norm = jnp.where(normed > 0.0, dot_t(dz, w2_ref[at, :]), 0.0)
            mean = jnp.sum(d_norm, axis=0, keepdims=True) / rows
            slope = jnp.sum(d_norm * normed, axis=0, keepdims=True) / rows
            d_hidden = inv_ref[:, at] * (d_norm - mean - normed * slope)
            d_hidden = d_hidden.astype(jnp.bfloat16)
            dh_ref[:, at] = d_hidden
            store_rows(sent_ref, at, dot(xt_ref[...], d_hidden), crossed, size)
        if has_at and p == count - 1:
            store_rows(sent_ref, slice(cols, None), dot(at_ref[...], dz), True, size)


def send_half(dz, at, old, w2, normed, inv, pairs):
    rows, emb = dz.shape
    operands, in_specs, shapes = [dz], [whole(dz.shape)], []
    if at is not None:
        half = at.shape[0] // 2
        operands.append(at)
        in_specs.append(pl.BlockSpec((half, rows), lambda i: (1, 0)))
    if old is not None:
        half = old[0].shape[0] // 2
        operands += old[:2]
        in_specs += [whole((half, rows)), whole(old[1].shape)]
        shapes.append(jax.ShapeDtypeStruct((half // 2, old[1].shape[1]), jnp.float32))
    for p, (xt, place, cols, *_) in enumerate(pairs):
        half = xt.shape[0] // 2
        operands += [xt, w2, normed, inv]
        in_specs += [
            pl.BlockSpec((half, rows), lambda i: (1, 0)),
            pl.BlockSpec((cols, emb), lambda i, place=place: (place, 0)),
            pl.BlockSpec((rows, cols), lambda i, place=place: (0, place)),
            pl.BlockSpec((1, cols), lambda i, place=place: (0, place)),
        ]
        extra = emb if at is not None and p == len(pairs) - 1 else 0
        shapes.append(jax.ShapeDtypeStruct((rows, cols), jnp.bfloat16))
        shapes.append(jax.ShapeDtypeStruct((half, cols + extra), jnp.bfloat16))
    sizes = [pair[3:] for pair in pairs]
    old_plain = 0 if old is None else old[2]
    return pl.pallas_call(
        lambda *refs: send_kernel(sizes, old_plain, at is not None, *refs),
        grid=(1,),
        in_specs=in_specs,
        out_specs=[whole(shape.shape) for shape in shapes],
        out_shape=shapes,
        cost_estimate=pl.CostEstimate(
            flops=2 * rows * half * sum(pair[2] for pair in pairs),
            bytes_accessed=8 * rows * half,
            transcendentals=0,
        ),
        compiler_params=params(36),
        name="send_half",
    )(*operands)


def keep_half(dz, dh, xt, at, plain, size, made, place):
    rows, emb = dz.shape
    cols = dh.shape[1]
    block = pl.BlockSpec((made, rows), lambda i: (place, 0))
    operands = [xt, dh]
    in_specs = [block, whole((rows, cols))]
    if at is None:
        blocks = tuple(range(made // size * place, made // size * (place + 1)))
        kernel = lambda x, d, g: keep_blocks(g, x, d, plain, size, blocks)
        in_specs[0] = whole((4 * size, rows))
    else:
        kernel = lambda x, d, a, z, g: keep_rows(g, x, d, plain, size, a, z)
        operands += [at, dz]
        in_specs += [block, whole((rows, emb))]
        cols += emb
    return pl.pallas_call(
        kernel,
        grid=(1,),
        in_specs=in_specs,
        out_specs=whole((made, cols)),
        out_shape=jax.ShapeDtypeStruct((made, cols), jnp.float32),
        cost_estimate=pl.CostEstimate(
            flops=2 * rows * made * cols, bytes_accessed=8 * rows * made, transcendentals=0
        ),
        compiler_params=params(28),
        name="keep_half",
    )(*operands)


def swap(x, axis, bit):
    size = lax.axis_size(axis)
    return lax.ppermute(x, axis, [(i, i ^ bit) for i in range(size)])


def after(x, *others):
    return lax.optimization_barrier((x,) + others)[0]


def fold_kernel(split, form, counts, *refs):
    both, left, right = counts
    joined = refs[:both]
    sides = (refs[both:both + left], refs[both + left:both + left + right])
    outs = refs[both + left + right:]
    for side, cols in enumerate((slice(0, split), slice(split, refs[0].shape[1]))):
        v = joined[0][:, cols].astype(jnp.float32)
        for ref in joined[1:]:
            v = v + ref[:, cols].astype(jnp.float32)
        for ref in sides[side]:
            v = v + ref[...].astype(jnp.float32)
        if form == "halves":
            half = v.shape[0] // 2
            outs[0][:, cols] = v[:half]
            outs[1][:, cols] = v[half:].astype(jnp.bfloat16)
        elif form == "sides":
            width = v.shape[1]
            outs[side][:, :width] = v.astype(jnp.bfloat16)
            if outs[side].shape[1] > width:
                outs[side][:, width:] = jnp.zeros_like(outs[side][:, width:])
        else:
            outs[0][:, cols] = v.astype(outs[0].dtype)


def fold(keep, keep_place, both, left, right, split, rows, place, form, even):
    cols = keep.shape[1]

    def spec(width, place=place):
        return pl.BlockSpec((rows, width), lambda i: (place, 0))

    low, full = jnp.bfloat16, jnp.float32
    widths = (split, cols - split)
    if even:
        widths = (max(widths),) * 2
    shapes = {
        "halves": [((rows // 2, cols), full), ((rows // 2, cols), low)],
        "sides": [((rows, width), low) for width in widths],
        "send": [((rows, cols), low)],
        "own": [((rows, cols), full)],
    }[form]
    in_specs = [spec(cols, keep_place)] + [spec(cols)] * len(both)
    in_specs += [spec(split)] * len(left) + [spec(cols - split)] * len(right)
    return pl.pallas_call(
        lambda *refs: fold_kernel(split, form, (1 + len(both), len(left), len(right)), *refs),
        grid=(1,),
        in_specs=in_specs,
        out_specs=[whole(shape) for shape, _ in shapes],
        out_shape=[jax.ShapeDtypeStruct(*shape) for shape in shapes],
        cost_estimate=SOON,
        compiler_params=params(16),
        name="fold",
    )(keep, *both, *left, *right)


class Pair:
    def __init__(self, keep, came, split):
        self.keep, self.both, self.split = keep, [came], split
        self.left, self.right = [], []

    def hold(self, *others):
        for came in (self.both, self.left, self.right):
            if came:
                came[-1] = after(came[-1], *others)

    def add(self, rows, place, form, even=False):
        keep, start = self.keep
        keep_place = (place * rows - start) // rows
        out = fold(
            keep, keep_place, self.both, self.left, self.right, self.split, rows, place, form, even
        )
        return lax.optimization_barrier(out)

    def cross_first(self, out):
        self.left.append(swap(out[0], "dp", 1))
        self.right.append(swap(out[1], "crop", 2))

    def cross_second(self, out):
        self.left.append(swap(out[0], "crop", 2))
        self.right.append(swap(out[1], "dp", 1))

    def cross_line(self, out, bit):
        self.both.append(swap(out[0], "dp", 2 * bit))

    def cross_third(self, out):
        own, send = out
        return own + swap(send, "dp", 2).astype(jnp.float32)

    def cross_rest(self, own):
        length = lax.axis_size("dp") // 2
        bit = 1
        while 2 * bit < length:
            bit *= 2
            half = own.shape[0] // 2
            own, send = own[:half], own[half:].astype(jnp.bfloat16)
            own = own + swap(send, "dp", 2 * bit).astype(jnp.float32)
        return own


def per_device(
    query_crops, key_crops, shuffle, distractor_bank, query_inner, query_outer, key_inner, key_outer
):
    n_dp, n_crop = lax.axis_size("dp"), lax.axis_size("crop")
    group_count = n_dp * n_crop
    row_count = query_crops.shape[0]
    hid = query_inner.shape[1]
    per_peer = row_count // group_count
    all_rows = float(row_count * group_count)

    wanted = (shuffle % row_count).reshape(group_count, per_peer)
    wanted = jnp.pad(wanted.astype(jnp.float32), ((0, 0), (0, 128 - per_peer)))
    requested = lax.all_to_all(wanted, AXES, split_axis=0, concat_axis=0, tiled=True)
    flat_req = requested[:, :per_peer].astype(jnp.int32).reshape(-1)

    flat_col, flat_row = flat_req[:, None], flat_req[None, :]
    hidden_k, sums = key_hidden(flat_col, key_crops, key_inner, group_count)
    came = lax.all_to_all(sums, AXES, split_axis=0, concat_axis=0, tiled=True)

    length = n_dp // 2
    bits = length.bit_length() - 1
    dp, crop = lax.axis_index("dp"), lax.axis_index("crop")
    block = lax.iota(jnp.int32, group_count // 2)
    z, x, y = block // n_crop, (block // (n_crop // 2)) % 2, block % (n_crop // 2)
    plane = (x ^ (dp % 2)) * (n_crop // 2) + (y ^ (crop // 2))
    line = jnp.zeros_like(block)
    for bit in range(bits):
        line = line * 2 + (((z ^ (dp // 2)) >> bit) & 1)
    order = jnp.stack(
        [plane * length + line, line * n_crop + plane, jnp.full_like(block, crop % 2)]
    )

    normed, inv_q, z_q, q_low, xt, xt3, at3 = query_forward(
        order, group_count, after(query_crops, sums), query_inner, query_outer
    )
    came, q_low, flat_row = lax.optimization_barrier((came, q_low, flat_row))
    told = batch(came, row_count)
    told = lax.all_to_all(told, AXES, split_axis=0, concat_axis=0, tiled=True)

    negs = negatives(q_low, distractor_bank)
    told, negs = lax.optimization_barrier((told, negs))
    d_z = embed(flat_row, hidden_k, told, key_outer, z_q, negs, all_rows)

    def send(last, old, pairs):
        return send_half(d_z, last, old, query_outer, normed, inv_q, pairs)

    large = hid // 16 * 7
    small = hid - 2 * large
    wide = hid // 4
    narrow = large - wide
    half = xt.shape[0] // 2
    size, size_3 = half // 4, half // (4 * length)
    dh_1, sent_1 = send(None, None, [(xt, 0, large, wide, size)])
    came_1 = swap(sent_1, "crop", 1)
    keep_1, dh_2, sent_2, dh_3, sent_3 = send(
        at3,
        (xt, dh_1, wide),
        [
            (xt, 1, large, narrow, size),
            (xt3, 2 * large // small, small, small // 2, size_3),
        ],
    )
    came_2 = swap(sent_2, "crop", 1)
    came_3 = swap(sent_3, "crop", 1)

    def piece(part, rows, place, *others):
        if part == 3:
            dh = after(dh_3, *others)
            keep = keep_half(d_z, dh, xt3, at3, small // 2, size_3, rows, place)
        else:
            dh = after(dh_1 if part == 1 else dh_2, *others)
            plain = wide if part == 1 else narrow
            keep = keep_half(d_z, dh, xt, None, plain, size, rows, place)
        return keep, rows * place

    half_rows, rows = half // 2, half // 4
    one = Pair((keep_1, half_rows), came_1, wide)
    out = one.add(half_rows, 1, "sides")
    one.cross_first(out)
    two = Pair(piece(2, half_rows, 1, *out), came_2, narrow)
    out = two.add(half_rows, 1, "sides")
    two.cross_first(out)
    three = Pair(piece(3, half_rows, 1, *out), came_3, small // 2)
    out = three.add(half_rows, 1, "send")
    three.cross_line(out, 1)
    one.keep = piece(1, rows, 1, *out)
    three.keep = piece(3, half_rows, 0, one.keep[0])
    one.hold(three.keep[0])
    out = one.add(rows, 1, "sides")
    one.cross_second(out)
    line_rows = half_rows
    for bit in range(1, bits):
        line_rows //= 2
        three.hold(*out)
        out = three.add(line_rows, 1, "send")
        three.cross_line(out, 2 ** bit)
    two.keep = piece(2, half_rows, 0, *out)
    one.keep = piece(1, rows, 0, two.keep[0])
    two.hold(two.keep[0], one.keep[0])
    out = two.add(rows, 1, "sides", even=True)
    two.cross_second(out)
    three.hold(*out)
    line_rows //= 2
    out = three.add(line_rows, 1, "sides")
    three.cross_first(out)
    one.hold(*out)
    c_1 = one.add(rows, 0, "halves")
    two.hold(*c_1)
    c_2 = two.add(rows, 0, "halves")
    own_1 = lax.optimization_barrier(one.cross_third(c_1))
    own_2 = lax.optimization_barrier(two.cross_third(c_2))
    three.hold(own_1, own_2)
    line_rows //= 2
    out = three.add(line_rows, 1, "sides")
    three.cross_second(out)
    own_1 = one.cross_rest(own_1)
    own_2 = two.cross_rest(own_2)
    own_3 = three.add(line_rows, 0, "own")[0]
    grad_inner = jnp.concatenate([own_1, own_2, own_3[:, :small]], axis=1)
    return (grad_inner, own_3[:, small:])


def solution(mesh):
    placed = (
        P(AXES, None),
        P(AXES, None),
        P(AXES),
        P(),
        P(),
        P(),
        P(),
        P(),
    )
    return jax.shard_map(
        per_device,
        mesh=mesh,
        in_specs=placed,
        out_specs=(P(AXES, None), P(AXES, None)),
        check_vma=False,
    )
```

```python
import math
import jax
import jax.numpy as jnp
from jax import lax
from jax.experimental import pallas as pl
from jax.experimental.pallas import tpu as pltpu
from jax.sharding import PartitionSpec as P

sharpness_divisor = 0.2
loss_scale = 4096.0
bn_eps = 1e-05
norm_eps = 1e-06
AXES = ("dp", "crop")
QUARTER = 0.25


def neg_kernel(q_ref, bank_ref, out_ref):
    rows, emb = q_ref.shape

    @pl.when(pl.program_id(0) == 0)
    def _():
        out_ref[...] = jnp.zeros_like(out_ref)

    q = q_ref[...]
    step = 512
    for j in range(bank_ref.shape[0] // step):
        bank = bank_ref[j * step:(j + 1) * step, :]
        s = lax.dot_general(q, bank, (((1,), (1,)), ((), ())), preferred_element_type=jnp.float32)
        e = jnp.exp2(s * (1.0 / (sharpness_divisor * math.log(2.0))) - 2.0)
        total = e[:, :128]
        for i in range(1, step // 128):
            total = total + e[:, i * 128:(i + 1) * 128]
        out_ref[:, emb:] += total
        out_ref[:, :emb] += jnp.dot(
            e.astype(jnp.bfloat16), bank, preferred_element_type=jnp.float32
        )


def negatives(q, bank):
    rows, emb = q.shape
    tile = 2048
    return pl.pallas_call(
        neg_kernel,
        grid=(bank.shape[0] // tile,),
        in_specs=[
            pl.BlockSpec((rows, emb), lambda i: (0, 0)),
            pl.BlockSpec((tile, emb), lambda i: (i, 0)),
        ],
        out_specs=pl.BlockSpec((rows, emb + 128), lambda i: (0, 0)),
        out_shape=jax.ShapeDtypeStruct((rows, emb + 128), jnp.float32),
        cost_estimate=pl.CostEstimate(
            flops=4 * rows * bank.shape[0] * emb,
            bytes_accessed=bank.shape[0] * emb * 2,
            transcendentals=rows * bank.shape[0],
        ),
        compiler_params=params(44),
        name="negatives",
    )(q, bank)


TILE = 256
STEP = 512
MIB = 1024 * 1024
SOON = pl.CostEstimate(flops=1, bytes_accessed=1, transcendentals=0)


def params(limit=24):
    return pltpu.CompilerParams(
        dimension_semantics=("arbitrary",), vmem_limit_bytes=limit * MIB
    )


def dot(a, b):
    return jnp.dot(a, b, preferred_element_type=jnp.float32)


def dot_t(a, b):
    return lax.dot_general(a, b, (((1,), (1,)), ((), ())), preferred_element_type=jnp.float32)


def whole(shape):
    return pl.BlockSpec(shape, lambda *_: (0,) * len(shape))


def group_rows(groups, per_peer):
    rows = groups * per_peer
    row = lax.broadcasted_iota(jnp.int32, (groups, rows), 1)
    group = lax.broadcasted_iota(jnp.int32, (groups, rows), 0)
    inside = (row >= group * per_peer) & (row < (group + 1) * per_peer)
    return jnp.where(inside, 1.0, 0.0).astype(jnp.float32)


def group_sum(h, groups):
    rows, cols = h.shape
    per_peer = rows // groups
    if per_peer % 8 == 0:
        return jnp.sum(h.reshape(groups, per_peer, cols), axis=1)
    return jnp.dot(
        group_rows(groups, per_peer),
        h,
        precision=lax.Precision.HIGHEST,
        preferred_element_type=jnp.float32,
    )


def group_spread(v, rows):
    groups, cols = v.shape
    per_peer = rows // groups
    if per_peer % 8 == 0:
        return jnp.broadcast_to(v[:, None, :], (groups, per_peer, cols)).reshape(rows, cols)
    return lax.dot_general(
        group_rows(groups, per_peer),
        v,
        (((0,), (0,)), ((), ())),
        precision=lax.Precision.HIGHEST,
        preferred_element_type=jnp.float32,
    )


def key_hidden_kernel(groups, flat_ref, k_ref, w_ref, h_ref, sums_ref, sorted_ref):
    rows = k_ref.shape[0]

    @pl.when(pl.program_id(0) == 0)
    def _():
        cols = lax.broadcasted_iota(jnp.int32, (rows, rows), 1)
        pick = jnp.where(flat_ref[...] == cols, 1.0, 0.0).astype(jnp.bfloat16)
        for i in range(0, k_ref.shape[1], 512):
            sorted_ref[:, i:i + 512] = dot(pick, k_ref[:, i:i + 512]).astype(jnp.bfloat16)

    x = sorted_ref[...]
    for t in range(0, STEP, TILE):
        h = dot(x, w_ref[:, t:t + TILE])
        h_ref[:, t:t + TILE] = h
        sums_ref[:, 0, 2 * t:2 * t + TILE] = group_sum(h, groups)
        sums_ref[:, 0, 2 * t + TILE:2 * t + 2 * TILE] = group_sum(h * h, groups)


def key_hidden(flat_col, k, w, groups):
    rows, d = k.shape
    hid = w.shape[1]
    return pl.pallas_call(
        lambda *refs: key_hidden_kernel(groups, *refs),
        grid=(hid // STEP,),
        in_specs=[
            whole((rows, 1)),
            whole((rows, d)),
            pl.BlockSpec((d, STEP), lambda i: (0, i)),
        ],
        out_specs=[
            pl.BlockSpec((rows, STEP), lambda i: (0, i)),
            pl.BlockSpec((groups, 1, 2 * STEP), lambda i: (0, 0, i)),
        ],
        out_shape=[
            jax.ShapeDtypeStruct((rows, hid), jnp.float32),
            jax.ShapeDtypeStruct((groups, 1, 2 * hid), jnp.float32),
        ],
        scratch_shapes=[pltpu.VMEM((rows, d), jnp.bfloat16)],
        cost_estimate=pl.CostEstimate(
            flops=2 * rows * d * (hid + rows), bytes_accessed=2 * d * hid, transcendentals=0
        ),
        compiler_params=params(54),
        name="key_hidden",
    )(flat_col, k, w)


def batch_kernel(rows, part_ref, told_ref):
    groups, _, size = part_ref.shape
    for t in range(0, size, 2 * TILE):
        total = jnp.sum(part_ref[:, 0, t:t + 2 * TILE], axis=0, keepdims=True) / rows
        mu = total[:, :TILE]
        inv = lax.rsqrt(total[:, TILE:] - mu * mu + bn_eps)
        told = jnp.concatenate([mu, inv], axis=1)
        told_ref[:, 0, t:t + 2 * TILE] = jnp.broadcast_to(told, (groups, 2 * TILE))


def batch(part, rows):
    return pl.pallas_call(
        lambda *refs: batch_kernel(rows, *refs),
        grid=(1,),
        in_specs=[whole(part.shape)],
        out_specs=whole(part.shape),
        out_shape=jax.ShapeDtypeStruct(part.shape, jnp.float32),
        compiler_params=params(),
        name="batch",
    )(part)


def place_rows(order_ref, which, first, rows, t, out_ref):
    for i in range(t.shape[0] // (2 * rows)):
        at = order_ref[which, first + i]
        core = order_ref[2, 0]
        out_ref[core, at] = t[2 * i * rows:(2 * i + 1) * rows]
        out_ref[1 - core, at] = t[(2 * i + 1) * rows:(2 * i + 2) * rows]


def query_kernel(
    rows_of_block, order_ref, x_ref, w_ref, w2_ref,
    n_ref, inv_ref, z_ref, q_ref, xt_ref, xt3_ref, at3_ref, sum_ref,
):
    i = pl.program_id(0)
    rows = x_ref.shape[0]

    @pl.when(i == 0)
    def _():
        sum_ref[...] = jnp.zeros_like(sum_ref)

    x = x_ref[...]
    z = None
    for t in range(0, STEP, TILE):
        h = dot(x, w_ref[:, t:t + TILE])
        mu = jnp.sum(h, axis=0, keepdims=True) / rows
        inv = lax.rsqrt(jnp.sum(h * h, axis=0, keepdims=True) / rows - mu * mu + bn_eps)
        normed = ((h - mu) * inv).astype(jnp.bfloat16)
        n_ref[:, t:t + TILE] = normed
        inv_ref[:, t:t + TILE] = inv
        active = jnp.maximum(normed, 0)
        term = dot(active, w2_ref[t:t + TILE, :])
        z = term if z is None else z + term
        block = (i * STEP + t) // (2 * rows_of_block)
        own = x_ref[:, pl.ds(pl.multiple_of(i * STEP + t, TILE), TILE)].T
        place_rows(order_ref, 0, block, rows_of_block, own, xt_ref)
        place_rows(order_ref, 1, block, rows_of_block, own, xt3_ref)
        place_rows(order_ref, 1, block, rows_of_block, active.T, at3_ref)
    sum_ref[...] += z

    @pl.when(i == pl.num_programs(0) - 1)
    def _():
        z = sum_ref[...]
        z_ref[...] = z
        q = z * lax.rsqrt(jnp.sum(z * z, axis=-1, keepdims=True) + norm_eps)
        q_ref[...] = q.astype(jnp.bfloat16)


def query_forward(order, blocks, x, w, w2):
    rows, d = x.shape
    hid, emb = w2.shape
    half, size = blocks // 2, d // blocks
    turned = jax.ShapeDtypeStruct((2, half, size, rows), jnp.bfloat16)
    out = pl.pallas_call(
        lambda *refs: query_kernel(size, *refs),
        grid_spec=pltpu.PrefetchScalarGridSpec(
            num_scalar_prefetch=1,
            grid=(hid // STEP,),
            in_specs=[
                whole((rows, d)),
                pl.BlockSpec((d, STEP), lambda i, o: (0, i)),
                pl.BlockSpec((STEP, emb), lambda i, o: (i, 0)),
            ],
            out_specs=[
                pl.BlockSpec((rows, STEP), lambda i, o: (0, i)),
                pl.BlockSpec((1, STEP), lambda i, o: (0, i)),
                whole((rows, emb)),
                whole((rows, emb)),
                whole(turned.shape),
                whole(turned.shape),
                whole(turned.shape),
            ],
            scratch_shapes=[pltpu.VMEM((rows, emb), jnp.float32)],
        ),
        out_shape=[
            jax.ShapeDtypeStruct((rows, hid), jnp.bfloat16),
            jax.ShapeDtypeStruct((1, hid), jnp.float32),
            jax.ShapeDtypeStruct((rows, emb), jnp.float32),
            jax.ShapeDtypeStruct((rows, emb), jnp.bfloat16),
            turned,
            turned,
            turned,
        ],
        cost_estimate=pl.CostEstimate(
            flops=2 * rows * hid * (d + emb), bytes_accessed=2 * d * hid, transcendentals=0
        ),
        compiler_params=params(44),
        name="query_forward",
    )(order, x, w, w2)
    return (*out[:4], *(t.reshape(d, rows) for t in out[4:]))


def embed_kernel(all_rows, flat_ref, h_ref, told_ref, w2_ref, zq_ref, neg_ref, dz_ref, z_ref):
    i = pl.program_id(0)
    rows, emb = zq_ref.shape

    @pl.when(i == 0)
    def _():
        z_ref[...] = jnp.zeros_like(z_ref)

    z = None
    for t in range(0, STEP, TILE):
        mu = group_spread(told_ref[:, 0, 2 * t:2 * t + TILE], rows)
        inv = group_spread(told_ref[:, 0, 2 * t + TILE:2 * t + 2 * TILE], rows)
        active = jnp.maximum((h_ref[:, t:t + TILE] - mu) * inv, 0.0).astype(jnp.bfloat16)
        term = dot(active, w2_ref[t:t + TILE, :])
        z = term if z is None else z + term
    z_ref[...] += z

    @pl.when(i == pl.num_programs(0) - 1)
    def _():
        z = z_ref[...]
        z = z * lax.rsqrt(jnp.sum(z * z, axis=-1, keepdims=True) + norm_eps)
        back = jnp.where(
            flat_ref[...] == lax.broadcasted_iota(jnp.int32, (rows, rows), 0), 1.0, 0.0
        ).astype(jnp.bfloat16)
        high = z.astype(jnp.bfloat16)
        rest = z - high.astype(jnp.float32)
        mid = rest.astype(jnp.bfloat16)
        low = (rest - mid.astype(jnp.float32)).astype(jnp.bfloat16)
        positives = dot(back, high) + dot(back, mid) + dot(back, low)
        zq = zq_ref[...]
        inv_len = lax.rsqrt(jnp.sum(zq * zq, axis=-1, keepdims=True) + norm_eps)
        q = zq * inv_len
        scale_coef = loss_scale / all_rows
        pos = jnp.sum(q * positives, axis=-1, keepdims=True) / sharpness_divisor
        exp_pos = jnp.exp(pos) * QUARTER
        total = exp_pos + jnp.sum(neg_ref[:, emb:], axis=-1, keepdims=True)
        d_pos = scale_coef * (exp_pos / total - 1.0)
        weighted = neg_ref[:, :emb] * (scale_coef / total)
        d_q = (d_pos * positives + weighted) / sharpness_divisor
        d_z = (d_q - q * jnp.sum(d_q * q, axis=-1, keepdims=True)) * inv_len
        dz_ref[...] = d_z.astype(jnp.bfloat16)


def embed(flat_row, h, told, w2, zq, negs, all_rows):
    rows, hid = h.shape
    emb = w2.shape[1]
    groups = told.shape[0]
    return pl.pallas_call(
        lambda *refs: embed_kernel(all_rows, *refs),
        grid=(hid // STEP,),
        in_specs=[
            whole((1, rows)),
            pl.BlockSpec((rows, STEP), lambda i: (0, i)),
            pl.BlockSpec((groups, 1, 2 * STEP), lambda i: (0, 0, i)),
            pl.BlockSpec((STEP, emb), lambda i: (i, 0)),
            whole((rows, emb)),
            whole(negs.shape),
        ],
        out_specs=whole((rows, emb)),
        out_shape=jax.ShapeDtypeStruct((rows, emb), jnp.bfloat16),
        scratch_shapes=[pltpu.VMEM((rows, emb), jnp.float32)],
        cost_estimate=pl.CostEstimate(
            flops=2 * rows * hid * emb, bytes_accessed=4 * rows * hid, transcendentals=0
        ),
        compiler_params=params(30),
        name="embed",
    )(flat_row, h, told, w2, zq, negs)


def store_rows(out_ref, at, value, crossed, size):
    if not crossed:
        out_ref[:, at] = value.astype(out_ref.dtype)
        return
    for four in range(0, value.shape[0], 4 * size):
        for i, j in enumerate((0, 2, 1, 3)):
            i, j = four + i * size, four + j * size
            out_ref[i:i + size, at] = value[j:j + size].astype(out_ref.dtype)


def column_tiles(cols, plain):
    for start, end in ((0, plain), (plain, cols)):
        for t in range(start, end, TILE):
            yield slice(t, min(t + TILE, end)), start > 0


def keep_rows(keep_ref, xt_ref, dh_ref, plain, size, at_ref=None, dz_ref=None):
    cols = dh_ref.shape[1]
    for at, crossed in column_tiles(cols, plain):
        store_rows(keep_ref, at, dot(xt_ref[...], dh_ref[:, at]), crossed, size)
    if at_ref is not None:
        store_rows(keep_ref, slice(cols, None), dot(at_ref[...], dz_ref[...]), True, size)


def keep_blocks(keep_ref, xt_ref, dh_ref, plain, size, blocks):
    for at, crossed in column_tiles(dh_ref.shape[1], plain):
        for i, block in enumerate(blocks):
            j = (0, 2, 1, 3)[block] if crossed else block
            keep_ref[i * size:(i + 1) * size, at] = dot(
                xt_ref[j * size:(j + 1) * size, :], dh_ref[:, at]
            )


def send_kernel(sizes, old_plain, has_at, *refs):
    refs = list(refs)
    count = len(sizes)
    dz_ref = refs.pop(0)
    at_ref = refs.pop(0) if has_at else None
    dz = dz_ref[...]
    rows = dz.shape[0]
    if old_plain:
        old_xt_ref, old_ref = refs[:2]
        refs = refs[2:]
    ins, outs = refs[:4 * count], refs[4 * count:]
    if old_plain:
        keep_blocks(outs.pop(0), old_xt_ref, old_ref, old_plain, sizes[0][1], (2, 3))
    for p in range(count):
        xt_ref, w2_ref, n_ref, inv_ref = ins[4 * p:4 * p + 4]
        dh_ref, sent_ref = outs[2 * p:2 * p + 2]
        cols = n_ref.shape[1]
        plain, size = sizes[p]
        for at, crossed in column_tiles(cols, plain):
            normed = n_ref[:, at].astype(jnp.float32)
            d_norm = jnp.where(normed > 0.0, dot_t(dz, w2_ref[at, :]), 0.0)
            mean = jnp.sum(d_norm, axis=0, keepdims=True) / rows
            slope = jnp.sum(d_norm * normed, axis=0, keepdims=True) / rows
            d_hidden = inv_ref[:, at] * (d_norm - mean - normed * slope)
            d_hidden = d_hidden.astype(jnp.bfloat16)
            dh_ref[:, at] = d_hidden
            store_rows(sent_ref, at, dot(xt_ref[...], d_hidden), crossed, size)
        if has_at and p == count - 1:
            store_rows(sent_ref, slice(cols, None), dot(at_ref[...], dz), True, size)


def send_half(dz, at, old, w2, normed, inv, pairs):
    rows, emb = dz.shape
    operands, in_specs, shapes = [dz], [whole(dz.shape)], []
    if at is not None:
        half = at.shape[0] // 2
        operands.append(at)
        in_specs.append(pl.BlockSpec((half, rows), lambda i: (1, 0)))
    if old is not None:
        half = old[0].shape[0] // 2
        operands += old[:2]
        in_specs += [whole((half, rows)), whole(old[1].shape)]
        shapes.append(jax.ShapeDtypeStruct((half // 2, old[1].shape[1]), jnp.float32))
    for p, (xt, place, cols, *_) in enumerate(pairs):
        half = xt.shape[0] // 2
        operands += [xt, w2, normed, inv]
        in_specs += [
            pl.BlockSpec((half, rows), lambda i: (1, 0)),
            pl.BlockSpec((cols, emb), lambda i, place=place: (place, 0)),
            pl.BlockSpec((rows, cols), lambda i, place=place: (0, place)),
            pl.BlockSpec((1, cols), lambda i, place=place: (0, place)),
        ]
        extra = emb if at is not None and p == len(pairs) - 1 else 0
        shapes.append(jax.ShapeDtypeStruct((rows, cols), jnp.bfloat16))
        shapes.append(jax.ShapeDtypeStruct((half, cols + extra), jnp.bfloat16))
    sizes = [pair[3:] for pair in pairs]
    old_plain = 0 if old is None else old[2]
    return pl.pallas_call(
        lambda *refs: send_kernel(sizes, old_plain, at is not None, *refs),
        grid=(1,),
        in_specs=in_specs,
        out_specs=[whole(shape.shape) for shape in shapes],
        out_shape=shapes,
        cost_estimate=pl.CostEstimate(
            flops=2 * rows * half * sum(pair[2] for pair in pairs),
            bytes_accessed=8 * rows * half,
            transcendentals=0,
        ),
        compiler_params=params(36),
        name="send_half",
    )(*operands)


def keep_half(dz, dh, xt, at, plain, size, made, place):
    rows, emb = dz.shape
    cols = dh.shape[1]
    block = pl.BlockSpec((made, rows), lambda i: (place, 0))
    operands = [xt, dh]
    in_specs = [block, whole((rows, cols))]
    if at is None:
        blocks = tuple(range(made // size * place, made // size * (place + 1)))
        kernel = lambda x, d, g: keep_blocks(g, x, d, plain, size, blocks)
        in_specs[0] = whole((4 * size, rows))
    else:
        kernel = lambda x, d, a, z, g: keep_rows(g, x, d, plain, size, a, z)
        operands += [at, dz]
        in_specs += [block, whole((rows, emb))]
        cols += emb
    return pl.pallas_call(
        kernel,
        grid=(1,),
        in_specs=in_specs,
        out_specs=whole((made, cols)),
        out_shape=jax.ShapeDtypeStruct((made, cols), jnp.float32),
        cost_estimate=pl.CostEstimate(
            flops=2 * rows * made * cols, bytes_accessed=8 * rows * made, transcendentals=0
        ),
        compiler_params=params(28),
        name="keep_half",
    )(*operands)


def swap(x, axis, bit):
    size = lax.axis_size(axis)
    return lax.ppermute(x, axis, [(i, i ^ bit) for i in range(size)])


def after(x, *others):
    return lax.optimization_barrier((x,) + others)[0]


def fold_kernel(split, form, counts, *refs):
    both, left, right = counts
    joined = refs[:both]
    sides = (refs[both:both + left], refs[both + left:both + left + right])
    outs = refs[both + left + right:]
    for side, cols in enumerate((slice(0, split), slice(split, refs[0].shape[1]))):
        v = joined[0][:, cols].astype(jnp.float32)
        for ref in joined[1:]:
            v = v + ref[:, cols].astype(jnp.float32)
        for ref in sides[side]:
            v = v + ref[...].astype(jnp.float32)
        if form == "halves":
            half = v.shape[0] // 2
            outs[0][:, cols] = v[:half]
            outs[1][:, cols] = v[half:].astype(jnp.bfloat16)
        elif form == "sides":
            width = v.shape[1]
            outs[side][:, :width] = v.astype(jnp.bfloat16)
            if outs[side].shape[1] > width:
                outs[side][:, width:] = jnp.zeros_like(outs[side][:, width:])
        else:
            outs[0][:, cols] = v.astype(outs[0].dtype)


def fold(keep, keep_place, both, left, right, split, rows, place, form, even):
    cols = keep.shape[1]

    def spec(width, place=place):
        return pl.BlockSpec((rows, width), lambda i: (place, 0))

    low, full = jnp.bfloat16, jnp.float32
    widths = (split, cols - split)
    if even:
        widths = (max(widths),) * 2
    shapes = {
        "halves": [((rows // 2, cols), full), ((rows // 2, cols), low)],
        "sides": [((rows, width), low) for width in widths],
        "send": [((rows, cols), low)],
        "own": [((rows, cols), full)],
    }[form]
    in_specs = [spec(cols, keep_place)] + [spec(cols)] * len(both)
    in_specs += [spec(split)] * len(left) + [spec(cols - split)] * len(right)
    return pl.pallas_call(
        lambda *refs: fold_kernel(split, form, (1 + len(both), len(left), len(right)), *refs),
        grid=(1,),
        in_specs=in_specs,
        out_specs=[whole(shape) for shape, _ in shapes],
        out_shape=[jax.ShapeDtypeStruct(*shape) for shape in shapes],
        cost_estimate=SOON,
        compiler_params=params(16),
        name="fold",
    )(keep, *both, *left, *right)


class Pair:
    def __init__(self, keep, came, split):
        self.keep, self.both, self.split = keep, [came], split
        self.left, self.right = [], []

    def hold(self, *others):
        for came in (self.both, self.left, self.right):
            if came:
                came[-1] = after(came[-1], *others)

    def add(self, rows, place, form, even=False):
        keep, start = self.keep
        keep_place = (place * rows - start) // rows
        out = fold(
            keep, keep_place, self.both, self.left, self.right, self.split, rows, place, form, even
        )
        return lax.optimization_barrier(out)

    def cross_first(self, out):
        self.left.append(swap(out[0], "dp", 1))
        self.right.append(swap(out[1], "crop", 2))

    def cross_second(self, out):
        self.left.append(swap(out[0], "crop", 2))
        self.right.append(swap(out[1], "dp", 1))

    def cross_line(self, out, bit):
        self.both.append(swap(out[0], "dp", 2 * bit))

    def cross_third(self, out):
        own, send = out
        return own + swap(send, "dp", 2).astype(jnp.float32)

    def cross_rest(self, own):
        length = lax.axis_size("dp") // 2
        bit = 1
        while 2 * bit < length:
            bit *= 2
            half = own.shape[0] // 2
            own, send = own[:half], own[half:].astype(jnp.bfloat16)
            own = own + swap(send, "dp", 2 * bit).astype(jnp.float32)
        return own


def per_device(
    query_crops, key_crops, shuffle, distractor_bank, query_inner, query_outer, key_inner, key_outer
):
    n_dp, n_crop = lax.axis_size("dp"), lax.axis_size("crop")
    group_count = n_dp * n_crop
    row_count = query_crops.shape[0]
    hid = query_inner.shape[1]
    per_peer = row_count // group_count
    all_rows = float(row_count * group_count)

    wanted = (shuffle % row_count).reshape(group_count, per_peer)
    wanted = jnp.pad(wanted.astype(jnp.float32), ((0, 0), (0, 128 - per_peer)))
    requested = lax.all_to_all(wanted, AXES, split_axis=0, concat_axis=0, tiled=True)
    flat_req = requested[:, :per_peer].astype(jnp.int32).reshape(-1)

    flat_col, flat_row = flat_req[:, None], flat_req[None, :]
    hidden_k, sums = key_hidden(flat_col, key_crops, key_inner, group_count)
    came = lax.all_to_all(sums, AXES, split_axis=0, concat_axis=0, tiled=True)

    length = n_dp // 2
    bits = length.bit_length() - 1
    dp, crop = lax.axis_index("dp"), lax.axis_index("crop")
    block = lax.iota(jnp.int32, group_count // 2)
    z, x, y = block // n_crop, (block // (n_crop // 2)) % 2, block % (n_crop // 2)
    plane = (x ^ (dp % 2)) * (n_crop // 2) + (y ^ (crop // 2))
    line = jnp.zeros_like(block)
    for bit in range(bits):
        line = line * 2 + (((z ^ (dp // 2)) >> bit) & 1)
    order = jnp.stack(
        [plane * length + line, line * n_crop + plane, jnp.full_like(block, crop % 2)]
    )

    normed, inv_q, z_q, q_low, xt, xt3, at3 = query_forward(
        order, group_count, after(query_crops, sums), query_inner, query_outer
    )
    came, q_low, flat_row = lax.optimization_barrier((came, q_low, flat_row))
    told = batch(came, row_count)
    told = lax.all_to_all(told, AXES, split_axis=0, concat_axis=0, tiled=True)

    negs = negatives(q_low, distractor_bank)
    told, negs = lax.optimization_barrier((told, negs))
    d_z = embed(flat_row, hidden_k, told, key_outer, z_q, negs, all_rows)

    def send(last, old, pairs):
        return send_half(d_z, last, old, query_outer, normed, inv_q, pairs)

    large = hid // 16 * 7
    small = hid - 2 * large
    wide = hid // 4
    narrow = large - wide
    half = xt.shape[0] // 2
    size, size_3 = half // 4, half // (4 * length)
    dh_1, sent_1 = send(None, None, [(xt, 0, large, wide, size)])
    came_1 = swap(sent_1, "crop", 1)
    keep_1, dh_2, sent_2, dh_3, sent_3 = send(
        at3,
        (xt, dh_1, wide),
        [
            (xt, 1, large, narrow, size),
            (xt3, 2 * large // small, small, small // 2, size_3),
        ],
    )
    came_2 = swap(sent_2, "crop", 1)
    came_3 = swap(sent_3, "crop", 1)

    def piece(part, rows, place, *others):
        if part == 3:
            dh = after(dh_3, *others)
            keep = keep_half(d_z, dh, xt3, at3, small // 2, size_3, rows, place)
        else:
            dh = after(dh_1 if part == 1 else dh_2, *others)
            plain = wide if part == 1 else narrow
            keep = keep_half(d_z, dh, xt, None, plain, size, rows, place)
        return keep, rows * place

    half_rows, rows = half // 2, half // 4
    one = Pair((keep_1, half_rows), came_1, wide)
    out = one.add(half_rows, 1, "sides")
    one.cross_first(out)
    two = Pair(piece(2, half_rows, 1, *out), came_2, narrow)
    out = two.add(half_rows, 1, "sides")
    two.cross_first(out)
    three = Pair(piece(3, half_rows, 1, *out), came_3, small // 2)
    out = three.add(half_rows, 1, "send")
    three.cross_line(out, 1)
    one.keep = piece(1, rows, 1, *out)
    three.keep = piece(3, half_rows, 0, one.keep[0])
    one.hold(three.keep[0])
    out = one.add(rows, 1, "sides")
    one.cross_second(out)
    line_rows = half_rows
    for bit in range(1, bits):
        line_rows //= 2
        three.hold(*out)
        out = three.add(line_rows, 1, "send")
        three.cross_line(out, 2 ** bit)
    two.keep = piece(2, half_rows, 0, *out)
    one.keep = piece(1, rows, 0, two.keep[0])
    two.hold(two.keep[0], one.keep[0])
    out = two.add(rows, 1, "sides", even=True)
    two.cross_second(out)
    three.hold(*out)
    line_rows //= 2
    out = three.add(line_rows, 1, "sides")
    three.cross_first(out)
    one.hold(*out)
    c_1 = one.add(rows, 0, "halves")
    two.hold(*c_1)
    c_2 = two.add(rows, 0, "halves")
    own_1 = lax.optimization_barrier(one.cross_third(c_1))
    own_2 = lax.optimization_barrier(two.cross_third(c_2))
    three.hold(own_1)
    line_rows //= 2
    out = three.add(line_rows, 1, "sides")
    three.cross_second(out)
    own_1 = one.cross_rest(own_1)
    own_2 = two.cross_rest(own_2)
    own_3 = three.add(line_rows, 0, "own")[0]
    grad_inner = jnp.concatenate([own_1, own_2, own_3[:, :small]], axis=1)
    return (grad_inner, own_3[:, small:])


def solution(mesh):
    placed = (
        P(AXES, None),
        P(AXES, None),
        P(AXES),
        P(),
        P(),
        P(),
        P(),
        P(),
    )
    return jax.shard_map(
        per_device,
        mesh=mesh,
        in_specs=placed,
        out_specs=(P(AXES, None), P(AXES, None)),
        check_vma=False,
    )
```
